32 devices in a mesh: fsdp: 32 (over z, y, x, core).
Axes of the slice: x: 2, y: 2, z: 4, core: 2. Of those that a mesh axis runs over, the one named last changes fastest.
Arguments:
- tokens: bfloat16 [8192, 2048], P('fsdp'), may hold values from -6 to 6
- w_query: bfloat16 [2048, 2048], P('fsdp'), may hold values from -0.125 to 0.125
- w_key: bfloat16 [2048, 2048], P('fsdp'), may hold values from -0.125 to 0.125
- w_value: bfloat16 [2048, 2048], P('fsdp'), may hold values from -0.125 to 0.125
- w_out: bfloat16 [2048, 2048], P('fsdp'), may hold values from -2 to 2
- w_router: bfloat16 [2048, 16], P('fsdp'), may hold values from -0.0625 to 0.0625
- gain_attn: bfloat16 [2048], P('fsdp'), may hold values from 0.5 to 1.5
- gain_moe: bfloat16 [2048], P('fsdp'), may hold values from 0.5 to 1.5
- w_gate: bfloat16 [16384, 2048], P('fsdp'), may hold values from -0.125 to 0.125
- w_up: bfloat16 [16384, 2048], P('fsdp'), may hold values from -0.125 to 0.125
- w_down: bfloat16 [16384, 2048], P('fsdp'), may hold values from -0.75 to 0.75
- routes: int32 [8192, 8], P('fsdp'), may hold values from 0 to 15, all different within a row; in each aligned block of 256 rows (0 to 255, 256 to 511, ...) at most 192 rows name the same one
- doc_lengths: int32 [2, 4], replicated, may hold values from 1 to 2048, 4096 in all within a row
- clip_limit: float32 [16], replicated, may hold values from 3.5 to 7.5
- cotangent: bfloat16 [8192, 2048], P('fsdp'), may hold values from -6 to 6
Outputs:
- mixed: bfloat16 [8192, 2048], P('fsdp')
- grad_tokens: float32 [8192, 2048], P('fsdp')
- grad_query: float32 [2048, 2048], P('fsdp')
- grad_key: float32 [2048, 2048], P('fsdp')
- grad_value: float32 [2048, 2048], P('fsdp')
- grad_out: float32 [2048, 2048], P('fsdp')
- grad_router: float32 [2048, 16], P('fsdp')
- grad_gain_attn: float32 [2048], P('fsdp')
- grad_gain_moe: float32 [2048], P('fsdp')
- grad_gate: float32 [16384, 2048], P('fsdp')
- grad_up: float32 [16384, 2048], P('fsdp')
- grad_down: float32 [16384, 2048], P('fsdp')
- clipped_query: bfloat16 [2048, 2048], P('fsdp')
- clipped_key: bfloat16 [2048, 2048], P('fsdp')
The draws below stay inside these ranges and needn't reach their ends.
Inputs may be any that keep to these rules, and one draw needn't show every extreme that they name: `routes`: each token names 8 different experts. Among the 256 tokens of one device no expert is named more than 192 times, a bound that some block reaches. `doc_lengths`: each row holds the lengths of the 4 documents of one packed sequence in order; a row sums to 4096 and its largest length is exactly 2048.
All inputs are finite; a program needn't handle non-finite values.
Results may differ from the reference program's by a relative error of at most 0.018.
Values may be sent and summed in bfloat16 or wider, within the bound.
A program may use at most 384 MiB of HBM per device.

```python
import math
import jax
import jax.numpy as jnp
import numpy as np
from jax import lax

D = 2048
H = 16
HD = 128
FF = 1024
TOPK = 8
TOK_DEV = 256
SEQS = 2
DOCS = 4
HALF = 512
E = 16
TOKENS = 8192
SEQ_LEN = 4096
CAP = 192


def level_of(key, dims, shards, least, top_value):
    factor_of = 1.0
    for position, parts in shards:
        heights = jax.random.uniform(jax.random.fold_in(jax.random.fold_in(key, 6), position), (parts,), jnp.float32, least / len(shards), top_value / len(shards))
        factor_of = factor_of * jnp.repeat(jnp.exp(heights), dims[position] // parts).reshape((-1,) + (1,) * (len(dims) - 1 - position))
    return factor_of


def split_up(amount, total, limit, slope):
    portions = [(1 << 20) // math.isqrt(rank ** slope) + 1 for rank in range(2, amount + 1)]
    rest, given = total - limit - (amount - 1), [1] * (amount - 1)
    while rest > 0:
        movable = [i for i in range(amount - 1) if given[i] < limit]
        whole, budget = sum([portions[i] for i in movable]), rest
        for i in movable:
            extra = min(limit - given[i], max(1, budget * portions[i] // whole), rest)
            given[i] = given[i] + extra
            rest = rest - extra
    return np.array([limit] + given)


def ragged(rng, number_of, total, reach, lean):
    if number_of == 2:
        one = jax.random.randint(rng, (), max(1, total - reach), min(reach, total - 1) + 1)
        return jnp.stack([one, total - one])
    sizes = jnp.asarray(split_up(number_of, total, reach, lean), jnp.int32)
    couples = (number_of - 1) // 2
    giver, taker = sizes[1:1 + 2 * couples:2], sizes[2:2 + 2 * couples:2]
    slack = jnp.minimum(giver - 1, reach - taker)
    shifted = jax.random.randint(jax.random.fold_in(rng, 1), (couples,), 0, 1 << 20) % (slack + 1)
    sizes = sizes.at[1:1 + 2 * couples:2].set(giver - shifted).at[2:2 + 2 * couples:2].set(taker + shifted)
    return sizes[jax.random.permutation(jax.random.fold_in(rng, 2), number_of)]


def assign_block(rng, own, number, rows, number_of, top, bound, skew):
    ranking = jax.random.permutation(rng, number_of)
    packed, common = shares(number_of, rows * top, bound, skew, True), shares(number_of, rows * top, bound, skew, False)
    places = jnp.arange(number_of)

    def named(lengths, offset_by):
        used = int((lengths > 0).sum())
        fixed = max(1, used // 4)
        passed = fixed + (places - fixed + offset_by * (used - fixed)) % max(1, number_of - fixed)
        return jnp.zeros((number_of,), jnp.int32).at[ranking[jnp.where(places < fixed, places, passed)]].set(jnp.asarray(lengths, jnp.int32))

    lengths = jnp.where(number % 4 == 0, named(packed, number // 4), named(common, number - number // 4 - 1))
    mixed = jax.random.permutation(jax.random.fold_in(own, 3), number_of)
    giver, taker = mixed[0:number_of // 2 * 2:2], mixed[1:number_of // 2 * 2:2]
    slack = jnp.minimum(lengths[giver] - 1, bound - lengths[taker]) // 2
    slack = jnp.where((giver == ranking[0]) | (taker == ranking[0]) | (lengths[taker] == 0), 0, jnp.maximum(slack, 0))
    passed = jax.random.randint(jax.random.fold_in(own, 4), (number_of // 2,), 0, 1 << 20) % (slack + 1)
    lengths = lengths.at[giver].add(-passed).at[taker].add(passed)
    labels = jnp.searchsorted(jnp.cumsum(lengths), jnp.arange(rows * top), side="right").astype(jnp.int32)
    table = labels.reshape(top, rows).T
    table = table[jax.random.permutation(jax.random.fold_in(own, 1), rows)]
    offset_by = jax.random.randint(jax.random.fold_in(own, 2), (rows, 1), 0, top)
    return jnp.take_along_axis(table, (jnp.arange(top)[None, :] + offset_by) % top, axis=1)


def shares(count, total, bound, slope, full):
    weights = [(1 << 20) // math.isqrt(rank ** slope) + 1 for rank in range(1, count + 1)]
    largest = bound if full else min(bound, max(-(-total // count), total * weights[0] // sum(weights)))
    least = 1 if total - largest >= count - 1 else 0
    counts, spare = [largest] + [least] * (count - 1), total - largest - least * (count - 1)
    while spare > 0:
        free = [i for i in range(1, count) if counts[i] < largest] or [i for i in range(1, count) if counts[i] < bound]
        pool, left = sum([weights[i] for i in free]), spare
        for i in free:
            extra = min(bound - counts[i], max(1, left * weights[i] // pool), spare)
            counts[i] = counts[i] + extra
            spare = spare - extra
    return np.array(counts)


def gaussian(key, dims, width, most, shards=(), kind=jnp.bfloat16):
    loudness = level_of(key, dims, shards, -0.22, 0.18) if shards else 1.0
    values = jax.random.normal(key, dims, jnp.float32) * width * loudness
    return jnp.minimum(jnp.maximum(values, -most), most).astype(kind)


def setup_inputs(seed: int = 0) -> dict:
    splits = jax.random.split(jax.random.key(seed), 16)
    tokens = gaussian(splits[0], (TOKENS, D), 1.0, 6.0, ((0, 32),))
    w_query = gaussian(splits[1], (D, D), D ** -0.5, 0.125, ((0, 32),))
    w_key = gaussian(splits[2], (D, D), D ** -0.5, 0.125, ((0, 32),))
    w_value = gaussian(splits[3], (D, D), D ** -0.5, 0.125, ((0, 32),))
    w_out = gaussian(splits[4], (D, D), (max(D // 256, 1)) ** -0.5, 2.0, ((0, 32),))
    w_router = gaussian(splits[5], (D, E), (4 * D) ** -0.5, 0.0625, ((0, 32),))
    gain_attn = jnp.clip(1.0 + 0.1 * jax.random.normal(splits[6], (D,), jnp.float32), 0.5, 1.5).astype(jnp.bfloat16)
    gain_moe = jnp.clip(1.0 + 0.1 * jax.random.normal(splits[7], (D,), jnp.float32), 0.5, 1.5).astype(jnp.bfloat16)
    w_gate = gaussian(splits[8], (E * FF, D), D ** -0.5, 0.125, ((0, 32),))
    w_up = gaussian(splits[9], (E * FF, D), D ** -0.5, 0.125, ((0, 32),))
    w_down = gaussian(splits[10], (E * FF, D), (FF // 16) ** -0.5, 0.75, ((0, 32),))
    routes_keys = jax.random.split(jax.random.fold_in(splits[11], 1), TOKENS // TOK_DEV)
    routes_turns = jax.random.permutation(jax.random.fold_in(splits[11], 3), TOKENS // TOK_DEV)
    routes = jax.vmap(lambda own, number: assign_block(jax.random.fold_in(splits[11], 2), own, number, TOK_DEV, E, TOPK, CAP, 2))(routes_keys, routes_turns).reshape((TOKENS, TOPK))
    doc_lengths = jax.vmap(lambda own: ragged(own, DOCS, SEQ_LEN, SEQ_LEN // 2, 1))(jax.random.split(splits[12], SEQS)).reshape((SEQS, DOCS)).astype(jnp.int32)
    clip_limit = jnp.clip(jax.random.uniform(splits[13], (H,), jnp.float32, 3.5, 7.5), 3.5, 7.5)
    cotangent = gaussian(splits[14], (TOKENS, D), 1.0, 6.0, ((0, 32),))
    return {"tokens": tokens, "w_query": w_query, "w_key": w_key, "w_value": w_value, "w_out": w_out, "w_router": w_router, "gain_attn": gain_attn, "gain_moe": gain_moe, "w_gate": w_gate, "w_up": w_up, "w_down": w_down, "routes": routes, "doc_lengths": doc_lengths, "clip_limit": clip_limit, "cotangent": cotangent}


epsilon = 1e-05
masked = -1e+30
highest = lax.Precision.HIGHEST

@jax.custom_vjp
def low(v):
    return lax.optimization_barrier(v.astype(jnp.bfloat16)).astype(jnp.float32)

@jax.custom_vjp
def low_back(v):
    return v

def low_keep(v):
    return (low(v), None)

def low_pass(kept, grad):
    return (grad,)

def back_keep(v):
    return (v, None)

def back_low(kept, grad):
    return (low(grad),)
low.defvjp(low_keep, low_pass)
low_back.defvjp(back_keep, back_low)

def round_both(value):
    return low(low_back(value))

def rms_norm(source, gain):
    return source * lax.rsqrt(lax.optimization_barrier(jnp.mean(source * source, axis=-1, keepdims=True)) + epsilon) * gain

def document_ids(doc_lengths):
    doc_ends = jnp.cumsum(doc_lengths.astype(jnp.int32), axis=1).astype(jnp.int32)
    places = jnp.arange(SEQ_LEN, dtype=jnp.int32)
    return lax.optimization_barrier(jnp.sum((places[None, :, None] >= doc_ends[:, None, :]).astype(jnp.int32), axis=2)).astype(jnp.int32)

def attend(pieces, w_query, w_key, w_value):
    normed, doc_ids = pieces
    score_scale = HD ** (-0.5)
    queries = round_both(jnp.dot(normed, w_query, precision=highest)).reshape(SEQ_LEN, H, HD)
    key_rows = round_both(jnp.dot(normed, w_key, precision=highest)).reshape(SEQ_LEN, H, HD)
    value_rows = round_both(jnp.dot(normed, w_value, precision=highest)).reshape(SEQ_LEN, H, HD)
    scores = low_back(jnp.einsum('qhd,khd->hqk', queries, key_rows, precision=highest) * score_scale)
    places = jnp.arange(SEQ_LEN, dtype=jnp.int32)
    visible = (doc_ids[:, None] == doc_ids[None, :]) & (jnp.abs(places[:, None] - places[None, :]) < HALF)
    masked_scores = jnp.where(visible[None], scores, masked)
    head_max = lax.optimization_barrier(jnp.max(masked_scores, axis=(1, 2)))
    weights = low(jax.nn.softmax(masked_scores, axis=-1))
    context = jnp.einsum('hqk,khd->qhd', weights, value_rows, precision=highest).reshape(SEQ_LEN, H * HD)
    return (round_both(context), head_max)

def expert_step(running, pieces, normed_moe):
    gate_share, gate_rows, up_rows, down_rows = pieces
    entering = low_back(normed_moe)
    gate_pre = low_back(jnp.dot(entering, gate_rows.T, precision=highest))
    up_pre = low_back(jnp.dot(entering, up_rows.T, precision=highest))
    hidden = low(jax.nn.silu(gate_pre) * up_pre)
    result = round_both(jnp.dot(hidden, down_rows, precision=highest))
    return (running + gate_share[:, None] * result, None)

def forward(tokens, w_query, w_key, w_value, w_out, w_router, gain_attn, gain_moe, w_gate, w_up, w_down, routes, doc_ids):
    normed_attn = low(rms_norm(tokens, gain_attn))
    sequences = TOKENS // SEQ_LEN
    attention = jax.checkpoint(lambda pieces: attend(pieces, w_query, w_key, w_value))
    context, head_max = lax.map(attention, (normed_attn.reshape(sequences, SEQ_LEN, D), doc_ids))
    attended = tokens + low_back(jnp.dot(context.reshape(TOKENS, D), w_out, precision=highest))
    normed_moe = low(rms_norm(attended, gain_moe))
    logits = jnp.dot(normed_moe, w_router, precision=highest)
    chosen = jnp.take_along_axis(logits, routes, axis=1)
    gate_share = jax.nn.softmax(chosen, axis=1)
    matches = (routes[:, :, None] == jnp.arange(E, dtype=jnp.int32)[None, None, :]).astype(jnp.float32)
    per_expert = lax.optimization_barrier(jnp.sum(gate_share[:, :, None] * matches, axis=1))
    stepper = jax.checkpoint(lambda running, pieces: expert_step(running, pieces, normed_moe))
    mixture, unused = lax.scan(stepper, jnp.zeros((TOKENS, D), jnp.float32), (per_expert.T, w_gate.reshape(E, FF, D), w_up.reshape(E, FF, D), w_down.reshape(E, FF, D)))
    return (attended + mixture, lax.optimization_barrier(jnp.max(head_max, axis=0)))

def reference(tokens, w_query, w_key, w_value, w_out, w_router, gain_attn, gain_moe, w_gate, w_up, w_down, routes, doc_lengths, clip_limit, cotangent):
    doc_ids = document_ids(doc_lengths)
    floats = [array.astype(jnp.float32) for array in (tokens, w_query, w_key, w_value, w_out, w_router, gain_attn, gain_moe, w_gate, w_up, w_down)]

    def wrapped(*values):
        return forward(*values, routes, doc_ids)
    output, pullback, head_max = jax.vjp(wrapped, *floats, has_aux=True)
    grads = pullback(cotangent.astype(jnp.float32))
    factor = clip_limit / jnp.maximum(head_max, clip_limit)
    columns = jnp.repeat(jnp.sqrt(factor), HD)
    clipped_query = (floats[1] * columns[None, :]).astype(jnp.bfloat16)
    clipped_key = (floats[2] * columns[None, :]).astype(jnp.bfloat16)
    return (output.astype(jnp.bfloat16), grads[0], grads[1], grads[2], grads[3], grads[4], grads[5], grads[6], grads[7], grads[8], grads[9], grads[10], clipped_query, clipped_key)
```

```python
import functools
from functools import reduce

import jax
import jax.numpy as jnp
from jax import lax
from jax.experimental import pallas as pl
from jax.experimental.pallas import tpu as pltpu
from jax.sharding import PartitionSpec as P

HALF = 512


epsilon = 1e-05
masked = -1e30
highest = lax.Precision.HIGHEST


def passed_along(x, axis, by):
    length = lax.axis_size(axis)
    pairs = [(i, i + by) for i in range(length) if 0 <= i + by < length]
    return lax.ppermute(x, axis, pairs)


def swapped(block, axis, apart):
    count = lax.axis_size(axis)
    route = []
    for low in range(count):
        high = low | 1 << apart
        if high != low and high < count:
            route += [(low, high), (high, low)]
    return lax.ppermute(block, axis, route)


def rms_scale(source):
    return lax.rsqrt(jnp.mean(source * source, axis=-1, keepdims=True) + epsilon)


def norm_back(grad_normed, source, scale_rows, gain):
    unit_rows = source * scale_rows
    grad_unit = grad_normed * gain
    grad_gain = jnp.sum(grad_normed * unit_rows, axis=0)
    grad_source = scale_rows * (
        grad_unit - unit_rows * jnp.mean(grad_unit * unit_rows, axis=-1, keepdims=True)
    )
    return (grad_source, grad_gain)


def document_of(places, doc_lengths, seq_len):
    doc_ends = jnp.cumsum(doc_lengths, axis=1)
    seq_count = doc_lengths.shape[0]
    doc_count = doc_lengths.shape[1]
    sequence = places // seq_len
    within = places % seq_len
    picked = (sequence[:, None] == jnp.arange(seq_count, dtype=jnp.int32)[None, :]).astype(
        jnp.int32
    )
    ends_of = jnp.dot(picked, doc_ends)
    local_doc = jnp.sum((within[:, None] >= ends_of).astype(jnp.int32), axis=1)
    inside = (places >= 0) & (places < seq_count * seq_len)
    return jnp.where(inside, sequence * doc_count + local_doc, -1)


def contract(left, right, left_dim, right_dim):
    return lax.dot_general(
        left, right, (((left_dim,), (right_dim,)), ((), ())), preferred_element_type=jnp.float32
    )


def routed_layer(
    tokens,
    w_query,
    w_key,
    w_value,
    w_out,
    w_router,
    gain_attn,
    gain_moe,
    w_gate,
    w_up,
    w_down,
    routes,
    doc_lengths,
    clip_limit,
    cotangent,
):
    devices = lax.axis_size("fsdp")
    device = lax.axis_index("fsdp")
    tok_rows = tokens.shape[0]
    model_width = tokens.shape[1]
    head_count = clip_limit.shape[0]
    head_size = model_width // head_count
    experts = w_router.shape[1]
    top_count = routes.shape[1]
    seq_len = devices * tok_rows // doc_lengths.shape[0]
    score_scale = head_size ** (-0.5)
    gathered = (
        lax.all_gather(w_query, "fsdp", axis=0, tiled=True),
        lax.all_gather(w_key, "fsdp", axis=0, tiled=True),
        lax.all_gather(w_value, "fsdp", axis=0, tiled=True),
        lax.all_gather(w_out, "fsdp", axis=0, tiled=True),
        lax.all_gather(w_router, "fsdp", axis=0, tiled=True),
        lax.all_gather(gain_attn, "fsdp", axis=0, tiled=True),
        lax.all_gather(gain_moe, "fsdp", axis=0, tiled=True),
    )
    query_full, key_full, value_full, out_full, router_full, gain_one, gain_two = gathered
    token_values = tokens.astype(jnp.float32)
    scale_one = rms_scale(token_values)
    attn_gain = gain_one.astype(jnp.float32)
    normed_attn = (token_values * scale_one * attn_gain).astype(jnp.bfloat16)
    queries = jnp.dot(normed_attn, query_full, preferred_element_type=jnp.float32).astype(
        jnp.bfloat16
    )
    kv_own = jnp.concatenate(
        (
            jnp.dot(normed_attn, key_full, preferred_element_type=jnp.float32),
            jnp.dot(normed_attn, value_full, preferred_element_type=jnp.float32),
        ),
        axis=1,
    ).astype(jnp.bfloat16)
    reach_count = (HALF - 2) // tok_rows + 1
    offsets = list(range(reach_count, 0, -1)) + list(range(-1, -reach_count - 1, -1))
    arrived = [passed_along(kv_own, "fsdp", offset) for offset in offsets]
    kv_rows = jnp.concatenate(arrived[:reach_count] + [kv_own] + arrived[reach_count:], axis=0)
    ordered = offsets[:reach_count] + [0] + offsets[reach_count:]
    row_index = jnp.arange(tok_rows, dtype=jnp.int32)
    query_places = device * tok_rows + row_index
    key_places = jnp.concatenate([(device - offset) * tok_rows + row_index for offset in ordered])
    query_docs = document_of(query_places, doc_lengths, seq_len)
    key_docs = document_of(key_places, doc_lengths, seq_len)
    visible = (
        (query_docs[:, None] == key_docs[None, :])
        & (key_docs[None, :] >= 0)
        & (jnp.abs(query_places[:, None] - key_places[None, :]) < HALF)
    )
    key_count = kv_rows.shape[0]
    query_heads = queries.reshape(tok_rows, head_count, head_size)
    key_heads = kv_rows[:, :model_width].reshape(key_count, head_count, head_size)
    value_heads = kv_rows[:, model_width:].reshape(key_count, head_count, head_size)

    def scores_of():
        raw_scores = (
            jnp.einsum("qhd,khd->hqk", query_heads, key_heads, preferred_element_type=jnp.float32)
            * score_scale
        )
        return jnp.where(visible[None], raw_scores, masked)

    scores = scores_of()
    head_top = jnp.max(scores, axis=2, keepdims=True)
    exponents = jnp.exp(scores - head_top)
    totals = jnp.sum(exponents, axis=2, keepdims=True)
    log_total = head_top + jnp.log(totals)
    probs_low = (exponents / totals).astype(jnp.bfloat16)
    head_max = lax.pmax(jnp.max(head_top, axis=(1, 2)), "fsdp")
    context = (
        jnp.einsum("hqk,khd->qhd", probs_low, value_heads, preferred_element_type=jnp.float32)
        .reshape(tok_rows, model_width)
        .astype(jnp.bfloat16)
    )
    attended = token_values + jnp.dot(context, out_full, preferred_element_type=jnp.float32)
    factor = clip_limit / jnp.maximum(head_max, clip_limit)
    columns = jnp.repeat(jnp.sqrt(factor), head_size)
    clipped_query = (w_query.astype(jnp.float32) * columns[None, :]).astype(jnp.bfloat16)
    clipped_key = (w_key.astype(jnp.float32) * columns[None, :]).astype(jnp.bfloat16)
    scale_two = rms_scale(attended)
    moe_gain = gain_two.astype(jnp.float32)
    normed_moe = (attended * scale_two * moe_gain).astype(jnp.bfloat16)
    logits = jnp.dot(normed_moe, router_full, preferred_element_type=jnp.float32)
    matches = routes[:, :, None] == jnp.arange(experts, dtype=jnp.int32)[None, None, :]
    chosen = jnp.sum(jnp.where(matches, logits[:, None, :], 0.0), axis=2)
    gate_share = jax.nn.softmax(chosen, axis=1)
    pair_count = tok_rows * top_count
    capacity = 3 * tok_rows * top_count // devices
    half_cap = capacity // 2
    flat_route = routes.reshape(pair_count)
    one_hot = (flat_route[:, None] == jnp.arange(experts, dtype=jnp.int32)[None, :]).astype(
        jnp.int32
    )
    slot_rank = jnp.sum(jnp.cumsum(one_hot, axis=0) * one_hot, axis=1) - 1
    target_device = 2 * flat_route + slot_rank // half_cap
    target_slot = slot_rank % half_cap
    flat_slot = target_device * half_cap + target_slot
    slot_total = devices * half_cap
    outgoing = (
        jnp.zeros((slot_total, model_width), jnp.bfloat16)
        .at[flat_slot]
        .set(jnp.repeat(normed_moe, top_count, axis=0))
    )
    live_out = jnp.zeros((slot_total,), jnp.int32).at[flat_slot].set(1)
    incoming, live_in = (
        lax.all_to_all(outgoing, "fsdp", split_axis=0, concat_axis=0, tiled=True),
        lax.all_to_all(live_out, "fsdp", split_axis=0, concat_axis=0, tiled=True),
    )
    packed_order = jnp.cumsum(live_in) - 1
    packed_index = jnp.where(live_in > 0, packed_order, slot_total)
    back_index = jnp.clip(packed_order, 0, slot_total - 1)
    live_count = jnp.sum(live_in)
    tile_rows = 128
    tile_count = (live_count + tile_rows - 1) // tile_rows
    packed_rows = (
        jnp.zeros((slot_total + 1, model_width), jnp.bfloat16)
        .at[packed_index]
        .set(incoming)[:slot_total]
    )
    partner_half = swapped((w_gate, w_up, w_down), "fsdp", 0)
    lower = device % 2 == 0

    def joined(own_half, other_half):
        return jnp.where(
            lower, jnp.concatenate((own_half, other_half)), jnp.concatenate((other_half, own_half))
        )

    gate_full = joined(w_gate, partner_half[0])
    up_full = joined(w_up, partner_half[1])
    down_full = joined(w_down, partner_half[2])
    hidden_units = gate_full.shape[0]

    def forward_tile(tile_step, loop_state):
        out_rows, gate_keep, up_keep = loop_state
        tile_start = tile_step * tile_rows
        tile_input = lax.dynamic_slice_in_dim(packed_rows, tile_start, tile_rows, 0)
        gate_pre = contract(tile_input, gate_full, 1, 1)
        up_pre = contract(tile_input, up_full, 1, 1)
        hidden = (jax.nn.silu(gate_pre) * up_pre).astype(jnp.bfloat16)
        result = jnp.dot(hidden, down_full, preferred_element_type=jnp.float32).astype(jnp.bfloat16)
        return (
            lax.dynamic_update_slice_in_dim(out_rows, result, tile_start, 0),
            lax.dynamic_update_slice_in_dim(gate_keep, gate_pre, tile_start, 0),
            lax.dynamic_update_slice_in_dim(up_keep, up_pre, tile_start, 0),
        )

    start_state = (
        jnp.zeros((slot_total, model_width), jnp.bfloat16),
        jnp.zeros((slot_total, hidden_units), jnp.float32),
        jnp.zeros((slot_total, hidden_units), jnp.float32),
    )
    expert_out, gate_keep, up_keep = lax.fori_loop(0, tile_count, forward_tile, start_state)
    returning = jnp.where(live_in[:, None] > 0, expert_out[back_index], jnp.zeros((), jnp.bfloat16))
    came_back = lax.all_to_all(returning, "fsdp", split_axis=0, concat_axis=0, tiled=True)
    pair_out = came_back[flat_slot].reshape(tok_rows, top_count, model_width)
    mixture = jnp.sum(gate_share[:, :, None] * pair_out, axis=1)
    mixed = (attended + mixture).astype(jnp.bfloat16)
    query_back, key_back, value_back, out_back = (
        lax.all_gather(w_query, "fsdp", axis=0, tiled=True),
        lax.all_gather(w_key, "fsdp", axis=0, tiled=True),
        lax.all_gather(w_value, "fsdp", axis=0, tiled=True),
        lax.all_gather(w_out, "fsdp", axis=0, tiled=True),
    )
    grad_mixed = cotangent.astype(jnp.float32)
    grad_share = jnp.sum(grad_mixed[:, None, :] * pair_out, axis=2)
    grad_pair = (
        (gate_share[:, :, None] * grad_mixed[:, None, :])
        .astype(jnp.bfloat16)
        .reshape(pair_count, model_width)
    )
    grad_outgoing = jnp.zeros((slot_total, model_width), jnp.bfloat16).at[flat_slot].set(grad_pair)
    grad_incoming = lax.all_to_all(grad_outgoing, "fsdp", split_axis=0, concat_axis=0, tiled=True)
    grad_packed = (
        jnp.zeros((slot_total + 1, model_width), jnp.bfloat16)
        .at[packed_index]
        .set(grad_incoming)[:slot_total]
    )

    def backward_tile(tile_step, loop_state):
        grad_rows, gate_sum, up_sum, down_sum = loop_state
        tile_start = tile_step * tile_rows
        tile_input = lax.dynamic_slice_in_dim(packed_rows, tile_start, tile_rows, 0)
        tile_grad = lax.dynamic_slice_in_dim(grad_packed, tile_start, tile_rows, 0)
        gate_pre = lax.dynamic_slice_in_dim(gate_keep, tile_start, tile_rows, 0)
        up_pre = lax.dynamic_slice_in_dim(up_keep, tile_start, tile_rows, 0)
        sigmoid_gate = jax.nn.sigmoid(gate_pre)
        silu_gate = gate_pre * sigmoid_gate
        hidden = (silu_gate * up_pre).astype(jnp.bfloat16)
        grad_hidden = contract(tile_grad, down_full, 1, 1)
        grad_gate_pre = (
            grad_hidden * up_pre * sigmoid_gate * (1.0 + gate_pre * (1.0 - sigmoid_gate))
        ).astype(jnp.bfloat16)
        grad_up_pre = (grad_hidden * silu_gate).astype(jnp.bfloat16)
        down_sum = down_sum + contract(hidden, tile_grad, 0, 0)
        gate_sum = gate_sum + contract(grad_gate_pre, tile_input, 0, 0)
        up_sum = up_sum + contract(grad_up_pre, tile_input, 0, 0)
        grad_input = (
            jnp.dot(grad_gate_pre, gate_full, preferred_element_type=jnp.float32)
            + jnp.dot(grad_up_pre, up_full, preferred_element_type=jnp.float32)
        ).astype(jnp.bfloat16)
        return (
            lax.dynamic_update_slice_in_dim(grad_rows, grad_input, tile_start, 0),
            gate_sum,
            up_sum,
            down_sum,
        )

    weight_zero = jnp.zeros((hidden_units, model_width), jnp.float32)
    back_state = (
        jnp.zeros((slot_total, model_width), jnp.bfloat16),
        weight_zero,
        weight_zero,
        weight_zero,
    )
    grad_rows, gate_sum, up_sum, down_sum = lax.fori_loop(0, tile_count, backward_tile, back_state)
    grad_returning = jnp.where(
        live_in[:, None] > 0, grad_rows[back_index], jnp.zeros((), jnp.bfloat16)
    )
    grad_came = lax.all_to_all(grad_returning, "fsdp", split_axis=0, concat_axis=0, tiled=True)
    grad_from_experts = jnp.sum(
        grad_came[flat_slot].reshape(tok_rows, top_count, model_width), axis=1, dtype=jnp.float32
    )
    half_units = w_gate.shape[0]

    def partner_part(grad_sum):
        return jnp.where(lower, grad_sum[half_units:], grad_sum[:half_units])

    def own_part(grad_sum):
        return jnp.where(lower, grad_sum[:half_units], grad_sum[half_units:])

    partner_terms = (
        swapped(partner_part(gate_sum).astype(jnp.bfloat16), "fsdp", 0).astype(jnp.float32),
        swapped(partner_part(up_sum).astype(jnp.bfloat16), "fsdp", 0).astype(jnp.float32),
        swapped(partner_part(down_sum).astype(jnp.bfloat16), "fsdp", 0).astype(jnp.float32),
    )
    grad_gate = own_part(gate_sum) + partner_terms[0]
    grad_up = own_part(up_sum) + partner_terms[1]
    grad_down = own_part(down_sum) + partner_terms[2]
    grad_chosen = gate_share * (
        grad_share - jnp.sum(gate_share * grad_share, axis=1, keepdims=True)
    )
    grad_logits = jnp.sum(jnp.where(matches, grad_chosen[:, :, None], 0.0), axis=1)
    grad_router_part = jnp.dot(normed_moe.astype(jnp.float32).T, grad_logits, precision=highest)
    grad_normed_moe = grad_from_experts + jnp.dot(
        grad_logits, router_full.astype(jnp.float32).T, precision=highest
    )
    grad_from_norm, grad_gain_two = norm_back(grad_normed_moe, attended, scale_two, moe_gain)
    grad_attended = grad_mixed + grad_from_norm
    grad_attended_low = grad_attended.astype(jnp.bfloat16)
    grad_out_part = contract(context, grad_attended_low, 0, 0)
    grad_context = (
        contract(grad_attended_low, out_back, 1, 1)
        .astype(jnp.bfloat16)
        .reshape(tok_rows, head_count, head_size)
    )
    probs = jnp.exp(scores_of() - log_total)
    probs_back = probs.astype(jnp.bfloat16)
    grad_values = jnp.einsum(
        "hqk,qhd->khd", probs_back, grad_context, preferred_element_type=jnp.float32
    )
    grad_probs = jnp.einsum(
        "qhd,khd->hqk", grad_context, value_heads, preferred_element_type=jnp.float32
    )
    grad_scores = (
        probs * (grad_probs - jnp.sum(probs * grad_probs, axis=2, keepdims=True))
    ).astype(jnp.bfloat16)
    grad_queries = (
        (
            jnp.einsum("hqk,khd->qhd", grad_scores, key_heads, preferred_element_type=jnp.float32)
            * score_scale
        )
        .reshape(tok_rows, model_width)
        .astype(jnp.bfloat16)
    )
    grad_keys = (
        jnp.einsum("hqk,qhd->khd", grad_scores, query_heads, preferred_element_type=jnp.float32)
        * score_scale
    )
    grad_kv = jnp.concatenate(
        (grad_keys.reshape(key_count, model_width), grad_values.reshape(key_count, model_width)),
        axis=1,
    )
    grad_blocks = [
        grad_kv[position * tok_rows : (position + 1) * tok_rows] for position in range(len(ordered))
    ]
    own_block = grad_blocks[reach_count]
    remote = grad_blocks[:reach_count] + grad_blocks[reach_count + 1 :]
    returned = [
        passed_along(grad_block.astype(jnp.bfloat16), "fsdp", -offset).astype(grad_block.dtype)
        for grad_block, offset in zip(remote, offsets)
    ]
    grad_kv_low = reduce(jnp.add, returned, own_block).astype(jnp.bfloat16)
    grad_query_part = contract(normed_attn, grad_queries, 0, 0)
    grad_kv_part = contract(normed_attn, grad_kv_low, 0, 0)
    grad_normed_attn = (
        contract(grad_queries, query_back, 1, 1)
        + contract(grad_kv_low[:, :model_width], key_back, 1, 1)
        + contract(grad_kv_low[:, model_width:], value_back, 1, 1)
    )
    grad_from_first, grad_gain_one = norm_back(grad_normed_attn, token_values, scale_one, attn_gain)
    grad_tokens = grad_attended + grad_from_first
    reduced = (
        lax.psum_scatter(grad_query_part, "fsdp", scatter_dimension=0, tiled=True),
        lax.psum_scatter(grad_kv_part[:, :model_width], "fsdp", scatter_dimension=0, tiled=True),
        lax.psum_scatter(grad_kv_part[:, model_width:], "fsdp", scatter_dimension=0, tiled=True),
        lax.psum_scatter(grad_out_part, "fsdp", scatter_dimension=0, tiled=True),
        lax.psum_scatter(grad_router_part, "fsdp", scatter_dimension=0, tiled=True),
        lax.psum_scatter(grad_gain_one, "fsdp", scatter_dimension=0, tiled=True),
        lax.psum_scatter(grad_gain_two, "fsdp", scatter_dimension=0, tiled=True),
    )
    return (
        mixed,
        grad_tokens,
        reduced[0],
        reduced[1],
        reduced[2],
        reduced[3],
        reduced[4],
        reduced[5],
        reduced[6],
        grad_gate,
        grad_up,
        grad_down,
        clipped_query,
        clipped_key,
    )


MESH = pl.DeviceIdType.MESH
f32 = jnp.float32
bf = jnp.bfloat16

def place():
    me = lax.axis_index("fsdp")
    core = lax.rem(me, 2)
    x = lax.rem(lax.div(me, 2), 2)
    y = lax.rem(lax.div(me, 4), 2)
    z = lax.div(me, 8)
    return z, y, x, core

def index_of(z, y, x, core):
    return ((z * 2 + y) * 2 + x) * 2 + core

def remote(src, dst, send, recv, device):
    return pltpu.make_async_remote_copy(
        src_ref=src, dst_ref=dst, send_sem=send, recv_sem=recv, device_id=(device,), device_id_type=MESH)

def greet(devices, conditions):
    barrier = pltpu.get_barrier_semaphore()
    for device, condition in zip(devices, conditions):
        if condition is None:
            pl.semaphore_signal(barrier, inc=1, device_id=(device,), device_id_type=MESH)
        else:
            @pl.when(condition)
            def _(device=device):
                pl.semaphore_signal(barrier, inc=1, device_id=(device,), device_id_type=MESH)
    count = 0
    for condition in conditions:
        count = count + (1 if condition is None else jnp.where(condition, 1, 0))
    pl.semaphore_wait(barrier, count)

def line_items(z):
    low = z < 2
    near = z + 1 - 2 * lax.rem(z, 2)
    return [z, near, jnp.where(low, 2, 1), jnp.where(low, 3, 0)]

def gather_plane(ins, outs, ssem, rsem, lsem):
    count = len(ins)
    z, y, x, core = place()
    mid = (z == 1) | (z == 2)
    up, down = z < 3, z > 0
    y_dev = index_of(z, 1 - y, x, core)
    up_dev = index_of(jnp.minimum(z + 1, 3), y, x, core)
    down_dev = index_of(jnp.maximum(z - 1, 0), y, x, core)
    greet([y_dev, up_dev, down_dev], [None, up, down])
    own = [pltpu.make_async_copy(ins[a], outs[a].at[z * 2 + y], lsem.at[a]) for a in range(count)]
    for copy in own:
        copy.start()
    pending = []

    def go(kind, a, o, src, device, condition=None):
        def make():
            return remote(src, outs[a].at[o * 2 + y], ssem.at[kind, o, a], rsem.at[kind, o, a], device)
        if condition is None:
            make().start()
        else:
            pl.when(condition)(lambda: make().start())
        pending.append((make, condition))

    for i, o in enumerate(line_items(z)):
        for a in range(count):
            src = ins[a] if i == 0 else outs[a].at[o * 2 + y]
            if i == 0:
                go(0, a, o, src, up_dev, up)
                go(1, a, o, src, down_dev, down)
            else:
                from_below = o < z
                for kind, condition in ((0, from_below), (1, jnp.logical_not(from_below))):
                    @pl.when(condition)
                    def _(kind=kind, a=a, o=o, src=src):
                        remote(src, src, ssem.at[kind, o, a], rsem.at[kind, o, a], y_dev).wait_recv()
                go(0, a, o, src, up_dev, mid & from_below)
                go(1, a, o, src, down_dev, mid & jnp.logical_not(from_below))
            go(2, a, o, src, y_dev)
    for i, o in enumerate(line_items(z)):
        for a in range(count):
            land = outs[a].at[o * 2 + 1 - y]
            remote(land, land, ssem.at[2, o, a], rsem.at[2, o, a], y_dev).wait_recv()
    for make, condition in pending:
        if condition is None:
            make().wait_send()
        else:
            pl.when(condition)(lambda make=make: make().wait_send())
    for copy in own:
        copy.wait()

def plane_gather(arrays, cid):
    count = len(arrays)
    anys = pl.BlockSpec(memory_space=pl.ANY)
    def body(*refs):
        gather_plane(refs[:count], refs[count:2 * count], *refs[2 * count:])
    return pl.pallas_call(
        body, in_specs=[anys] * count, out_specs=[anys] * count,
        out_shape=[jax.ShapeDtypeStruct((8,) + a.shape, a.dtype) for a in arrays],
        scratch_shapes=[pltpu.SemaphoreType.DMA((3, 4, count)), pltpu.SemaphoreType.DMA((3, 4, count)),
                        pltpu.SemaphoreType.DMA((count,))],
        compiler_params=pltpu.CompilerParams(collective_id=cid, has_side_effects=True),
        name="plane_gather")(*arrays)

def gather_all(ins, outs, ssem, rsem, lsem):
    count = len(ins)
    z, y, x, core = place()
    mid = (z == 1) | (z == 2)
    up, down = z < 3, z > 0
    x_dev = index_of(z, y, 1 - x, core)
    y_dev = index_of(z, 1 - y, x, core)
    c_dev = index_of(z, y, x, 1 - core)
    up_dev = index_of(jnp.minimum(z + 1, 3), y, x, core)
    down_dev = index_of(jnp.maximum(z - 1, 0), y, x, core)
    greet([x_dev, y_dev, c_dev, up_dev, down_dev], [None, None, None, up, down])
    own = [pltpu.make_async_copy(ins[a], outs[a].at[index_of(z, y, x, core)], lsem.at[a]) for a in range(count)]
    for copy in own:
        copy.start()
    pending = []

    def go(kind, a, o, src, dst, device, condition=None):
        def make():
            return remote(src, dst, ssem.at[kind, o, a], rsem.at[kind, o, a], device)
        if condition is None:
            make().start()
        else:
            pl.when(condition)(lambda: make().start())
        pending.append((make, condition))

    def arrived(kind, a, o, land):
        remote(land, land, ssem.at[kind, o, a], rsem.at[kind, o, a], c_dev).wait_recv()

    items = line_items(z)

    def first(i):
        o = items[i]
        for a in range(count):
            slot = index_of(o, y, x, core)
            dst = outs[a].at[slot]
            src = ins[a] if i == 0 else dst
            if i == 0:
                go(0, a, o, src, dst, up_dev, up)
                go(1, a, o, src, dst, down_dev, down)
            else:
                from_below = o < z
                for kind, condition in ((0, from_below), (1, jnp.logical_not(from_below))):
                    pl.when(condition)(lambda kind=kind, a=a, o=o, dst=dst: arrived(kind, a, o, dst))
                go(0, a, o, src, dst, up_dev, mid & from_below)
                go(1, a, o, src, dst, down_dev, mid & jnp.logical_not(from_below))
            go(2, a, o, src, dst, x_dev)
            go(3, a, o, src, dst, y_dev)
            go(6, a, o, src, dst, c_dev)

    def second(i):
        o = items[i]
        for a in range(count):
            half = ins[a].shape[0] // 2
            from_x = outs[a].at[index_of(o, y, 1 - x, core)]
            arrived(2, a, o, from_x)
            go(5, a, o, from_x.at[pl.ds(0, half)], from_x.at[pl.ds(0, half)], y_dev)
            from_y = outs[a].at[index_of(o, 1 - y, x, core)]
            arrived(3, a, o, from_y)
            go(4, a, o, from_y.at[pl.ds(half, half)], from_y.at[pl.ds(half, half)], x_dev)
            go(7, a, o, from_x, from_x, c_dev)
            go(8, a, o, from_y, from_y, c_dev)

    def third(i):
        o = items[i]
        for a in range(count):
            half = ins[a].shape[0] // 2
            corner = outs[a].at[index_of(o, 1 - y, 1 - x, core)]
            arrived(5, a, o, corner.at[pl.ds(0, half)])
            arrived(4, a, o, corner.at[pl.ds(half, half)])
            go(9, a, o, corner, corner, c_dev)

    first(0); first(1); second(0); first(2); second(1); third(0); first(3); second(2); third(1); second(3); third(2); third(3)
    for i in range(4):
        o = items[i]
        for a in range(count):
            for kind, (yy, xx) in ((6, (y, x)), (7, (y, 1 - x)), (8, (1 - y, x)), (9, (1 - y, 1 - x))):
                arrived(kind, a, o, outs[a].at[index_of(o, yy, xx, 1 - core)])
    for make, condition in pending:
        if condition is None:
            make().wait_send()
        else:
            pl.when(condition)(lambda make=make: make().wait_send())
    for copy in own:
        copy.wait()

def full_gather(arrays, cid):
    count = len(arrays)
    anys = pl.BlockSpec(memory_space=pl.ANY)
    def body(*refs):
        gather_all(refs[:count], refs[count:2 * count], *refs[2 * count:])
    return pl.pallas_call(
        body, in_specs=[anys] * count, out_specs=[anys] * count,
        out_shape=[jax.ShapeDtypeStruct((32,) + a.shape, a.dtype) for a in arrays],
        scratch_shapes=[pltpu.SemaphoreType.DMA((10, 4, count)), pltpu.SemaphoreType.DMA((10, 4, count)),
                        pltpu.SemaphoreType.DMA((count,))],
        compiler_params=pltpu.CompilerParams(collective_id=cid, has_side_effects=True),
        name="full_gather")(*arrays)

def add_into(target, *terms, rows=16):
    total = target.shape[0]
    step = min(rows, total)
    def one(r, carry):
        part = pl.ds(pl.multiple_of(r * step, step), step)
        value = target[part, :].astype(f32)
        for term in terms:
            value = value + term[part, :].astype(f32)
        target[part, :] = value.astype(target.dtype)
        return carry
    lax.fori_loop(0, total // step, one, 0)

def reduce_plane(parts, outs, accs, yrecvs, zrecvs, ssem, rsem, lsem, osem, ahead=3):
    count = len(parts)
    z, y, x, core = place()
    mid = (z == 1) | (z == 2)
    up, down = z < 3, z > 0
    y_dev = index_of(z, 1 - y, x, core)
    up_dev = index_of(jnp.minimum(z + 1, 3), y, x, core)
    down_dev = index_of(jnp.maximum(z - 1, 0), y, x, core)
    greet([y_dev, up_dev, down_dev], [None, up, down])
    items = line_items(z)[::-1]
    order = [(a, i) for a in range(count) for i in range(4)]
    loads = {}
    for a, i in order:
        o = items[i]
        copy = pltpu.make_async_copy(parts[a].at[o * 2 + y], accs[a].at[o], lsem.at[o, a])
        copy.start()
        loads[a, i] = copy
    pending = []

    def y_copy(a, i):
        o = items[i]
        return remote(parts[a].at[o * 2 + 1 - y], yrecvs[a].at[o], ssem.at[0, o, a], rsem.at[0, o, a], y_dev)

    for a, i in order[:ahead]:
        y_copy(a, i).start()
    for k, (a, i) in enumerate(order):
        o = items[i]
        y_copy(a, i).wait_recv()
        if k + ahead < len(order):
            y_copy(*order[k + ahead]).start()
        loads[a, i].wait()
        acc = accs[a].at[o]
        if i < 3:
            @pl.when(mid)
            def _(a=a, o=o, acc=acc):
                land = zrecvs[a].at[o]
                remote(land, land, ssem.at[1, o, a], rsem.at[1, o, a], y_dev).wait_recv()
                add_into(acc, yrecvs[a].at[o], land)
            @pl.when(jnp.logical_not(mid))
            def _(a=a, o=o, acc=acc):
                add_into(acc, yrecvs[a].at[o])
            rising = o > z
            for sign, dev in ((1, up_dev), (-1, down_dev)):
                condition = rising if sign > 0 else jnp.logical_not(rising)
                def make(a=a, o=o, acc=acc, sign=sign, dev=dev):
                    slot = o if sign > 0 else jnp.where(z - 1 == o, 4, o)
                    return remote(acc, zrecvs[a].at[slot], ssem.at[1, o, a], rsem.at[1, slot, a], dev)
                pl.when(condition)(lambda make=make: make().start())
                pending.append((make, condition))
        else:
            for condition, slots in ((z == 0, (4,)), (z == 3, (3,)), (mid, (None, 4))):
                @pl.when(condition)
                def _(a=a, o=o, acc=acc, slots=slots):
                    terms = [yrecvs[a].at[o]]
                    for slot in slots:
                        slot = o if slot is None else slot
                        land = zrecvs[a].at[slot]
                        remote(land, land, ssem.at[1, o, a], rsem.at[1, slot, a], y_dev).wait_recv()
                        terms.append(land)
                    add_into(acc, *terms)
            out = pltpu.make_async_copy(acc, outs[a], osem.at[a])
            out.start()
            pending.append((lambda out=out: out, "local"))
    for a, i in order:
        y_copy(a, i).wait_send()
    for make, condition in pending:
        if condition == "local" if isinstance(condition, str) else False:
            make().wait()
        else:
            pl.when(condition)(lambda make=make: make().wait_send())

def plane_reduce(parts, cid):
    count = len(parts)
    anys = pl.BlockSpec(memory_space=pl.ANY)
    def body(*refs):
        it = iter(refs)
        take = lambda n: [next(it) for _ in range(n)]
        ins, outs, accs, yr, zr = take(count), take(count), take(count), take(count), take(count)
        reduce_plane(ins, outs, accs, yr, zr, *it)
    shape = [p.shape[1:] for p in parts]
    sem = pltpu.SemaphoreType.DMA
    return pl.pallas_call(
        body, in_specs=[anys] * count, out_specs=[anys] * count,
        out_shape=[jax.ShapeDtypeStruct(s, p.dtype) for s, p in zip(shape, parts)],
        scratch_shapes=[pltpu.VMEM((n,) + s, p.dtype) for n in (4, 4, 5) for s, p in zip(shape, parts)]
        + [sem((2, 5, count)), sem((2, 5, count)), sem((4, count)), sem((count,))],
        compiler_params=pltpu.CompilerParams(collective_id=cid, has_side_effects=True, vmem_limit_bytes=56 * 2**20),
        name="plane_reduce")(*parts)

def reduce_all(parts, outs, accs, crecvs, dxs, dys, xrecvs, yrecvs, zrecvs, ssem, rsem, lsem, osem):
    count = len(parts)
    z, y, x, core = place()
    mid = (z == 1) | (z == 2)
    up, down = z < 3, z > 0
    x_dev = index_of(z, y, 1 - x, core)
    y_dev = index_of(z, 1 - y, x, core)
    c_dev = index_of(z, y, x, 1 - core)
    up_dev = index_of(jnp.minimum(z + 1, 3), y, x, core)
    down_dev = index_of(jnp.maximum(z - 1, 0), y, x, core)
    greet([x_dev, y_dev, c_dev, up_dev, down_dev], [None, None, None, up, down])
    items = line_items(z)[::-1]
    mine, xp, yp, dp = y * 2 + x, y * 2 + 1 - x, (1 - y) * 2 + x, (1 - y) * 2 + 1 - x
    pending = []

    def go(make, condition=None):
        if condition is None:
            make().start()
        else:
            pl.when(condition)(lambda: make().start())
        pending.append((make, condition))

    def arrived(kind, a, o, land):
        remote(land, land, ssem.at[kind, 0, a], rsem.at[kind, o, a], c_dev).wait_recv()

    loads = {}
    for i, o in enumerate(items):
        for a in range(count):
            go(lambda o=o, a=a: remote(parts[a].at[pl.ds(o * 4, 4), 1 - core], crecvs[a].at[o],
                                       ssem.at[0, o, a], rsem.at[0, o, a], c_dev))
            loads[i, a] = pltpu.make_async_copy(parts[a].at[pl.ds(o * 4, 4), core], accs[a].at[o], lsem.at[o, a])
            loads[i, a].start()

    def first(i):
        o = items[i]
        for a in range(count):
            half = parts[a].shape[2] // 2
            arrived(0, a, o, crecvs[a].at[o])
            loads[i, a].wait()
            for p in (dp, xp, yp, mine):
                add_into(accs[a].at[o, p], crecvs[a].at[o, p])
                if p is dp:
                    go(lambda a=a, half=half: remote(accs[a].at[o, dp, pl.ds(0, half)], dxs[a].at[o], ssem.at[1, o, a], rsem.at[1, o, a], x_dev))
                    go(lambda a=a, half=half: remote(accs[a].at[o, dp, pl.ds(half, half)], dys[a].at[o], ssem.at[2, o, a], rsem.at[2, o, a], y_dev))

    def second(i):
        o = items[i]
        for a in range(count):
            half = parts[a].shape[2] // 2
            arrived(1, a, o, dxs[a].at[o])
            add_into(accs[a].at[o, yp, pl.ds(0, half)], dxs[a].at[o])
            go(lambda a=a, half=half: remote(accs[a].at[o, yp], yrecvs[a].at[o], ssem.at[4, o, a], rsem.at[4, o, a], y_dev))
            arrived(2, a, o, dys[a].at[o])
            add_into(accs[a].at[o, xp, pl.ds(half, half)], dys[a].at[o])
            go(lambda a=a, half=half: remote(accs[a].at[o, xp], xrecvs[a].at[o], ssem.at[3, o, a], rsem.at[3, o, a], x_dev))

    def third(i):
        o = items[i]
        for a in range(count):
            acc = accs[a].at[o, mine]
            arrived(3, a, o, xrecvs[a].at[o])
            arrived(4, a, o, yrecvs[a].at[o])
            if i < 3:
                @pl.when(mid)
                def _():
                    arrived(5, a, o, zrecvs[a].at[o])
                    add_into(acc, xrecvs[a].at[o], yrecvs[a].at[o], zrecvs[a].at[o])
                @pl.when(jnp.logical_not(mid))
                def _():
                    add_into(acc, xrecvs[a].at[o], yrecvs[a].at[o])
                rising = o > z
                go(lambda o=o, a=a, acc=acc: remote(acc, zrecvs[a].at[o], ssem.at[5, o, a], rsem.at[5, o, a], up_dev), rising)
                def lower(o=o, a=a, acc=acc):
                    slot = jnp.where(z - 1 == o, 4, o)
                    return remote(acc, zrecvs[a].at[slot], ssem.at[5, o, a], rsem.at[5, slot, a], down_dev)
                go(lower, jnp.logical_not(rising))
            else:
                for condition, slots in ((z == 0, (4,)), (z == 3, (3,)), (mid, (None, 4))):
                    @pl.when(condition)
                    def _(slots=slots):
                        terms = [xrecvs[a].at[o], yrecvs[a].at[o]]
                        for slot in slots:
                            slot = o if slot is None else slot
                            arrived(5, a, slot, zrecvs[a].at[slot])
                            terms.append(zrecvs[a].at[slot])
                        rows, step = outs[a].shape[0], 16
                        def one(r, carry):
                            part = pl.ds(pl.multiple_of(r * step, step), step)
                            value = acc[part, :].astype(f32)
                            for term in terms:
                                value = value + term[part, :].astype(f32)
                            outs[a][part, :] = value
                            return carry
                        lax.fori_loop(0, rows // step, one, 0)

    first(0); first(1); second(0); first(2); second(1); third(0); first(3); second(2); third(1); second(3); third(2); third(3)
    for make, condition in pending:
        if condition is None:
            make().wait_send()
        else:
            pl.when(condition)(lambda make=make: make().wait_send())

def full_reduce(parts, cid):
    count = len(parts)
    anys = pl.BlockSpec(memory_space=pl.ANY)
    def body(*refs):
        it = iter(refs)
        take = lambda n: [next(it) for _ in range(n)]
        reduce_all(*[take(count) for _ in range(9)], *it)
    sem = pltpu.SemaphoreType.DMA
    scratch = []
    for lead, cut in (((4, 4), 1), ((4, 4), 1), ((4,), 2), ((4,), 2), ((4,), 1), ((4,), 1), ((5,), 1)):
        scratch += [pltpu.VMEM(lead + (p.shape[2] // cut, p.shape[3]), p.dtype) for p in parts]
    return pl.pallas_call(
        body, in_specs=[anys] * count, out_specs=[pl.BlockSpec(memory_space=pltpu.VMEM)] * count,
        out_shape=[jax.ShapeDtypeStruct(p.shape[2:], f32) for p in parts],
        scratch_shapes=scratch + [sem((6, 5, count)), sem((6, 5, count)), sem((4, count)), sem((count,))],
        compiler_params=pltpu.CompilerParams(collective_id=cid, has_side_effects=True, vmem_limit_bytes=62 * 2**20),
        name="full_reduce")(*parts)
def nt(left, right):
    return lax.dot_general(left, right, (((1,), (1,)), ((), ())), preferred_element_type=f32)


def tn(left, right):
    return lax.dot_general(left, right, (((0,), (0,)), ((), ())), preferred_element_type=f32)


def nn(left, right):
    return lax.dot_general(left, right, (((1,), (0,)), ((), ())), preferred_element_type=f32)


def expert_body(rows, width, half, tile, block, cut, *refs):
    it = iter(refs)
    take = lambda n: [next(it) for _ in range(n)]
    x_hbm, c_hbm, s_hbm = take(3)
    weights = [[take(2) for _ in range(3)] for _ in range(2)]
    mix, gx, gs = take(3)
    grads = [take(2) for _ in range(2)]
    xv, cv, sv, wv, acc, hid_s, gate_s, up_s, gst, ostage, prev, stage = take(12)
    wsem, insem, osem, psem, dsem, gsem = take(6)
    hidden = 2 * half
    shard = s_hbm.shape[1] - 8
    per_tile = tile // shard
    tiles = rows // tile
    cuts = width // cut
    steps = tiles * cuts
    chip = lax.div(lax.axis_index("fsdp"), 2)
    experts = (chip, chip + 1 - 2 * lax.rem(chip, 2))
    lane = lax.broadcasted_iota(jnp.int32, (1, 128), 1)

    def incoming(t, slot):
        copies = []
        for r in range(per_tile):
            part = pl.ds(r * shard, shard)
            copies += [
                pltpu.make_async_copy(x_hbm.at[t * per_tile + r], xv.at[slot, part], insem.at[0, r, slot]),
                pltpu.make_async_copy(c_hbm.at[t * per_tile + r], cv.at[slot, part], insem.at[1, r, slot]),
                pltpu.make_async_copy(
                    s_hbm.at[t * per_tile + r, pl.ds(0, shard)], sv.at[slot, part], insem.at[2, r, slot]
                ),
            ]
        return copies

    def spot(k):
        t, n = lax.div(k, cuts), lax.rem(k, cuts)
        return pl.ds(pl.multiple_of(t * tile, tile), tile), pl.ds(pl.multiple_of(n * cut, cut), cut)

    def outgoing(k, slot):
        r, c = spot(k)
        return [
            pltpu.make_async_copy(ostage.at[slot, i], ref.at[r, c], osem.at[i, slot])
            for i, ref in enumerate((mix, gx))
        ]

    def earlier(k, slot):
        r, c = spot(k)
        return [
            pltpu.make_async_copy(ref.at[r, c], prev.at[slot, i], psem.at[i, slot])
            for i, ref in enumerate((mix, gx))
        ]

    for number in range(2):
        loads = [
            pltpu.make_async_copy(weights[number][i][h], wv.at[i, pl.ds(h * half, half)], wsem.at[i, h])
            for i in range(3)
            for h in range(2)
        ]
        for copy in loads:
            copy.start()
        for copy in incoming(0, 0):
            copy.start()
        if number:
            for copy in earlier(0, 0):
                copy.start()
        acc[...] = jnp.zeros_like(acc)
        for copy in loads:
            copy.wait()
        pick = (lane == experts[number]).astype(f32)

        def one_tile(t, carry, number=number, pick=pick):
            slot = lax.rem(t, 2)

            @pl.when(t + 1 < tiles)
            def _():
                for copy in incoming(t + 1, 1 - slot):
                    copy.start()

            for copy in incoming(t, slot):
                copy.wait()
            share = jnp.sum(sv[slot] * pick, axis=1, keepdims=True)

            def hidden_block(j, dots):
                part = pl.ds(pl.multiple_of(j * block, block), block)
                x, c = xv[slot], cv[slot]
                gate_pre = nt(x, wv[0, part, :])
                up_pre = nt(x, wv[1, part, :])
                grad_raw = nt(c, wv[2, part, :])
                sig = jax.nn.sigmoid(gate_pre)
                silu = gate_pre * sig
                hid = silu * up_pre
                low = hid.astype(bf).astype(f32)
                dots = dots + jnp.sum(low * grad_raw, axis=1, keepdims=True)
                grad_hid = grad_raw * share
                grad_gate = (grad_hid * up_pre * sig * (1.0 + gate_pre * (1.0 - sig))).astype(bf)
                grad_up = (grad_hid * silu).astype(bf)
                shared = (low * share).astype(bf)
                hid_s[:, part] = shared
                gate_s[:, part] = grad_gate
                up_s[:, part] = grad_up
                acc[0, part, :] += tn(grad_gate, x)
                acc[1, part, :] += tn(grad_up, x)
                acc[2, part, :] += tn(shared, c)
                return dots

            dots = lax.fori_loop(0, hidden // block, hidden_block, jnp.zeros((tile, 1), f32))
            both = dots * pick
            for r in range(per_tile):
                turned = jnp.transpose(both[r * shard : (r + 1) * shard, :])[: gst.shape[1], :]
                spot_now = t * per_tile + r
                gst[spot_now] = gst[spot_now] + turned if number else turned

            def column_block(n, inner):
                k = t * cuts + n
                place_now = lax.rem(k, 2)
                columns = pl.ds(pl.multiple_of(n * cut, cut), cut)

                @pl.when(k >= 2)
                def _():
                    for copy in outgoing(k - 2, place_now):
                        copy.wait()

                out = nn(hid_s[...], wv[2, :, columns])
                back = nn(gate_s[...], wv[0, :, columns]) + nn(up_s[...], wv[1, :, columns])
                if number:
                    @pl.when(k + 1 < steps)
                    def _():
                        for copy in earlier(k + 1, 1 - place_now):
                            copy.start()

                    for copy in earlier(k, place_now):
                        copy.wait()
                    out = out + prev[place_now, 0].astype(f32)
                    back = back + prev[place_now, 1].astype(f32)
                ostage[place_now, 0] = out.astype(bf)
                ostage[place_now, 1] = back.astype(bf)
                for copy in outgoing(k, place_now):
                    copy.start()
                return inner

            lax.fori_loop(0, cuts, column_block, 0)
            return carry

        lax.fori_loop(0, tiles, one_tile, 0)
        for k in (steps - 2, steps - 1):
            for copy in outgoing(k, k % 2):
                copy.wait()
        chunk = stage.shape[1]
        per_half = half // chunk
        spots = [(i, h, r) for i in range(3) for h in range(2) for r in range(per_half)]

        def flush(k, number=number):
            i, h, r = spots[k]
            return pltpu.make_async_copy(
                stage.at[k % 2], grads[number][h].at[i, pl.ds(r * chunk, chunk)], dsem.at[k % 2]
            )

        for k, (i, h, r) in enumerate(spots):
            if k >= 2:
                flush(k - 2).wait()
            first = h * half + r * chunk
            stage[k % 2] = acc[i, first : first + chunk, :].astype(bf)
            flush(k).start()
        for k in (len(spots) - 2, len(spots) - 1):
            flush(k).wait()
    last = pltpu.make_async_copy(gst, gs, gsem)
    last.start()
    last.wait()


def expert_pass(x_all, c_all, s_all, weights, gs_rows):
    blocks, shard, width = x_all.shape
    rows = blocks * shard
    half = weights[0][0][0].shape[0]
    hidden = 2 * half
    tile, block, cut = 2 * shard, half, 512
    anys = pl.BlockSpec(memory_space=pl.ANY)
    sem = pltpu.SemaphoreType.DMA
    flat = [w for one in weights for pair in one for w in pair]
    shapes = [
        jax.ShapeDtypeStruct((rows, width), bf),
        jax.ShapeDtypeStruct((rows, width), bf),
        jax.ShapeDtypeStruct((blocks, gs_rows, shard), f32),
    ] + [jax.ShapeDtypeStruct((3, half, width), bf)] * 4
    return pl.pallas_call(
        functools.partial(expert_body, rows, width, half, tile, block, cut),
        in_specs=[anys] * (3 + len(flat)),
        out_specs=[anys] * 7,
        out_shape=shapes,
        scratch_shapes=[
            pltpu.VMEM((2, tile, width), bf),
            pltpu.VMEM((2, tile, width), bf),
            pltpu.VMEM((2, tile, 128), f32),
            pltpu.VMEM((3, hidden, width), bf),
            pltpu.VMEM((3, hidden, width), f32),
            pltpu.VMEM((tile, hidden), bf),
            pltpu.VMEM((tile, hidden), bf),
            pltpu.VMEM((tile, hidden), bf),
            pltpu.VMEM((blocks, gs_rows, shard), f32),
            pltpu.VMEM((2, 2, tile, cut), bf),
            pltpu.VMEM((2, 2, tile, cut), bf),
            pltpu.VMEM((2, 64, width), bf),
            sem((3, 2)),
            sem((3, 2, 2)),
            sem((2, 2)),
            sem((2, 2)),
            sem((2,)),
            sem,
        ],
        compiler_params=pltpu.CompilerParams(vmem_limit_bytes=63 * 2**20),
        name="expert_pass",
    )(x_all, c_all, s_all, *flat)
def dense_layer(
    tokens,
    w_query,
    w_key,
    w_value,
    w_out,
    w_router,
    gain_attn,
    gain_moe,
    w_gate,
    w_up,
    w_down,
    routes,
    doc_lengths,
    clip_limit,
    cotangent,
):
    devices = lax.axis_size("fsdp")
    device = lax.axis_index("fsdp")
    tok_rows = tokens.shape[0]
    model_width = tokens.shape[1]
    weight_rows = w_query.shape[0]
    head_count = clip_limit.shape[0]
    head_size = model_width // head_count
    experts = w_router.shape[1]
    seq_len = devices * tok_rows // doc_lengths.shape[0]
    score_scale = head_size ** (-0.5)
    wide_width = 3 * model_width
    extra = jnp.pad(
        jnp.concatenate((w_router, gain_attn[:, None], gain_moe[:, None]), axis=1),
        ((0, 0), (0, 128 - experts - 2)),
    )
    wide_own = jnp.concatenate((w_query, w_key, w_value, extra), axis=1)
    wide_full, out_full = full_gather([wide_own, w_out], 2)
    wide_full = wide_full.reshape(model_width, wide_width + 128)
    out_full = out_full.reshape(model_width, model_width)
    later = lax.optimization_barrier((out_full, cotangent, w_gate, w_up, w_down))
    out_full, cot_own, gate_own, up_own, down_own = later
    planes = [
        [index_of(z, y, x, core) for z in range(4) for y in range(2)] for x in range(2) for core in range(2)
    ]
    c_all = lax.all_gather(cot_own, "fsdp", axis_index_groups=planes)
    x_weights = [swapped(w, "fsdp", 1) for w in (gate_own, up_own, down_own)]
    core_weights = [swapped(w, "fsdp", 0) for w in (gate_own, up_own, down_own)]
    corner_weights = [swapped(w, "fsdp", 0) for w in x_weights]
    expert_weights = [
        list(zip((gate_own, up_own, down_own), core_weights)),
        list(zip(x_weights, corner_weights)),
    ]
    router_full = wide_full[:, wide_width : wide_width + experts]
    gain_one = wide_full[:, wide_width + experts]
    gain_two = wide_full[:, wide_width + experts + 1]
    token_values = tokens.astype(f32)
    scale_one = rms_scale(token_values)
    attn_gain = gain_one.astype(f32)
    normed_attn = (token_values * scale_one * attn_gain).astype(bf)
    qkv = jnp.dot(normed_attn, wide_full, preferred_element_type=f32).astype(bf)
    queries = qkv[:, :model_width]
    kv_own = qkv[:, model_width:wide_width]
    reach_count = (HALF - 2) // tok_rows + 1
    offsets = list(range(reach_count, 0, -1)) + list(range(-1, -reach_count - 1, -1))
    arrived = [passed_along(kv_own, "fsdp", offset) for offset in offsets]
    kv_rows = jnp.concatenate(arrived[:reach_count] + [kv_own] + arrived[reach_count:], axis=0)
    ordered = offsets[:reach_count] + [0] + offsets[reach_count:]
    row_index = jnp.arange(tok_rows, dtype=jnp.int32)
    query_places = device * tok_rows + row_index
    key_places = jnp.concatenate([(device - offset) * tok_rows + row_index for offset in ordered])
    query_docs = document_of(query_places, doc_lengths, seq_len)
    key_docs = document_of(key_places, doc_lengths, seq_len)
    visible = (
        (query_docs[:, None] == key_docs[None, :])
        & (key_docs[None, :] >= 0)
        & (jnp.abs(query_places[:, None] - key_places[None, :]) < HALF)
    )
    key_count = kv_rows.shape[0]
    query_heads = queries.reshape(tok_rows, head_count, head_size)
    key_heads = kv_rows[:, :model_width].reshape(key_count, head_count, head_size)
    value_heads = kv_rows[:, model_width:].reshape(key_count, head_count, head_size)

    def scores_of():
        raw_scores = (
            jnp.einsum("qhd,khd->hqk", query_heads, key_heads, preferred_element_type=f32)
            * score_scale
        )
        return jnp.where(visible[None], raw_scores, masked)

    scores = scores_of()
    head_top = jnp.max(scores, axis=2, keepdims=True)
    exponents = jnp.exp(scores - head_top)
    totals = jnp.sum(exponents, axis=2, keepdims=True)
    log_total = head_top + jnp.log(totals)
    probs_low = (exponents / totals).astype(bf)
    own_top = jnp.max(head_top, axis=(1, 2))
    context = (
        jnp.einsum("hqk,khd->qhd", probs_low, value_heads, preferred_element_type=f32)
        .reshape(tok_rows, model_width)
        .astype(bf)
    )
    attended = token_values + jnp.dot(context, out_full, preferred_element_type=f32)
    scale_two = rms_scale(attended)
    moe_gain = gain_two.astype(f32)
    normed_moe = (attended * scale_two * moe_gain).astype(bf)
    logits = jnp.dot(normed_moe, router_full, preferred_element_type=f32)
    named = jnp.any(routes[:, :, None] == jnp.arange(experts, dtype=jnp.int32)[None, None, :], axis=1)
    chosen = jnp.where(named, logits, masked)
    lifted = jnp.where(named, jnp.exp(logits - jnp.max(chosen, axis=1, keepdims=True)), 0.0)
    gate_share = lifted / jnp.sum(lifted, axis=1, keepdims=True)
    share_rows = jnp.concatenate(
        (
            jnp.pad(gate_share, ((0, 0), (0, 128 - experts))),
            jnp.pad(own_top[None, :], ((0, 7), (0, 128 - head_count))),
        ),
        axis=0,
    )
    x_all, s_all = plane_gather([normed_moe, share_rows], 0)
    head_max = jnp.max(s_all[:, tok_rows, :head_count], axis=0)
    head_max = jnp.maximum(head_max, swapped(head_max, "fsdp", 0))
    head_max = jnp.maximum(head_max, swapped(head_max, "fsdp", 1))
    factor = clip_limit / jnp.maximum(head_max, clip_limit)
    columns = jnp.repeat(jnp.sqrt(factor), head_size)
    clipped_query = (w_query.astype(f32) * columns[None, :]).astype(bf)
    clipped_key = (w_key.astype(f32) * columns[None, :]).astype(bf)
    mix_part, gx_part, gs_part, own_grads, core_grads, x_grads, corner_grads = expert_pass(
        x_all, c_all, s_all, expert_weights, experts
    )
    plane_shape = x_all.shape
    grad_from_experts, grad_share, mixture = plane_reduce(
        [gx_part.reshape(plane_shape), gs_part, mix_part.reshape(plane_shape)], 1
    )
    mixed = (attended + mixture.astype(f32)).astype(bf)
    grad_share = jnp.transpose(grad_share)
    core_terms, corner_terms = swapped((core_grads, corner_grads), "fsdp", 0)
    own_sum = own_grads.astype(f32) + core_terms.astype(f32)
    x_sum = (x_grads.astype(f32) + corner_terms.astype(f32)).astype(bf)
    x_terms = swapped(x_sum, "fsdp", 1)
    expert_grads = own_sum + x_terms.astype(f32)
    grad_gate, grad_up, grad_down = expert_grads[0], expert_grads[1], expert_grads[2]
    grad_mixed = cotangent.astype(f32)
    grad_logits = gate_share * (grad_share - jnp.sum(gate_share * grad_share, axis=1, keepdims=True))
    grad_router_part = jnp.dot(normed_moe.astype(f32).T, grad_logits, precision=highest)
    grad_normed_moe = grad_from_experts.astype(f32) + jnp.dot(
        grad_logits, router_full.astype(f32).T, precision=highest
    )
    grad_from_norm, grad_gain_two = norm_back(grad_normed_moe, attended, scale_two, moe_gain)
    grad_attended = grad_mixed + grad_from_norm
    grad_attended_low = grad_attended.astype(bf)
    grad_out_part = contract(context, grad_attended_low, 0, 0).astype(bf)
    grad_context = (
        contract(grad_attended_low, out_full, 1, 1)
        .astype(bf)
        .reshape(tok_rows, head_count, head_size)
    )
    probs = jnp.exp(scores_of() - log_total)
    probs_back = probs.astype(bf)
    grad_values = jnp.einsum("hqk,qhd->khd", probs_back, grad_context, preferred_element_type=f32)
    grad_probs = jnp.einsum("qhd,khd->hqk", grad_context, value_heads, preferred_element_type=f32)
    grad_scores = (
        probs * (grad_probs - jnp.sum(probs * grad_probs, axis=2, keepdims=True))
    ).astype(bf)
    grad_queries = (
        (
            jnp.einsum("hqk,khd->qhd", grad_scores, key_heads, preferred_element_type=f32)
            * score_scale
        )
        .reshape(tok_rows, model_width)
        .astype(bf)
    )
    grad_keys = (
        jnp.einsum("hqk,qhd->khd", grad_scores, query_heads, preferred_element_type=f32)
        * score_scale
    )
    grad_kv = jnp.concatenate(
        (grad_keys.reshape(key_count, model_width), grad_values.reshape(key_count, model_width)),
        axis=1,
    )
    grad_blocks = [
        grad_kv[position * tok_rows : (position + 1) * tok_rows] for position in range(len(ordered))
    ]
    own_block = grad_blocks[reach_count]
    remote_blocks = grad_blocks[:reach_count] + grad_blocks[reach_count + 1 :]
    returned = [
        passed_along(grad_block.astype(bf), "fsdp", -offset).astype(grad_block.dtype)
        for grad_block, offset in zip(remote_blocks, offsets)
    ]
    grad_kv_low = reduce(jnp.add, returned, own_block).astype(bf)
    grad_qkv = jnp.concatenate((grad_queries, grad_kv_low), axis=1)
    grad_qkv_part = contract(normed_attn, grad_qkv, 0, 0).astype(bf)
    grad_normed_attn = contract(jnp.pad(grad_qkv, ((0, 0), (0, 128))), wide_full, 1, 1)
    grad_from_first, grad_gain_one = norm_back(grad_normed_attn, token_values, scale_one, attn_gain)
    grad_tokens = grad_attended + grad_from_first
    extra_part = jnp.pad(
        jnp.concatenate((grad_router_part, grad_gain_one[:, None], grad_gain_two[:, None]), axis=1),
        ((0, 0), (0, 128 - experts - 2)),
    )
    owners = (devices // 2, 2, weight_rows)
    qkv_sum, out_sum, extra_sum = full_reduce(
        [
            grad_qkv_part.reshape(owners + (wide_width,)),
            grad_out_part.reshape(owners + (model_width,)),
            extra_part.reshape(owners + (128,)),
        ],
        3,
    )
    return (
        mixed,
        grad_tokens,
        qkv_sum[:, :model_width],
        qkv_sum[:, model_width : 2 * model_width],
        qkv_sum[:, 2 * model_width :],
        out_sum,
        extra_sum[:, :experts],
        extra_sum[:, experts],
        extra_sum[:, experts + 1],
        grad_gate,
        grad_up,
        grad_down,
        clipped_query,
        clipped_key,
    )


def chosen_layer(mesh):
    def layer(*arrays):
        experts, top_count = arrays[5].shape[1], arrays[11].shape[1]
        if mesh.shape["fsdp"] == 32 and 2 * top_count >= experts:
            return dense_layer(*arrays)
        return routed_layer(*arrays)

    return layer


def solution(mesh):
    placed = (
        P("fsdp", None),
        P("fsdp", None),
        P("fsdp", None),
        P("fsdp", None),
        P("fsdp", None),
        P("fsdp", None),
        P("fsdp"),
        P("fsdp"),
        P("fsdp", None),
        P("fsdp", None),
        P("fsdp", None),
        P("fsdp", None),
        P(),
        P(),
        P("fsdp", None),
    )
    return jax.shard_map(
        chosen_layer(mesh),
        mesh=mesh,
        in_specs=placed,
        out_specs=(
            P("fsdp", None),
            P("fsdp", None),
            P("fsdp", None),
            P("fsdp", None),
            P("fsdp", None),
            P("fsdp", None),
            P("fsdp", None),
            P("fsdp"),
            P("fsdp"),
            P("fsdp", None),
            P("fsdp", None),
            P("fsdp", None),
            P("fsdp", None),
            P("fsdp", None),
        ),
        check_vma=False,
    )
```

```python
import functools
from functools import reduce

import jax
import jax.numpy as jnp
from jax import lax
from jax.experimental import pallas as pl
from jax.experimental.pallas import tpu as pltpu
from jax.sharding import PartitionSpec as P

HALF = 512


epsilon = 1e-05
masked = -1e30
highest = lax.Precision.HIGHEST


def passed_along(x, axis, by):
    length = lax.axis_size(axis)
    pairs = [(i, i + by) for i in range(length) if 0 <= i + by < length]
    return lax.ppermute(x, axis, pairs)


def swapped(block, axis, apart):
    count = lax.axis_size(axis)
    route = []
    for low in range(count):
        high = low | 1 << apart
        if high != low and high < count:
            route += [(low, high), (high, low)]
    return lax.ppermute(block, axis, route)


def rms_scale(source):
    return lax.rsqrt(jnp.mean(source * source, axis=-1, keepdims=True) + epsilon)


def norm_back(grad_normed, source, scale_rows, gain):
    unit_rows = source * scale_rows
    grad_unit = grad_normed * gain
    grad_gain = jnp.sum(grad_normed * unit_rows, axis=0)
    grad_source = scale_rows * (
        grad_unit - unit_rows * jnp.mean(grad_unit * unit_rows, axis=-1, keepdims=True)
    )
    return (grad_source, grad_gain)


def document_of(places, doc_lengths, seq_len):
    doc_ends = jnp.cumsum(doc_lengths, axis=1)
    seq_count = doc_lengths.shape[0]
    doc_count = doc_lengths.shape[1]
    sequence = places // seq_len
    within = places % seq_len
    picked = (sequence[:, None] == jnp.arange(seq_count, dtype=jnp.int32)[None, :]).astype(
        jnp.int32
    )
    ends_of = jnp.dot(picked, doc_ends)
    local_doc = jnp.sum((within[:, None] >= ends_of).astype(jnp.int32), axis=1)
    inside = (places >= 0) & (places < seq_count * seq_len)
    return jnp.where(inside, sequence * doc_count + local_doc, -1)


def contract(left, right, left_dim, right_dim):
    return lax.dot_general(
        left, right, (((left_dim,), (right_dim,)), ((), ())), preferred_element_type=jnp.float32
    )


def routed_layer(
    tokens,
    w_query,
    w_key,
    w_value,
    w_out,
    w_router,
    gain_attn,
    gain_moe,
    w_gate,
    w_up,
    w_down,
    routes,
    doc_lengths,
    clip_limit,
    cotangent,
):
    devices = lax.axis_size("fsdp")
    device = lax.axis_index("fsdp")
    tok_rows = tokens.shape[0]
    model_width = tokens.shape[1]
    head_count = clip_limit.shape[0]
    head_size = model_width // head_count
    experts = w_router.shape[1]
    top_count = routes.shape[1]
    seq_len = devices * tok_rows // doc_lengths.shape[0]
    score_scale = head_size ** (-0.5)
    gathered = (
        lax.all_gather(w_query, "fsdp", axis=0, tiled=True),
        lax.all_gather(w_key, "fsdp", axis=0, tiled=True),
        lax.all_gather(w_value, "fsdp", axis=0, tiled=True),
        lax.all_gather(w_out, "fsdp", axis=0, tiled=True),
        lax.all_gather(w_router, "fsdp", axis=0, tiled=True),
        lax.all_gather(gain_attn, "fsdp", axis=0, tiled=True),
        lax.all_gather(gain_moe, "fsdp", axis=0, tiled=True),
    )
    query_full, key_full, value_full, out_full, router_full, gain_one, gain_two = gathered
    token_values = tokens.astype(jnp.float32)
    scale_one = rms_scale(token_values)
    attn_gain = gain_one.astype(jnp.float32)
    normed_attn = (token_values * scale_one * attn_gain).astype(jnp.bfloat16)
    queries = jnp.dot(normed_attn, query_full, preferred_element_type=jnp.float32).astype(
        jnp.bfloat16
    )
    kv_own = jnp.concatenate(
        (
            jnp.dot(normed_attn, key_full, preferred_element_type=jnp.float32),
            jnp.dot(normed_attn, value_full, preferred_element_type=jnp.float32),
        ),
        axis=1,
    ).astype(jnp.bfloat16)
    reach_count = (HALF - 2) // tok_rows + 1
    offsets = list(range(reach_count, 0, -1)) + list(range(-1, -reach_count - 1, -1))
    arrived = [passed_along(kv_own, "fsdp", offset) for offset in offsets]
    kv_rows = jnp.concatenate(arrived[:reach_count] + [kv_own] + arrived[reach_count:], axis=0)
    ordered = offsets[:reach_count] + [0] + offsets[reach_count:]
    row_index = jnp.arange(tok_rows, dtype=jnp.int32)
    query_places = device * tok_rows + row_index
    key_places = jnp.concatenate([(device - offset) * tok_rows + row_index for offset in ordered])
    query_docs = document_of(query_places, doc_lengths, seq_len)
    key_docs = document_of(key_places, doc_lengths, seq_len)
    visible = (
        (query_docs[:, None] == key_docs[None, :])
        & (key_docs[None, :] >= 0)
        & (jnp.abs(query_places[:, None] - key_places[None, :]) < HALF)
    )
    key_count = kv_rows.shape[0]
    query_heads = queries.reshape(tok_rows, head_count, head_size)
    key_heads = kv_rows[:, :model_width].reshape(key_count, head_count, head_size)
    value_heads = kv_rows[:, model_width:].reshape(key_count, head_count, head_size)

    def scores_of():
        raw_scores = (
            jnp.einsum("qhd,khd->hqk", query_heads, key_heads, preferred_element_type=jnp.float32)
            * score_scale
        )
        return jnp.where(visible[None], raw_scores, masked)

    scores = scores_of()
    head_top = jnp.max(scores, axis=2, keepdims=True)
    exponents = jnp.exp(scores - head_top)
    totals = jnp.sum(exponents, axis=2, keepdims=True)
    log_total = head_top + jnp.log(totals)
    probs_low = (exponents / totals).astype(jnp.bfloat16)
    head_max = lax.pmax(jnp.max(head_top, axis=(1, 2)), "fsdp")
    context = (
        jnp.einsum("hqk,khd->qhd", probs_low, value_heads, preferred_element_type=jnp.float32)
        .reshape(tok_rows, model_width)
        .astype(jnp.bfloat16)
    )
    attended = token_values + jnp.dot(context, out_full, preferred_element_type=jnp.float32)
    factor = clip_limit / jnp.maximum(head_max, clip_limit)
    columns = jnp.repeat(jnp.sqrt(factor), head_size)
    clipped_query = (w_query.astype(jnp.float32) * columns[None, :]).astype(jnp.bfloat16)
    clipped_key = (w_key.astype(jnp.float32) * columns[None, :]).astype(jnp.bfloat16)
    scale_two = rms_scale(attended)
    moe_gain = gain_two.astype(jnp.float32)
    normed_moe = (attended * scale_two * moe_gain).astype(jnp.bfloat16)
    logits = jnp.dot(normed_moe, router_full, preferred_element_type=jnp.float32)
    matches = routes[:, :, None] == jnp.arange(experts, dtype=jnp.int32)[None, None, :]
    chosen = jnp.sum(jnp.where(matches, logits[:, None, :], 0.0), axis=2)
    gate_share = jax.nn.softmax(chosen, axis=1)
    pair_count = tok_rows * top_count
    capacity = 3 * tok_rows * top_count // devices
    half_cap = capacity // 2
    flat_route = routes.reshape(pair_count)
    one_hot = (flat_route[:, None] == jnp.arange(experts, dtype=jnp.int32)[None, :]).astype(
        jnp.int32
    )
    slot_rank = jnp.sum(jnp.cumsum(one_hot, axis=0) * one_hot, axis=1) - 1
    target_device = 2 * flat_route + slot_rank // half_cap
    target_slot = slot_rank % half_cap
    flat_slot = target_device * half_cap + target_slot
    slot_total = devices * half_cap
    outgoing = (
        jnp.zeros((slot_total, model_width), jnp.bfloat16)
        .at[flat_slot]
        .set(jnp.repeat(normed_moe, top_count, axis=0))
    )
    live_out = jnp.zeros((slot_total,), jnp.int32).at[flat_slot].set(1)
    incoming, live_in = (
        lax.all_to_all(outgoing, "fsdp", split_axis=0, concat_axis=0, tiled=True),
        lax.all_to_all(live_out, "fsdp", split_axis=0, concat_axis=0, tiled=True),
    )
    packed_order = jnp.cumsum(live_in) - 1
    packed_index = jnp.where(live_in > 0, packed_order, slot_total)
    back_index = jnp.clip(packed_order, 0, slot_total - 1)
    live_count = jnp.sum(live_in)
    tile_rows = 128
    tile_count = (live_count + tile_rows - 1) // tile_rows
    packed_rows = (
        jnp.zeros((slot_total + 1, model_width), jnp.bfloat16)
        .at[packed_index]
        .set(incoming)[:slot_total]
    )
    partner_half = swapped((w_gate, w_up, w_down), "fsdp", 0)
    lower = device % 2 == 0

    def joined(own_half, other_half):
        return jnp.where(
            lower, jnp.concatenate((own_half, other_half)), jnp.concatenate((other_half, own_half))
        )

    gate_full = joined(w_gate, partner_half[0])
    up_full = joined(w_up, partner_half[1])
    down_full = joined(w_down, partner_half[2])
    hidden_units = gate_full.shape[0]

    def forward_tile(tile_step, loop_state):
        out_rows, gate_keep, up_keep = loop_state
        tile_start = tile_step * tile_rows
        tile_input = lax.dynamic_slice_in_dim(packed_rows, tile_start, tile_rows, 0)
        gate_pre = contract(tile_input, gate_full, 1, 1)
        up_pre = contract(tile_input, up_full, 1, 1)
        hidden = (jax.nn.silu(gate_pre) * up_pre).astype(jnp.bfloat16)
        result = jnp.dot(hidden, down_full, preferred_element_type=jnp.float32).astype(jnp.bfloat16)
        return (
            lax.dynamic_update_slice_in_dim(out_rows, result, tile_start, 0),
            lax.dynamic_update_slice_in_dim(gate_keep, gate_pre, tile_start, 0),
            lax.dynamic_update_slice_in_dim(up_keep, up_pre, tile_start, 0),
        )

    start_state = (
        jnp.zeros((slot_total, model_width), jnp.bfloat16),
        jnp.zeros((slot_total, hidden_units), jnp.float32),
        jnp.zeros((slot_total, hidden_units), jnp.float32),
    )
    expert_out, gate_keep, up_keep = lax.fori_loop(0, tile_count, forward_tile, start_state)
    returning = jnp.where(live_in[:, None] > 0, expert_out[back_index], jnp.zeros((), jnp.bfloat16))
    came_back = lax.all_to_all(returning, "fsdp", split_axis=0, concat_axis=0, tiled=True)
    pair_out = came_back[flat_slot].reshape(tok_rows, top_count, model_width)
    mixture = jnp.sum(gate_share[:, :, None] * pair_out, axis=1)
    mixed = (attended + mixture).astype(jnp.bfloat16)
    query_back, key_back, value_back, out_back = (
        lax.all_gather(w_query, "fsdp", axis=0, tiled=True),
        lax.all_gather(w_key, "fsdp", axis=0, tiled=True),
        lax.all_gather(w_value, "fsdp", axis=0, tiled=True),
        lax.all_gather(w_out, "fsdp", axis=0, tiled=True),
    )
    grad_mixed = cotangent.astype(jnp.float32)
    grad_share = jnp.sum(grad_mixed[:, None, :] * pair_out, axis=2)
    grad_pair = (
        (gate_share[:, :, None] * grad_mixed[:, None, :])
        .astype(jnp.bfloat16)
        .reshape(pair_count, model_width)
    )
    grad_outgoing = jnp.zeros((slot_total, model_width), jnp.bfloat16).at[flat_slot].set(grad_pair)
    grad_incoming = lax.all_to_all(grad_outgoing, "fsdp", split_axis=0, concat_axis=0, tiled=True)
    grad_packed = (
        jnp.zeros((slot_total + 1, model_width), jnp.bfloat16)
        .at[packed_index]
        .set(grad_incoming)[:slot_total]
    )

    def backward_tile(tile_step, loop_state):
        grad_rows, gate_sum, up_sum, down_sum = loop_state
        tile_start = tile_step * tile_rows
        tile_input = lax.dynamic_slice_in_dim(packed_rows, tile_start, tile_rows, 0)
        tile_grad = lax.dynamic_slice_in_dim(grad_packed, tile_start, tile_rows, 0)
        gate_pre = lax.dynamic_slice_in_dim(gate_keep, tile_start, tile_rows, 0)
        up_pre = lax.dynamic_slice_in_dim(up_keep, tile_start, tile_rows, 0)
        sigmoid_gate = jax.nn.sigmoid(gate_pre)
        silu_gate = gate_pre * sigmoid_gate
        hidden = (silu_gate * up_pre).astype(jnp.bfloat16)
        grad_hidden = contract(tile_grad, down_full, 1, 1)
        grad_gate_pre = (
            grad_hidden * up_pre * sigmoid_gate * (1.0 + gate_pre * (1.0 - sigmoid_gate))
        ).astype(jnp.bfloat16)
        grad_up_pre = (grad_hidden * silu_gate).astype(jnp.bfloat16)
        down_sum = down_sum + contract(hidden, tile_grad, 0, 0)
        gate_sum = gate_sum + contract(grad_gate_pre, tile_input, 0, 0)
        up_sum = up_sum + contract(grad_up_pre, tile_input, 0, 0)
        grad_input = (
            jnp.dot(grad_gate_pre, gate_full, preferred_element_type=jnp.float32)
            + jnp.dot(grad_up_pre, up_full, preferred_element_type=jnp.float32)
        ).astype(jnp.bfloat16)
        return (
            lax.dynamic_update_slice_in_dim(grad_rows, grad_input, tile_start, 0),
            gate_sum,
            up_sum,
            down_sum,
        )

    weight_zero = jnp.zeros((hidden_units, model_width), jnp.float32)
    back_state = (
        jnp.zeros((slot_total, model_width), jnp.bfloat16),
        weight_zero,
        weight_zero,
        weight_zero,
    )
    grad_rows, gate_sum, up_sum, down_sum = lax.fori_loop(0, tile_count, backward_tile, back_state)
    grad_returning = jnp.where(
        live_in[:, None] > 0, grad_rows[back_index], jnp.zeros((), jnp.bfloat16)
    )
    grad_came = lax.all_to_all(grad_returning, "fsdp", split_axis=0, concat_axis=0, tiled=True)
    grad_from_experts = jnp.sum(
        grad_came[flat_slot].reshape(tok_rows, top_count, model_width), axis=1, dtype=jnp.float32
    )
    half_units = w_gate.shape[0]

    def partner_part(grad_sum):
        return jnp.where(lower, grad_sum[half_units:], grad_sum[:half_units])

    def own_part(grad_sum):
        return jnp.where(lower, grad_sum[:half_units], grad_sum[half_units:])

    partner_terms = (
        swapped(partner_part(gate_sum).astype(jnp.bfloat16), "fsdp", 0).astype(jnp.float32),
        swapped(partner_part(up_sum).astype(jnp.bfloat16), "fsdp", 0).astype(jnp.float32),
        swapped(partner_part(down_sum).astype(jnp.bfloat16), "fsdp", 0).astype(jnp.float32),
    )
    grad_gate = own_part(gate_sum) + partner_terms[0]
    grad_up = own_part(up_sum) + partner_terms[1]
    grad_down = own_part(down_sum) + partner_terms[2]
    grad_chosen = gate_share * (
        grad_share - jnp.sum(gate_share * grad_share, axis=1, keepdims=True)
    )
    grad_logits = jnp.sum(jnp.where(matches, grad_chosen[:, :, None], 0.0), axis=1)
    grad_router_part = jnp.dot(normed_moe.astype(jnp.float32).T, grad_logits, precision=highest)
    grad_normed_moe = grad_from_experts + jnp.dot(
        grad_logits, router_full.astype(jnp.float32).T, precision=highest
    )
    grad_from_norm, grad_gain_two = norm_back(grad_normed_moe, attended, scale_two, moe_gain)
    grad_attended = grad_mixed + grad_from_norm
    grad_attended_low = grad_attended.astype(jnp.bfloat16)
    grad_out_part = contract(context, grad_attended_low, 0, 0)
    grad_context = (
        contract(grad_attended_low, out_back, 1, 1)
        .astype(jnp.bfloat16)
        .reshape(tok_rows, head_count, head_size)
    )
    probs = jnp.exp(scores_of() - log_total)
    probs_back = probs.astype(jnp.bfloat16)
    grad_values = jnp.einsum(
        "hqk,qhd->khd", probs_back, grad_context, preferred_element_type=jnp.float32
    )
    grad_probs = jnp.einsum(
        "qhd,khd->hqk", grad_context, value_heads, preferred_element_type=jnp.float32
    )
    grad_scores = (
        probs * (grad_probs - jnp.sum(probs * grad_probs, axis=2, keepdims=True))
    ).astype(jnp.bfloat16)
    grad_queries = (
        (
            jnp.einsum("hqk,khd->qhd", grad_scores, key_heads, preferred_element_type=jnp.float32)
            * score_scale
        )
        .reshape(tok_rows, model_width)
        .astype(jnp.bfloat16)
    )
    grad_keys = (
        jnp.einsum("hqk,qhd->khd", grad_scores, query_heads, preferred_element_type=jnp.float32)
        * score_scale
    )
    grad_kv = jnp.concatenate(
        (grad_keys.reshape(key_count, model_width), grad_values.reshape(key_count, model_width)),
        axis=1,
    )
    grad_blocks = [
        grad_kv[position * tok_rows : (position + 1) * tok_rows] for position in range(len(ordered))
    ]
    own_block = grad_blocks[reach_count]
    remote = grad_blocks[:reach_count] + grad_blocks[reach_count + 1 :]
    returned = [
        passed_along(grad_block.astype(jnp.bfloat16), "fsdp", -offset).astype(grad_block.dtype)
        for grad_block, offset in zip(remote, offsets)
    ]
    grad_kv_low = reduce(jnp.add, returned, own_block).astype(jnp.bfloat16)
    grad_query_part = contract(normed_attn, grad_queries, 0, 0)
    grad_kv_part = contract(normed_attn, grad_kv_low, 0, 0)
    grad_normed_attn = (
        contract(grad_queries, query_back, 1, 1)
        + contract(grad_kv_low[:, :model_width], key_back, 1, 1)
        + contract(grad_kv_low[:, model_width:], value_back, 1, 1)
    )
    grad_from_first, grad_gain_one = norm_back(grad_normed_attn, token_values, scale_one, attn_gain)
    grad_tokens = grad_attended + grad_from_first
    reduced = (
        lax.psum_scatter(grad_query_part, "fsdp", scatter_dimension=0, tiled=True),
        lax.psum_scatter(grad_kv_part[:, :model_width], "fsdp", scatter_dimension=0, tiled=True),
        lax.psum_scatter(grad_kv_part[:, model_width:], "fsdp", scatter_dimension=0, tiled=True),
        lax.psum_scatter(grad_out_part, "fsdp", scatter_dimension=0, tiled=True),
        lax.psum_scatter(grad_router_part, "fsdp", scatter_dimension=0, tiled=True),
        lax.psum_scatter(grad_gain_one, "fsdp", scatter_dimension=0, tiled=True),
        lax.psum_scatter(grad_gain_two, "fsdp", scatter_dimension=0, tiled=True),
    )
    return (
        mixed,
        grad_tokens,
        reduced[0],
        reduced[1],
        reduced[2],
        reduced[3],
        reduced[4],
        reduced[5],
        reduced[6],
        grad_gate,
        grad_up,
        grad_down,
        clipped_query,
        clipped_key,
    )


MESH = pl.DeviceIdType.MESH
f32 = jnp.float32
bf = jnp.bfloat16

def place():
    me = lax.axis_index("fsdp")
    core = lax.rem(me, 2)
    x = lax.rem(lax.div(me, 2), 2)
    y = lax.rem(lax.div(me, 4), 2)
    z = lax.div(me, 8)
    return z, y, x, core

def index_of(z, y, x, core):
    return ((z * 2 + y) * 2 + x) * 2 + core

def remote(src, dst, send, recv, device):
    return pltpu.make_async_remote_copy(
        src_ref=src, dst_ref=dst, send_sem=send, recv_sem=recv, device_id=(device,), device_id_type=MESH)

def greet(devices, conditions):
    barrier = pltpu.get_barrier_semaphore()
    for device, condition in zip(devices, conditions):
        if condition is None:
            pl.semaphore_signal(barrier, inc=1, device_id=(device,), device_id_type=MESH)
        else:
            @pl.when(condition)
            def _(device=device):
                pl.semaphore_signal(barrier, inc=1, device_id=(device,), device_id_type=MESH)
    count = 0
    for condition in conditions:
        count = count + (1 if condition is None else jnp.where(condition, 1, 0))
    pl.semaphore_wait(barrier, count)

def line_items(z):
    low = z < 2
    near = z + 1 - 2 * lax.rem(z, 2)
    return [z, near, jnp.where(low, 2, 1), jnp.where(low, 3, 0)]

def gather_all(per_seq, ins, near_in, outs, near_out, ssem, rsem, lsem, nsend, nrecv):
    count = len(ins)
    z, y, x, core = place()
    mid = (z == 1) | (z == 2)
    up, down = z < 3, z > 0
    x_dev = index_of(z, y, 1 - x, core)
    y_dev = index_of(z, 1 - y, x, core)
    c_dev = index_of(z, y, x, 1 - core)
    up_dev = index_of(jnp.minimum(z + 1, 3), y, x, core)
    down_dev = index_of(jnp.maximum(z - 1, 0), y, x, core)
    previous, following, before, after = chain(z, y, x, core, per_seq)
    greet([x_dev, y_dev, c_dev, up_dev, down_dev, previous, following], [None, None, None, up, down, before, after])
    own = [pltpu.make_async_copy(ins[a], outs[a].at[index_of(z, y, x, core)], lsem.at[a]) for a in range(count)]
    own.append(pltpu.make_async_copy(near_in, near_out.at[2], lsem.at[count]))
    for copy in own:
        copy.start()
    passes = jnp.where(core == 0, after, before)
    pass_slot = 4 * (1 - core)

    def near(kind):
        src, slot, device = (
            (near_in, 0, following),
            (near_in, 4, previous),
            (near_in, 1 + 2 * core, c_dev),
            (near_out.at[pass_slot], 3 - 2 * core, c_dev),
        )[kind]
        return remote(src, near_out.at[slot], nsend.at[kind], nrecv.at[kind], device)

    pl.when(after)(lambda: near(0).start())
    pl.when(before)(lambda: near(1).start())
    near(2).start()
    pending = []

    def go(kind, a, o, src, dst, device, condition=None):
        def make():
            return remote(src, dst, ssem.at[kind, o, a], rsem.at[kind, o, a], device)
        if condition is None:
            make().start()
        else:
            pl.when(condition)(lambda: make().start())
        pending.append((make, condition))

    def arrived(kind, a, o, land):
        remote(land, land, ssem.at[kind, o, a], rsem.at[kind, o, a], c_dev).wait_recv()

    items = line_items(z)

    def first(i):
        o = items[i]
        for a in range(count):
            slot = index_of(o, y, x, core)
            dst = outs[a].at[slot]
            src = ins[a] if i == 0 else dst
            if i == 0:
                go(0, a, o, src, dst, up_dev, up)
                go(1, a, o, src, dst, down_dev, down)
            else:
                from_below = o < z
                for kind, condition in ((0, from_below), (1, jnp.logical_not(from_below))):
                    pl.when(condition)(lambda kind=kind, a=a, o=o, dst=dst: arrived(kind, a, o, dst))
                go(0, a, o, src, dst, up_dev, mid & from_below)
                go(1, a, o, src, dst, down_dev, mid & jnp.logical_not(from_below))
            go(2, a, o, src, dst, x_dev)
            go(3, a, o, src, dst, y_dev)
            go(6, a, o, src, dst, c_dev)

    def second(i):
        o = items[i]
        for a in range(count):
            half = ins[a].shape[0] // 2
            from_x = outs[a].at[index_of(o, y, 1 - x, core)]
            arrived(2, a, o, from_x)
            go(5, a, o, from_x.at[pl.ds(0, half)], from_x.at[pl.ds(0, half)], y_dev)
            from_y = outs[a].at[index_of(o, 1 - y, x, core)]
            arrived(3, a, o, from_y)
            go(4, a, o, from_y.at[pl.ds(half, half)], from_y.at[pl.ds(half, half)], x_dev)
            go(7, a, o, from_x, from_x, c_dev)
            go(8, a, o, from_y, from_y, c_dev)

    def third(i):
        o = items[i]
        for a in range(count):
            half = ins[a].shape[0] // 2
            corner = outs[a].at[index_of(o, 1 - y, 1 - x, core)]
            arrived(5, a, o, corner.at[pl.ds(0, half)])
            arrived(4, a, o, corner.at[pl.ds(half, half)])
            go(9, a, o, corner, corner, c_dev)

    first(0); first(1); second(0); first(2); second(1); third(0); first(3); second(2); third(1); second(3); third(2); third(3)
    pl.when(before)(lambda: near(0).wait_recv())
    pl.when(after)(lambda: near(1).wait_recv())
    pl.when(passes)(lambda: near(3).start())
    near(2).wait_recv()
    pl.when(jnp.where(core == 0, before, after))(lambda: near(3).wait_recv())
    pl.when(after)(lambda: near(0).wait_send())
    pl.when(before)(lambda: near(1).wait_send())
    near(2).wait_send()
    pl.when(passes)(lambda: near(3).wait_send())
    for i in range(4):
        o = items[i]
        for a in range(count):
            for kind, (yy, xx) in ((6, (y, x)), (7, (y, 1 - x)), (8, (1 - y, x)), (9, (1 - y, 1 - x))):
                arrived(kind, a, o, outs[a].at[index_of(o, yy, xx, 1 - core)])
    for make, condition in pending:
        if condition is None:
            make().wait_send()
        else:
            pl.when(condition)(lambda make=make: make().wait_send())
    for copy in own:
        copy.wait()

def full_gather(arrays, near_rows, per_seq, cid):
    count = len(arrays)
    anys = pl.BlockSpec(memory_space=pl.ANY)
    def body(*refs):
        ins, near_in = refs[:count], refs[count]
        outs, near_out = refs[count + 1:2 * count + 1], refs[2 * count + 1]
        gather_all(per_seq, ins, near_in, outs, near_out, *refs[2 * count + 2:])
    sem = pltpu.SemaphoreType.DMA
    return pl.pallas_call(
        body, in_specs=[anys] * (count + 1), out_specs=[anys] * (count + 1),
        out_shape=[jax.ShapeDtypeStruct((32,) + a.shape, a.dtype) for a in arrays]
        + [jax.ShapeDtypeStruct((5,) + near_rows.shape, near_rows.dtype)],
        scratch_shapes=[sem((10, 4, count)), sem((10, 4, count)), sem((count + 1,)), sem((4,)), sem((4,))],
        compiler_params=pltpu.CompilerParams(collective_id=cid, has_side_effects=True),
        name="full_gather")(*arrays, near_rows)

def add_into(target, *terms, rows=16):
    total = target.shape[0]
    step = min(rows, total)
    def one(r, carry):
        part = pl.ds(pl.multiple_of(r * step, step), step)
        value = target[part, :].astype(f32)
        for term in terms:
            value = value + term[part, :].astype(f32)
        target[part, :] = value.astype(target.dtype)
        return carry
    lax.fori_loop(0, total // step, one, 0)

def reduce_all(parts, outs, accs, crecvs, dxs, dys, xrecvs, yrecvs, zrecvs, ssem, rsem, lsem, osem):
    count = len(parts)
    z, y, x, core = place()
    mid = (z == 1) | (z == 2)
    up, down = z < 3, z > 0
    x_dev = index_of(z, y, 1 - x, core)
    y_dev = index_of(z, 1 - y, x, core)
    c_dev = index_of(z, y, x, 1 - core)
    up_dev = index_of(jnp.minimum(z + 1, 3), y, x, core)
    down_dev = index_of(jnp.maximum(z - 1, 0), y, x, core)
    greet([x_dev, y_dev, c_dev, up_dev, down_dev], [None, None, None, up, down])
    items = line_items(z)[::-1]
    mine, xp, yp, dp = y * 2 + x, y * 2 + 1 - x, (1 - y) * 2 + x, (1 - y) * 2 + 1 - x
    pending = []

    def go(make, condition=None):
        if condition is None:
            make().start()
        else:
            pl.when(condition)(lambda: make().start())
        pending.append((make, condition))

    def arrived(kind, a, o, land):
        remote(land, land, ssem.at[kind, 0, a], rsem.at[kind, o, a], c_dev).wait_recv()

    loads = {}
    for i, o in enumerate(items):
        for a in range(count):
            go(lambda o=o, a=a: remote(parts[a].at[pl.ds(o * 4, 4), 1 - core], crecvs[a].at[o],
                                       ssem.at[0, o, a], rsem.at[0, o, a], c_dev))
            loads[i, a] = pltpu.make_async_copy(parts[a].at[pl.ds(o * 4, 4), core], accs[a].at[o], lsem.at[o, a])
            loads[i, a].start()

    def first(i):
        o = items[i]
        for a in range(count):
            half = parts[a].shape[2] // 2
            arrived(0, a, o, crecvs[a].at[o])
            loads[i, a].wait()
            for p in (dp, xp, yp, mine):
                add_into(accs[a].at[o, p], crecvs[a].at[o, p])
                if p is dp:
                    go(lambda a=a, half=half: remote(accs[a].at[o, dp, pl.ds(0, half)], dxs[a].at[o], ssem.at[1, o, a], rsem.at[1, o, a], x_dev))
                    go(lambda a=a, half=half: remote(accs[a].at[o, dp, pl.ds(half, half)], dys[a].at[o], ssem.at[2, o, a], rsem.at[2, o, a], y_dev))

    def second(i):
        o = items[i]
        for a in range(count):
            half = parts[a].shape[2] // 2
            arrived(1, a, o, dxs[a].at[o])
            add_into(accs[a].at[o, yp, pl.ds(0, half)], dxs[a].at[o])
            go(lambda a=a, half=half: remote(accs[a].at[o, yp], yrecvs[a].at[o], ssem.at[4, o, a], rsem.at[4, o, a], y_dev))
            arrived(2, a, o, dys[a].at[o])
            add_into(accs[a].at[o, xp, pl.ds(half, half)], dys[a].at[o])
            go(lambda a=a, half=half: remote(accs[a].at[o, xp], xrecvs[a].at[o], ssem.at[3, o, a], rsem.at[3, o, a], x_dev))

    def third(i):
        o = items[i]
        for a in range(count):
            acc = accs[a].at[o, mine]
            arrived(3, a, o, xrecvs[a].at[o])
            arrived(4, a, o, yrecvs[a].at[o])
            if i < 3:
                @pl.when(mid)
                def _():
                    arrived(5, a, o, zrecvs[a].at[o])
                    add_into(acc, xrecvs[a].at[o], yrecvs[a].at[o], zrecvs[a].at[o])
                @pl.when(jnp.logical_not(mid))
                def _():
                    add_into(acc, xrecvs[a].at[o], yrecvs[a].at[o])
                rising = o > z
                go(lambda o=o, a=a, acc=acc: remote(acc, zrecvs[a].at[o], ssem.at[5, o, a], rsem.at[5, o, a], up_dev), rising)
                def lower(o=o, a=a, acc=acc):
                    slot = jnp.where(z - 1 == o, 4, o)
                    return remote(acc, zrecvs[a].at[slot], ssem.at[5, o, a], rsem.at[5, slot, a], down_dev)
                go(lower, jnp.logical_not(rising))
            else:
                for condition, slots in ((z == 0, (4,)), (z == 3, (3,)), (mid, (None, 4))):
                    @pl.when(condition)
                    def _(slots=slots):
                        terms = [xrecvs[a].at[o], yrecvs[a].at[o]]
                        for slot in slots:
                            slot = o if slot is None else slot
                            arrived(5, a, slot, zrecvs[a].at[slot])
                            terms.append(zrecvs[a].at[slot])
                        rows, step = outs[a].shape[0], 16
                        def one(r, carry):
                            part = pl.ds(pl.multiple_of(r * step, step), step)
                            value = acc[part, :].astype(f32)
                            for term in terms:
                                value = value + term[part, :].astype(f32)
                            outs[a][part, :] = value
                            return carry
                        lax.fori_loop(0, rows // step, one, 0)

    first(0); first(1); second(0); first(2); second(1); third(0); first(3); second(2); third(1); second(3); third(2); third(3)
    for make, condition in pending:
        if condition is None:
            make().wait_send()
        else:
            pl.when(condition)(lambda make=make: make().wait_send())

def full_reduce(parts, cid):
    count = len(parts)
    anys = pl.BlockSpec(memory_space=pl.ANY)
    def body(*refs):
        it = iter(refs)
        take = lambda n: [next(it) for _ in range(n)]
        reduce_all(*[take(count) for _ in range(9)], *it)
    sem = pltpu.SemaphoreType.DMA
    scratch = []
    for lead, cut in (((4, 4), 1), ((4, 4), 1), ((4,), 2), ((4,), 2), ((4,), 1), ((4,), 1), ((5,), 1)):
        scratch += [pltpu.VMEM(lead + (p.shape[2] // cut, p.shape[3]), p.dtype) for p in parts]
    return pl.pallas_call(
        body, in_specs=[anys] * count, out_specs=[pl.BlockSpec(memory_space=pltpu.VMEM)] * count,
        out_shape=[jax.ShapeDtypeStruct(p.shape[2:], f32) for p in parts],
        scratch_shapes=scratch + [sem((6, 5, count)), sem((6, 5, count)), sem((4, count)), sem((count,))],
        compiler_params=pltpu.CompilerParams(collective_id=cid, has_side_effects=True, vmem_limit_bytes=62 * 2**20),
        name="full_reduce")(*parts)
def nt(left, right):
    return lax.dot_general(left, right, (((1,), (1,)), ((), ())), preferred_element_type=f32)


def tn(left, right):
    return lax.dot_general(left, right, (((0,), (0,)), ((), ())), preferred_element_type=f32)


def nn(left, right):
    return lax.dot_general(left, right, (((1,), (0,)), ((), ())), preferred_element_type=f32)


def expert_body(shard, width, half, block, cut, *refs):
    it = iter(refs)
    take = lambda n: [next(it) for _ in range(n)]
    x_own, s_own, c_all = take(3)
    weights = [[take(2) for _ in range(3)] for _ in range(2)]
    x_all, s_all, mix, gx, gx_sum, gs_sum, y_land, z_land = take(8)
    core_land = take(2)
    grad_sum = take(2)
    x_land = next(it)
    xv, cv, sv, wv, acc, hid_s, gate_s, up_s, gst, gs_y, gs_z, ostage, prev = take(13)
    gsend, grecv, lsem, rsend, rrecv, csend, crecv, xsend, xrecv = take(9)
    wsem, insem, osem, psem, dsem, hsem, tsem = take(7)
    hidden = 2 * half
    tile = 2 * shard
    cuts = width // cut
    tiles = 4
    z, y, x, core = place()
    mid = (z == 1) | (z == 2)
    up, down = z < 3, z > 0
    x_dev = index_of(z, y, 1 - x, core)
    y_dev = index_of(z, 1 - y, x, core)
    c_dev = index_of(z, y, x, 1 - core)
    up_dev = index_of(jnp.minimum(z + 1, 3), y, x, core)
    down_dev = index_of(jnp.maximum(z - 1, 0), y, x, core)
    chip = (z * 2 + y) * 2 + x
    experts = ((z * 2 + y) * 2 + 1 - x, chip)
    lane = lax.broadcasted_iota(jnp.int32, (1, 128), 1)
    items = line_items(z)

    def nearest(k):
        return jnp.where(k == 0, items[0], jnp.where(k == 1, items[1], jnp.where(k == 2, items[2], items[3])))

    def farthest(k):
        return nearest(3 - k)

    sources, landings = (x_own, s_own), (x_all, s_all)
    own_rows = xv.at[0, pl.ds(pl.multiple_of(y * shard, shard), shard)]
    own_in = [
        pltpu.make_async_copy(x_own, own_rows, lsem.at[0]),
        pltpu.make_async_copy(s_own, s_all.at[z * 2 + y], lsem.at[1]),
    ]
    own_out = pltpu.make_async_copy(own_rows, x_all.at[z * 2 + y], lsem.at[0])

    def hop(kind, a, o, src, device):
        return remote(src, landings[a].at[o * 2 + y], gsend.at[kind, o, a], grecv.at[kind, o, a], device)

    def gather_first():
        for copy in own_in:
            copy.start()
        for a in range(2):
            hop(2, a, z, sources[a], y_dev).start()
            pl.when(up)(lambda a=a: hop(0, a, z, sources[a], up_dev).start())
            pl.when(down)(lambda a=a: hop(1, a, z, sources[a], down_dev).start())

    def gather_next(k):
        o = nearest(k)
        from_below = o < z
        for a in range(2):
            land = landings[a].at[o * 2 + y]

            @pl.when(from_below)
            def _():
                hop(0, a, o, land, up_dev).wait_recv()
                pl.when(mid)(lambda: hop(0, a, o, land, up_dev).start())

            @pl.when(jnp.logical_not(from_below))
            def _():
                hop(1, a, o, land, down_dev).wait_recv()
                pl.when(mid)(lambda: hop(1, a, o, land, down_dev).start())

            hop(2, a, o, land, y_dev).start()

    def gather_landed(o):
        for a in range(2):
            land = landings[a].at[o * 2 + 1 - y]
            remote(land, land, gsend.at[2, o, a], grecv.at[2, o, a], y_dev).wait_recv()

    def gather_sent():
        for a in range(2):
            pl.when(up)(lambda a=a: hop(0, a, z, sources[a], up_dev).wait_send())
            pl.when(down)(lambda a=a: hop(1, a, z, sources[a], down_dev).wait_send())
            for k in range(4):
                hop(2, a, items[k], sources[a], y_dev).wait_send()
            for k in range(1, 4):
                o = items[k]
                pl.when(mid & (o < z))(lambda a=a, o=o: hop(0, a, o, sources[a], up_dev).wait_send())
                pl.when(mid & (o > z))(lambda a=a, o=o: hop(1, a, o, sources[a], down_dev).wait_send())

    def lines(block_index):
        return pl.ds(pl.multiple_of(block_index * shard, shard), shard)

    def y_copies(o):
        other = o * 2 + 1 - y
        return [
            remote(gx.at[lines(other)], y_land.at[o], rsend.at[0, o, 0], rrecv.at[0, o, 0], y_dev),
            remote(gst.at[other], gs_y.at[o], rsend.at[0, o, 1], rrecv.at[0, o, 1], y_dev),
        ]

    def z_copies(o, slot, device):
        own = o * 2 + y
        return [
            remote(gx.at[lines(own)], z_land.at[slot], rsend.at[1, o, 0], rrecv.at[1, slot, 0], device),
            remote(gst.at[own], gs_z.at[slot], rsend.at[1, o, 1], rrecv.at[1, slot, 1], device),
        ]

    def z_go(o, act):
        rising = o > z
        slot = jnp.where(z - 1 == o, 4, o)

        @pl.when(rising)
        def _():
            for copy in z_copies(o, o, up_dev):
                act(copy)

        @pl.when(jnp.logical_not(rising))
        def _():
            for copy in z_copies(o, slot, down_dev):
                act(copy)

    wide = width // 2

    def halves(hbm, vmem, slot, out=False):
        copies = []
        for h in range(2):
            far, near = hbm.at[:, pl.ds(h * wide, wide)], vmem.at[pl.ds(h * shard, shard)]
            if out:
                copies.append(pltpu.make_async_copy(near, far, tsem.at[slot, h]))
            else:
                copies.append(pltpu.make_async_copy(far, near, tsem.at[slot, h]))
        return copies

    def z_wait(slot):
        for copy in z_copies(z, slot, y_dev):
            copy.wait_recv()

    def add_up(terms):
        def some(r, carry):
            part = pl.ds(pl.multiple_of(r * 32, 32), 32)
            value = hid_s[part, :].astype(f32)
            for term in terms:
                value = value + term[part, :].astype(f32)
            hid_s[part, :] = value.astype(bf)
            return carry

        lax.fori_loop(0, tile // 32, some, 0)

    def pump(o, final):
        own = o * 2 + y
        load = halves(gx.at[lines(own)], hid_s, 0)
        for copy in load:
            copy.start()
        for copy in y_copies(o):
            copy.wait_recv()
        load_y = halves(y_land.at[o], gate_s, 1)
        for copy in load_y:
            copy.start()
        slot = jnp.where(z == 0, 4, o) if final else o

        def with_z():
            z_wait(slot)
            load_z = halves(z_land.at[slot], up_s, 2)
            for copy in load_z:
                copy.start()
            for copy in load + load_y + load_z:
                copy.wait()
            add_up([gate_s, up_s])
            gst[own] = gst[own] + gs_y[o] + gs_z[slot]

        if final:
            with_z()

            @pl.when(mid)
            def _():
                z_wait(4)
                load_z = halves(z_land.at[4], up_s, 2)
                for copy in load_z:
                    copy.start()
                for copy in load_z:
                    copy.wait()
                add_up([up_s])
                gst[own] = gst[own] + gs_z[4]

            store = halves(gx_sum, hid_s, 0, True)
            store.append(pltpu.make_async_copy(gst.at[own], gs_sum, tsem.at[1, 0]))
            for copy in store:
                copy.start()
            for copy in store:
                copy.wait()
        else:
            pl.when(mid)(with_z)

            @pl.when(jnp.logical_not(mid))
            def _():
                for copy in load + load_y:
                    copy.wait()
                add_up([gate_s])
                gst[own] = gst[own] + gs_y[o]

            store = halves(gx.at[lines(own)], hid_s, 0, True)
            for copy in store:
                copy.start()
            for copy in store:
                copy.wait()
            z_go(o, lambda copy: copy.start())

    tall = shard
    per_half = (half // tall) * (width // cut)
    pieces = 3 * per_half

    def piece(q):
        i, rest = lax.div(q, per_half), lax.rem(q, per_half)
        r, c = lax.div(rest, width // cut), lax.rem(rest, width // cut)
        return i, pl.multiple_of(r * tall, tall), pl.ds(pl.multiple_of(c * cut, cut), cut)

    slots = 8

    def eighth(ref, slot):
        low = pl.multiple_of(lax.rem(slot, 2) * tall, tall)
        return ref.at[lax.div(slot, 4), lax.rem(lax.div(slot, 2), 2), pl.ds(low, tall)]

    def stage(slot):
        return eighth(ostage, slot)

    def held(slot):
        return eighth(prev, slot)

    def flush(number):
        def across(q, slot):
            i, r, c = piece(q)
            land = core_land[number].at[i, pl.ds(r, tall), c]
            return remote(stage(slot), land, csend.at[number, slot], crecv.at[number], c_dev)

        def give(q, carry):
            slot = lax.rem(q, slots)
            pl.when(q >= slots)(lambda: across(q - slots, slot).wait_send())
            i, r, c = piece(q)
            stage(slot)[...] = acc[i, pl.ds(pl.multiple_of(half + r, tall), tall), c].astype(bf)
            across(q, slot).start()
            return carry

        lax.fori_loop(0, pieces, give, 0)

        def given(q, carry):
            across(q, lax.rem(q, slots)).wait_send()
            return carry

        lax.fori_loop(pieces - slots, pieces, given, 0)
        remote(core_land[number], core_land[number], csend.at[number, 0], crecv.at[number], c_dev).wait_recv()

        def bring(q, slot):
            i, r, c = piece(q)
            return pltpu.make_async_copy(core_land[number].at[i, pl.ds(r, tall), c], held(slot), hsem.at[slot])

        def store(q, slot):
            i, r, c = piece(q)
            return pltpu.make_async_copy(stage(slot), grad_sum[number].at[i, pl.ds(r, tall), c], dsem.at[slot])

        for q in range(slots - 1):
            bring(q, q).start()

        def keep(q, carry):
            slot = lax.rem(q, slots)
            coming = q + slots - 1
            pl.when(coming < pieces)(lambda: bring(coming, lax.rem(coming, slots)).start())
            pl.when(q >= slots)(lambda: store(q - slots, slot).wait())
            bring(q, slot).wait()
            i, r, c = piece(q)
            stage(slot)[...] = (acc[i, pl.ds(r, tall), c] + held(slot)[...].astype(f32)).astype(bf)
            store(q, slot).start()
            return carry

        lax.fori_loop(0, pieces, keep, 0)

        def kept(q, carry):
            store(q, lax.rem(q, slots)).wait()
            return carry

        lax.fori_loop(pieces - slots, pieces, kept, 0)

    def x_copy():
        return remote(grad_sum[0], x_land, xsend, xrecv, x_dev)

    def c_loads(o, slot):
        return [
            pltpu.make_async_copy(c_all.at[o * 2 + r], cv.at[slot, pl.ds(r * shard, shard)], insem.at[1, r, slot])
            for r in range(2)
        ]

    def x_loads(o, slot):
        copies = []
        for r in range(2):
            part = pl.ds(r * shard, shard)
            copies += [
                pltpu.make_async_copy(x_all.at[o * 2 + r], xv.at[slot, part], insem.at[0, r, slot]),
                pltpu.make_async_copy(s_all.at[o * 2 + r, pl.ds(0, shard)], sv.at[slot, part], insem.at[2, r, slot]),
            ]
        return copies

    def spot(o, n):
        return pl.ds(pl.multiple_of(o * tile, tile), tile), pl.ds(pl.multiple_of(n * cut, cut), cut)

    def outgoing(o, n, slot):
        r, c = spot(o, n)
        return [
            pltpu.make_async_copy(ostage.at[slot, i], ref.at[r, c], osem.at[i, slot])
            for i, ref in enumerate((mix, gx))
        ]

    def earlier(o, n, slot):
        r, c = spot(o, n)
        return [
            pltpu.make_async_copy(ref.at[r, c], prev.at[slot, i], psem.at[i, slot])
            for i, ref in enumerate((mix, gx))
        ]

    def weight_loads(number):
        return [
            pltpu.make_async_copy(weights[number][i][h], wv.at[i, pl.ds(h * half, half)], wsem.at[i, h])
            for i in range(3)
            for h in range(2)
        ]

    def run_tile(number, o, slot):
        if number:
            for copy in earlier(o, 0, 0):
                copy.start()
        pick = (lane == experts[number]).astype(f32)
        share = jnp.sum(sv[slot] * pick, axis=1, keepdims=True)

        def hidden_block(j, dots):
            part = pl.ds(pl.multiple_of(j * block, block), block)
            rows_in, cots = xv[slot], cv[slot]
            gate_pre = nt(rows_in, wv[0, part, :])
            up_pre = nt(rows_in, wv[1, part, :])
            grad_raw = nt(cots, wv[2, part, :])
            sig = jax.nn.sigmoid(gate_pre)
            silu = gate_pre * sig
            low = (silu * up_pre).astype(bf).astype(f32)
            dots = dots + jnp.sum(low * grad_raw, axis=1, keepdims=True)
            grad_hid = grad_raw * share
            grad_gate = (grad_hid * up_pre * sig * (1.0 + gate_pre * (1.0 - sig))).astype(bf)
            grad_up = (grad_hid * silu).astype(bf)
            shared = (low * share).astype(bf)
            hid_s[:, part] = shared
            gate_s[:, part] = grad_gate
            up_s[:, part] = grad_up
            acc[0, part, :] += tn(grad_gate, rows_in)
            acc[1, part, :] += tn(grad_up, rows_in)
            acc[2, part, :] += tn(shared, cots)
            return dots

        dots = lax.fori_loop(0, hidden // block, hidden_block, jnp.zeros((tile, 1), f32))
        both = dots * pick
        for r in range(2):
            turned = jnp.transpose(both[r * shard : (r + 1) * shard, :])[: gst.shape[1], :]
            gst[o * 2 + r] = gst[o * 2 + r] + turned if number else turned

        def column_block(n, inner):
            now = lax.rem(n, 2)
            columns = pl.ds(pl.multiple_of(n * cut, cut), cut)

            @pl.when(n >= 2)
            def _():
                for copy in outgoing(o, n - 2, now):
                    copy.wait()

            out = nn(hid_s[...], wv[2, :, columns])
            back = nn(gate_s[...], wv[0, :, columns]) + nn(up_s[...], wv[1, :, columns])
            if number:
                @pl.when(n + 1 < cuts)
                def _():
                    for copy in earlier(o, n + 1, 1 - now):
                        copy.start()

                for copy in earlier(o, n, now):
                    copy.wait()
                out = out + prev[now, 0].astype(f32)
                back = back + prev[now, 1].astype(f32)
            ostage[now, 0] = out.astype(bf)
            ostage[now, 1] = back.astype(bf)
            for copy in outgoing(o, n, now):
                copy.start()
            return inner

        lax.fori_loop(0, cuts, column_block, 0)
        for n in (cuts - 2, cuts - 1):
            for copy in outgoing(o, n, n % 2):
                copy.wait()

    greet([x_dev, y_dev, c_dev, up_dev, down_dev], [None, None, None, up, down])
    gather_first()
    loads = weight_loads(0) + c_loads(items[0], 0)
    for copy in loads:
        copy.start()
    acc[...] = jnp.zeros_like(acc)
    own_in[0].wait()
    own_out.start()
    for copy in loads[:-2]:
        copy.wait()
    own_out.wait()
    own_in[1].wait()

    def first_pass(t, carry):
        slot = lax.rem(t, 2)
        o = nearest(t)

        @pl.when(t + 1 < tiles)
        def _():
            gather_next(t + 1)
            for copy in c_loads(nearest(t + 1), 1 - slot):
                copy.start()

        gather_landed(o)
        now = x_loads(o, slot)
        for copy in now:
            copy.start()
        for copy in now + c_loads(o, slot):
            copy.wait()
        run_tile(0, o, slot)
        return carry

    lax.fori_loop(0, tiles, first_pass, 0)
    loads = weight_loads(1)
    begin = c_loads(items[3], 0) + x_loads(items[3], 0)
    for copy in loads + begin:
        copy.start()
    flush(0)
    x_copy().start()
    acc[...] = jnp.zeros_like(acc)
    for copy in loads:
        copy.wait()

    def second_pass(t, carry):
        slot = lax.rem(t, 2)
        o = farthest(t)

        @pl.when(t + 1 < tiles)
        def _():
            for copy in c_loads(farthest(t + 1), 1 - slot) + x_loads(farthest(t + 1), 1 - slot):
                copy.start()

        for copy in c_loads(o, slot) + x_loads(o, slot):
            copy.wait()
        run_tile(1, o, slot)
        for copy in y_copies(o):
            copy.start()
        k = jnp.where(mid, t - 2, t - 1)
        pl.when(k >= 0)(lambda: pump(farthest(k), False))
        return carry

    lax.fori_loop(0, tiles, second_pass, 0)
    pl.when(mid)(lambda: pump(items[1], False))
    flush(1)
    pump(z, True)
    for k in range(4):
        for copy in y_copies(items[k]):
            copy.wait_send()
        if k:
            z_go(items[k], lambda copy: copy.wait_send())
    gather_sent()
    x_copy().wait()


def expert_pass(x_own, s_own, c_all, weights, gs_rows, cid):
    blocks, shard, width = c_all.shape
    rows = blocks * shard
    half = weights[0][0][0].shape[0]
    hidden = 2 * half
    tile, block, cut = 2 * shard, half, 512
    anys = pl.BlockSpec(memory_space=pl.ANY)
    sem = pltpu.SemaphoreType.DMA
    flat = [w for one in weights for pair in one for w in pair]
    shaped = jax.ShapeDtypeStruct
    half_grads = shaped((3, half, width), bf)
    shapes = [
        shaped((blocks, shard, width), bf),
        shaped((blocks,) + s_own.shape, f32),
        shaped((rows, width), bf),
        shaped((rows, width), bf),
        shaped((shard, width), bf),
        shaped((gs_rows, shard), f32),
        shaped((4, shard, width), bf),
        shaped((5, shard, width), bf),
    ] + [half_grads] * 5
    return pl.pallas_call(
        functools.partial(expert_body, shard, width, half, block, cut),
        in_specs=[anys] * (3 + len(flat)),
        out_specs=[anys] * len(shapes),
        out_shape=shapes,
        scratch_shapes=[
            pltpu.VMEM((2, tile, width), bf),
            pltpu.VMEM((2, tile, width), bf),
            pltpu.VMEM((2, tile, 128), f32),
            pltpu.VMEM((3, hidden, width), bf),
            pltpu.VMEM((3, hidden, width), f32),
            pltpu.VMEM((tile, hidden), bf),
            pltpu.VMEM((tile, hidden), bf),
            pltpu.VMEM((tile, hidden), bf),
            pltpu.VMEM((blocks, gs_rows, shard), f32),
            pltpu.VMEM((4, gs_rows, shard), f32),
            pltpu.VMEM((5, gs_rows, shard), f32),
            pltpu.VMEM((2, 2, tile, cut), bf),
            pltpu.VMEM((2, 2, tile, cut), bf),
            sem((3, 4, 2)),
            sem((3, 4, 2)),
            sem((2,)),
            sem((2, 5, 2)),
            sem((2, 5, 2)),
            sem((2, 8)),
            sem((2,)),
            sem,
            sem,
            sem((3, 2)),
            sem((3, 2, 2)),
            sem((2, 2)),
            sem((2, 2)),
            sem((8,)),
            sem((8,)),
            sem((3, 2)),
        ],
        compiler_params=pltpu.CompilerParams(
            vmem_limit_bytes=63 * 2**20, collective_id=cid, has_side_effects=True
        ),
        name="expert_pass",
    )(x_own, s_own, c_all, *flat)
def attend_body(scale, q_ref, k_ref, v_ref, bias_ref, out_ref, lse_ref, top_ref):
    head = pl.program_id(0)
    scores = nt(q_ref[...], k_ref[...]) * scale + bias_ref[...]
    top = jnp.max(scores, axis=1, keepdims=True)
    parts = jnp.exp(scores - top)
    total = jnp.sum(parts, axis=1, keepdims=True)
    probs = (parts * (1.0 / total)).astype(bf)
    out_ref[...] = nn(probs, v_ref[...]).astype(bf)
    lane = lax.broadcasted_iota(jnp.int32, lse_ref.shape, 1)

    @pl.when(head == 0)
    def _():
        lse_ref[...] = jnp.zeros_like(lse_ref)
        top_ref[...] = jnp.zeros_like(top_ref)

    lse_ref[...] = jnp.where(lane == head, top + jnp.log(total), lse_ref[...])
    row = lax.broadcasted_iota(jnp.int32, top_ref.shape, 1)
    top_ref[...] = jnp.where(row == head, jnp.max(top), top_ref[...])


def attend(queries, keys_values, bias, heads, scale):
    rows, width = queries.shape
    keys = keys_values.shape[0]
    size = width // heads
    return pl.pallas_call(
        functools.partial(attend_body, scale),
        grid=(heads,),
        in_specs=[
            pl.BlockSpec((rows, size), lambda h: (0, h)),
            pl.BlockSpec((keys, size), lambda h: (0, h)),
            pl.BlockSpec((keys, size), lambda h: (0, heads + h)),
            pl.BlockSpec((rows, keys), lambda h: (0, 0)),
        ],
        out_specs=[
            pl.BlockSpec((rows, size), lambda h: (0, h)),
            pl.BlockSpec((rows, 128), lambda h: (0, 0)),
            pl.BlockSpec((8, 128), lambda h: (0, 0)),
        ],
        out_shape=[
            jax.ShapeDtypeStruct((rows, width), bf),
            jax.ShapeDtypeStruct((rows, 128), f32),
            jax.ShapeDtypeStruct((8, 128), f32),
        ],
        compiler_params=pltpu.CompilerParams(vmem_limit_bytes=48 * 2**20),
        name="attend",
    )(queries, keys_values, keys_values, bias)


def attend_back_body(scale, q_ref, k_ref, v_ref, g_ref, bias_ref, lse_ref, dq_ref, dk_ref, dv_ref):
    head = pl.program_id(0)
    lane = lax.broadcasted_iota(jnp.int32, lse_ref.shape, 1)
    lse = jnp.sum(jnp.where(lane == head, lse_ref[...], 0.0), axis=1, keepdims=True)
    queries, keys, grads = q_ref[...], k_ref[...], g_ref[...]
    probs = jnp.exp(nt(queries, keys) * scale + bias_ref[...] - lse)
    low = probs.astype(bf)
    dv_ref[...] = tn(low, grads).astype(bf)
    grad_probs = nt(grads, v_ref[...])
    shift = jnp.sum(probs * grad_probs, axis=1, keepdims=True)
    grad_scores = (probs * (grad_probs - shift)).astype(bf)
    dq_ref[...] = (nn(grad_scores, keys) * scale).astype(bf)
    dk_ref[...] = (tn(grad_scores, queries) * scale).astype(bf)


def attend_back(queries, keys_values, grads, bias, lse, heads, scale):
    rows, width = queries.shape
    keys = keys_values.shape[0]
    size = width // heads
    own = pl.BlockSpec((rows, size), lambda h: (0, h))
    seen = pl.BlockSpec((keys, size), lambda h: (0, h))
    return pl.pallas_call(
        functools.partial(attend_back_body, scale),
        grid=(heads,),
        in_specs=[
            own,
            seen,
            pl.BlockSpec((keys, size), lambda h: (0, heads + h)),
            own,
            pl.BlockSpec((rows, keys), lambda h: (0, 0)),
            pl.BlockSpec((rows, 128), lambda h: (0, 0)),
        ],
        out_specs=[own, seen, seen],
        out_shape=[
            jax.ShapeDtypeStruct((rows, width), bf),
            jax.ShapeDtypeStruct((keys, width), bf),
            jax.ShapeDtypeStruct((keys, width), bf),
        ],
        compiler_params=pltpu.CompilerParams(vmem_limit_bytes=48 * 2**20),
        name="attend_back",
    )(queries, keys_values, keys_values, grads, bias, lse)


def chain(z, y, x, core, per_seq):
    chip = (z * 2 + y) * 2 + x
    at = lax.rem(chip, per_seq)
    before, after = at > 0, at < per_seq - 1
    previous = (chip - jnp.where(before, 1, 0)) * 2 + core
    following = (chip + jnp.where(after, 1, 0)) * 2 + core
    return previous, following, before, after


def return_body(per_seq, *refs):
    parts, out = refs[:2], refs[2]
    far, own, adj, mine, lands, ssem, rsem, lsem = refs[3:]
    z, y, x, core = place()
    c_dev = index_of(z, y, x, 1 - core)
    previous, following, before, after = chain(z, y, x, core, per_seq)
    greet([c_dev, previous, following], [None, before, after])
    rows = own.shape[1]
    far_slot, plain_slot = 4 * (1 - core), 4 * core
    adds = jnp.where(core == 0, after, before)
    gives = jnp.where(core == 0, before, after)

    def to_core(kind, a):
        slot = jnp.where(kind == 0, 1 + 2 * core, 3 - 2 * core)
        land = adj.at[a] if kind == 0 else mine.at[a]
        return remote(parts[a].at[slot], land, ssem.at[kind, a], rsem.at[kind, a], c_dev)

    def plain(kind, a, device, sem):
        return remote(parts[a].at[plain_slot], lands.at[1 if kind == 2 else 0, a], ssem.at[sem, a], rsem.at[kind, a], device)

    def summed(kind, a, device, sem):
        return remote(far.at[a], lands.at[1 if kind == 2 else 0, a], ssem.at[sem, a], rsem.at[kind, a], device)

    loads = []
    for a in range(2):
        pl.when(gives)(lambda a=a: to_core(0, a).start())
        to_core(1, a).start()
        loads.append(pltpu.make_async_copy(parts[a].at[far_slot], far.at[a], lsem.at[0, a]))
        loads.append(pltpu.make_async_copy(parts[a].at[2], own.at[a], lsem.at[1, a]))
    for copy in loads:
        copy.start()
    for a in range(2):
        pl.when((core == 0) & before)(lambda a=a: plain(2, a, previous, 2).start())
        pl.when((core == 1) & after)(lambda a=a: plain(3, a, following, 2).start())
    for a in range(2):
        @pl.when(adds)
        def _(a=a):
            to_core(0, a).wait_recv()
        loads[2 * a].wait()

        @pl.when(adds)
        def _(a=a):
            add_into(far.at[a], adj.at[a])
            pl.when(core == 0)(lambda: summed(3, a, following, 3).start())
            pl.when(core == 1)(lambda: summed(2, a, previous, 3).start())

    width = own.shape[2]
    for a in range(2):
        loads[2 * a + 1].wait()
        to_core(1, a).wait_recv()
        add_into(own.at[a], mine.at[a])
    for a in range(2):
        @pl.when(before)
        def _(a=a):
            plain(3, a, previous, 2).wait_recv()
            add_into(own.at[a], lands.at[0, a])

        @pl.when(after)
        def _(a=a):
            plain(2, a, previous, 2).wait_recv()
            add_into(own.at[a], lands.at[1, a])

        out[:, a * width : (a + 1) * width] = own[a]
    for a in range(2):
        pl.when(gives)(lambda a=a: to_core(0, a).wait_send())
        to_core(1, a).wait_send()
        pl.when((core == 0) & before)(lambda a=a: plain(2, a, previous, 2).wait_send())
        pl.when((core == 1) & after)(lambda a=a: plain(3, a, following, 2).wait_send())
        pl.when((core == 0) & after)(lambda a=a: summed(3, a, following, 3).wait_send())
        pl.when((core == 1) & before)(lambda a=a: summed(2, a, previous, 3).wait_send())


def return_near(parts, per_seq, cid):
    slots, rows, width = parts[0].shape
    anys = pl.BlockSpec(memory_space=pl.ANY)
    sem = pltpu.SemaphoreType.DMA
    block = pltpu.VMEM((2, rows, width), bf)
    return pl.pallas_call(
        functools.partial(return_body, per_seq),
        in_specs=[anys, anys],
        out_specs=pl.BlockSpec(memory_space=pltpu.VMEM),
        out_shape=jax.ShapeDtypeStruct((rows, 2 * width), bf),
        scratch_shapes=[
            block,
            block,
            block,
            block,
            pltpu.VMEM((2, 2, rows, width), bf),
            sem((4, 2)),
            sem((4, 2)),
            sem((2, 2)),
        ],
        compiler_params=pltpu.CompilerParams(
            collective_id=cid, has_side_effects=True, vmem_limit_bytes=40 * 2**20
        ),
        name="return_near",
    )(*parts)


def dense_layer(
    tokens,
    w_query,
    w_key,
    w_value,
    w_out,
    w_router,
    gain_attn,
    gain_moe,
    w_gate,
    w_up,
    w_down,
    routes,
    doc_lengths,
    clip_limit,
    cotangent,
):
    devices = lax.axis_size("fsdp")
    device = lax.axis_index("fsdp")
    tok_rows = tokens.shape[0]
    model_width = tokens.shape[1]
    weight_rows = w_query.shape[0]
    head_count = clip_limit.shape[0]
    head_size = model_width // head_count
    experts = w_router.shape[1]
    seq_len = devices * tok_rows // doc_lengths.shape[0]
    score_scale = head_size ** (-0.5)
    wide_width = 3 * model_width
    extra = jnp.pad(
        jnp.concatenate((w_router, gain_attn[:, None], gain_moe[:, None]), axis=1),
        ((0, 0), (0, 128 - experts - 2)),
    )
    wide_own = jnp.concatenate((w_query, w_key, w_value, extra), axis=1)
    per_seq = devices // (2 * doc_lengths.shape[0])
    wide_full, out_full, near_tokens = full_gather([wide_own, w_out], tokens, per_seq, 2)
    wide_full = wide_full.reshape(model_width, wide_width + 128)
    out_full = out_full.reshape(model_width, model_width)
    later = lax.optimization_barrier((out_full, cotangent, w_gate, w_up, w_down))
    out_full, cot_own, gate_own, up_own, down_own = later
    planes = [
        [index_of(z, y, x, core) for z in range(4) for y in range(2)] for x in range(2) for core in range(2)
    ]
    c_all = lax.all_gather(cot_own, "fsdp", axis_index_groups=planes)
    x_weights = [swapped(w, "fsdp", 1) for w in (gate_own, up_own, down_own)]
    core_weights = [swapped(w, "fsdp", 0) for w in (gate_own, up_own, down_own)]
    corner_weights = [swapped(w, "fsdp", 0) for w in x_weights]
    expert_weights = [
        list(zip(x_weights, corner_weights)),
        list(zip((gate_own, up_own, down_own), core_weights)),
    ]
    router_full = wide_full[:, wide_width : wide_width + experts]
    gain_one = wide_full[:, wide_width + experts]
    gain_two = wide_full[:, wide_width + experts + 1]
    token_values = tokens.astype(f32)
    scale_one = rms_scale(token_values)
    attn_gain = gain_one.astype(f32)
    reach_count = (HALF - 2) // tok_rows + 1
    slots = 2 * reach_count + 1
    key_count = slots * tok_rows
    row_index = jnp.arange(tok_rows, dtype=jnp.int32)
    query_places = device * tok_rows + row_index
    key_places = (device - reach_count) * tok_rows + jnp.arange(key_count, dtype=jnp.int32)
    query_docs = document_of(query_places, doc_lengths, seq_len)
    key_docs = document_of(key_places, doc_lengths, seq_len)
    near_by = (key_docs >= 0) & (key_places // seq_len == query_places[0] // seq_len)
    visible = (
        (query_docs[:, None] == key_docs[None, :])
        & near_by[None, :]
        & (jnp.abs(query_places[:, None] - key_places[None, :]) < HALF)
    )
    bias = jnp.where(visible, 0.0, masked)
    near_values = jnp.where(near_by[:, None], near_tokens.reshape(key_count, model_width).astype(f32), 0.0)
    near_normed = (near_values * rms_scale(near_values) * attn_gain).astype(bf)
    own_first = reach_count * tok_rows
    normed_attn = near_normed[own_first : own_first + tok_rows]
    queries = jnp.dot(normed_attn, wide_full[:, :model_width], preferred_element_type=f32).astype(bf)
    keys_values = jnp.dot(
        near_normed, wide_full[:, model_width:wide_width], preferred_element_type=f32
    ).astype(bf)
    context, log_total, own_top = attend(queries, keys_values, bias, head_count, score_scale)
    attended = token_values + jnp.dot(context, out_full, preferred_element_type=f32)
    scale_two = rms_scale(attended)
    moe_gain = gain_two.astype(f32)
    normed_moe = (attended * scale_two * moe_gain).astype(bf)
    logits = jnp.dot(normed_moe, router_full, preferred_element_type=f32)
    named = jnp.any(routes[:, :, None] == jnp.arange(experts, dtype=jnp.int32)[None, None, :], axis=1)
    chosen = jnp.where(named, logits, masked)
    lifted = jnp.where(named, jnp.exp(logits - jnp.max(chosen, axis=1, keepdims=True)), 0.0)
    gate_share = lifted / jnp.sum(lifted, axis=1, keepdims=True)
    share_rows = jnp.concatenate(
        (
            jnp.pad(gate_share, ((0, 0), (0, 128 - experts))),
            own_top,
        ),
        axis=0,
    )
    expert_results = expert_pass(normed_moe, share_rows, c_all, expert_weights, experts, 0)
    s_all, mix_part, grad_from_experts, grad_share = [expert_results[i] for i in (1, 2, 4, 5)]
    x_terms, own_sum = expert_results[12], expert_results[11]
    head_max = jnp.max(s_all[:, tok_rows, :head_count], axis=0)
    head_max = jnp.maximum(head_max, swapped(head_max, "fsdp", 0))
    head_max = jnp.maximum(head_max, swapped(head_max, "fsdp", 1))
    factor = clip_limit / jnp.maximum(head_max, clip_limit)
    columns = jnp.repeat(jnp.sqrt(factor), head_size)
    clipped_query = (w_query.astype(f32) * columns[None, :]).astype(bf)
    clipped_key = (w_key.astype(f32) * columns[None, :]).astype(bf)
    mixture = lax.psum_scatter(mix_part, "fsdp", axis_index_groups=planes, tiled=True)
    grad_share = jnp.transpose(grad_share)
    grad_mixed = cotangent.astype(f32)
    grad_logits = gate_share * (grad_share - jnp.sum(gate_share * grad_share, axis=1, keepdims=True))
    grad_router_part = jnp.dot(normed_moe.astype(f32).T, grad_logits, precision=highest)
    grad_normed_moe = grad_from_experts.astype(f32) + jnp.dot(
        grad_logits, router_full.astype(f32).T, precision=highest
    )
    grad_from_norm, grad_gain_two = norm_back(grad_normed_moe, attended, scale_two, moe_gain)
    grad_attended = grad_mixed + grad_from_norm
    grad_attended_low = grad_attended.astype(bf)
    grad_out_part = contract(context, grad_attended_low, 0, 0).astype(bf)
    out_sum = lax.psum_scatter(grad_out_part, "fsdp", scatter_dimension=0, tiled=True)
    grad_context = contract(grad_attended_low, out_full, 1, 1).astype(bf)
    grad_queries, near_keys, near_values_grad = attend_back(
        queries, keys_values, grad_context, bias, log_total, head_count, score_scale
    )
    near_shape = (slots, tok_rows, model_width)
    grad_kv_low = return_near(
        [near_keys.reshape(near_shape), near_values_grad.reshape(near_shape)], per_seq, 1
    )
    grad_kv_low, own_sum, x_terms = lax.optimization_barrier((grad_kv_low, own_sum, x_terms))
    expert_grads = own_sum.astype(f32) + x_terms.astype(f32)
    grad_gate, grad_up, grad_down = expert_grads[0], expert_grads[1], expert_grads[2]
    grad_qkv = jnp.concatenate((grad_queries, grad_kv_low), axis=1)
    grad_qkv_part = contract(normed_attn, grad_qkv, 0, 0).astype(bf)
    grad_normed_attn = contract(jnp.pad(grad_qkv, ((0, 0), (0, 128))), wide_full, 1, 1)
    grad_from_first, grad_gain_one = norm_back(grad_normed_attn, token_values, scale_one, attn_gain)
    grad_tokens = grad_attended + grad_from_first
    extra_part = jnp.pad(
        jnp.concatenate((grad_router_part, grad_gain_one[:, None], grad_gain_two[:, None]), axis=1),
        ((0, 0), (0, 128 - experts - 2)),
    )
    owners = (devices // 2, 2, weight_rows)
    qkv_sum, extra_sum = full_reduce(
        [
            grad_qkv_part.reshape(owners + (wide_width,)),
            extra_part.reshape(owners + (128,)),
        ],
        3,
    )
    mixture, out_sum, qkv_sum = lax.optimization_barrier((mixture, out_sum, qkv_sum))
    mixed = (attended + mixture.astype(f32)).astype(bf)
    return (
        mixed,
        grad_tokens,
        qkv_sum[:, :model_width],
        qkv_sum[:, model_width : 2 * model_width],
        qkv_sum[:, 2 * model_width :],
        out_sum.astype(f32),
        extra_sum[:, :experts],
        extra_sum[:, experts],
        extra_sum[:, experts + 1],
        grad_gate,
        grad_up,
        grad_down,
        clipped_query,
        clipped_key,
    )


def chosen_layer(mesh):
    def layer(*arrays):
        experts, top_count = arrays[5].shape[1], arrays[11].shape[1]
        if mesh.shape["fsdp"] == 32 and 2 * top_count >= experts:
            return dense_layer(*arrays)
        return routed_layer(*arrays)

    return layer


def solution(mesh):
    placed = (
        P("fsdp", None),
        P("fsdp", None),
        P("fsdp", None),
        P("fsdp", None),
        P("fsdp", None),
        P("fsdp", None),
        P("fsdp"),
        P("fsdp"),
        P("fsdp", None),
        P("fsdp", None),
        P("fsdp", None),
        P("fsdp", None),
        P(),
        P(),
        P("fsdp", None),
    )
    return jax.shard_map(
        chosen_layer(mesh),
        mesh=mesh,
        in_specs=placed,
        out_specs=(
            P("fsdp", None),
            P("fsdp", None),
            P("fsdp", None),
            P("fsdp", None),
            P("fsdp", None),
            P("fsdp", None),
            P("fsdp", None),
            P("fsdp"),
            P("fsdp"),
            P("fsdp", None),
            P("fsdp", None),
            P("fsdp", None),
            P("fsdp", None),
            P("fsdp", None),
        ),
        check_vma=False,
    )
```

```python
import functools
from functools import reduce

import jax
import jax.numpy as jnp
from jax import lax
from jax.experimental import pallas as pl
from jax.experimental.pallas import tpu as pltpu
from jax.sharding import PartitionSpec as P

HALF = 512


epsilon = 1e-05
masked = -1e30
highest = lax.Precision.HIGHEST


def passed_along(x, axis, by):
    length = lax.axis_size(axis)
    pairs = [(i, i + by) for i in range(length) if 0 <= i + by < length]
    return lax.ppermute(x, axis, pairs)


def swapped(block, axis, apart):
    count = lax.axis_size(axis)
    route = []
    for low in range(count):
        high = low | 1 << apart
        if high != low and high < count:
            route += [(low, high), (high, low)]
    return lax.ppermute(block, axis, route)


def rms_scale(source):
    return lax.rsqrt(jnp.mean(source * source, axis=-1, keepdims=True) + epsilon)


def norm_back(grad_normed, source, scale_rows, gain):
    unit_rows = source * scale_rows
    grad_unit = grad_normed * gain
    grad_gain = jnp.sum(grad_normed * unit_rows, axis=0)
    grad_source = scale_rows * (
        grad_unit - unit_rows * jnp.mean(grad_unit * unit_rows, axis=-1, keepdims=True)
    )
    return (grad_source, grad_gain)


def document_of(places, doc_lengths, seq_len):
    doc_ends = jnp.cumsum(doc_lengths, axis=1)
    seq_count = doc_lengths.shape[0]
    doc_count = doc_lengths.shape[1]
    sequence = places // seq_len
    within = places % seq_len
    picked = (sequence[:, None] == jnp.arange(seq_count, dtype=jnp.int32)[None, :]).astype(
        jnp.int32
    )
    ends_of = jnp.dot(picked, doc_ends)
    local_doc = jnp.sum((within[:, None] >= ends_of).astype(jnp.int32), axis=1)
    inside = (places >= 0) & (places < seq_count * seq_len)
    return jnp.where(inside, sequence * doc_count + local_doc, -1)


def contract(left, right, left_dim, right_dim):
    return lax.dot_general(
        left, right, (((left_dim,), (right_dim,)), ((), ())), preferred_element_type=jnp.float32
    )


def routed_layer(
    tokens,
    w_query,
    w_key,
    w_value,
    w_out,
    w_router,
    gain_attn,
    gain_moe,
    w_gate,
    w_up,
    w_down,
    routes,
    doc_lengths,
    clip_limit,
    cotangent,
):
    devices = lax.axis_size("fsdp")
    device = lax.axis_index("fsdp")
    tok_rows = tokens.shape[0]
    model_width = tokens.shape[1]
    head_count = clip_limit.shape[0]
    head_size = model_width // head_count
    experts = w_router.shape[1]
    top_count = routes.shape[1]
    seq_len = devices * tok_rows // doc_lengths.shape[0]
    score_scale = head_size ** (-0.5)
    gathered = (
        lax.all_gather(w_query, "fsdp", axis=0, tiled=True),
        lax.all_gather(w_key, "fsdp", axis=0, tiled=True),
        lax.all_gather(w_value, "fsdp", axis=0, tiled=True),
        lax.all_gather(w_out, "fsdp", axis=0, tiled=True),
        lax.all_gather(w_router, "fsdp", axis=0, tiled=True),
        lax.all_gather(gain_attn, "fsdp", axis=0, tiled=True),
        lax.all_gather(gain_moe, "fsdp", axis=0, tiled=True),
    )
    query_full, key_full, value_full, out_full, router_full, gain_one, gain_two = gathered
    token_values = tokens.astype(jnp.float32)
    scale_one = rms_scale(token_values)
    attn_gain = gain_one.astype(jnp.float32)
    normed_attn = (token_values * scale_one * attn_gain).astype(jnp.bfloat16)
    queries = jnp.dot(normed_attn, query_full, preferred_element_type=jnp.float32).astype(
        jnp.bfloat16
    )
    kv_own = jnp.concatenate(
        (
            jnp.dot(normed_attn, key_full, preferred_element_type=jnp.float32),
            jnp.dot(normed_attn, value_full, preferred_element_type=jnp.float32),
        ),
        axis=1,
    ).astype(jnp.bfloat16)
    reach_count = (HALF - 2) // tok_rows + 1
    offsets = list(range(reach_count, 0, -1)) + list(range(-1, -reach_count - 1, -1))
    arrived = [passed_along(kv_own, "fsdp", offset) for offset in offsets]
    kv_rows = jnp.concatenate(arrived[:reach_count] + [kv_own] + arrived[reach_count:], axis=0)
    ordered = offsets[:reach_count] + [0] + offsets[reach_count:]
    row_index = jnp.arange(tok_rows, dtype=jnp.int32)
    query_places = device * tok_rows + row_index
    key_places = jnp.concatenate([(device - offset) * tok_rows + row_index for offset in ordered])
    query_docs = document_of(query_places, doc_lengths, seq_len)
    key_docs = document_of(key_places, doc_lengths, seq_len)
    visible = (
        (query_docs[:, None] == key_docs[None, :])
        & (key_docs[None, :] >= 0)
        & (jnp.abs(query_places[:, None] - key_places[None, :]) < HALF)
    )
    key_count = kv_rows.shape[0]
    query_heads = queries.reshape(tok_rows, head_count, head_size)
    key_heads = kv_rows[:, :model_width].reshape(key_count, head_count, head_size)
    value_heads = kv_rows[:, model_width:].reshape(key_count, head_count, head_size)

    def scores_of():
        raw_scores = (
            jnp.einsum("qhd,khd->hqk", query_heads, key_heads, preferred_element_type=jnp.float32)
            * score_scale
        )
        return jnp.where(visible[None], raw_scores, masked)

    scores = scores_of()
    head_top = jnp.max(scores, axis=2, keepdims=True)
    exponents = jnp.exp(scores - head_top)
    totals = jnp.sum(exponents, axis=2, keepdims=True)
    log_total = head_top + jnp.log(totals)
    probs_low = (exponents / totals).astype(jnp.bfloat16)
    head_max = lax.pmax(jnp.max(head_top, axis=(1, 2)), "fsdp")
    context = (
        jnp.einsum("hqk,khd->qhd", probs_low, value_heads, preferred_element_type=jnp.float32)
        .reshape(tok_rows, model_width)
        .astype(jnp.bfloat16)
    )
    attended = token_values + jnp.dot(context, out_full, preferred_element_type=jnp.float32)
    factor = clip_limit / jnp.maximum(head_max, clip_limit)
    columns = jnp.repeat(jnp.sqrt(factor), head_size)
    clipped_query = (w_query.astype(jnp.float32) * columns[None, :]).astype(jnp.bfloat16)
    clipped_key = (w_key.astype(jnp.float32) * columns[None, :]).astype(jnp.bfloat16)
    scale_two = rms_scale(attended)
    moe_gain = gain_two.astype(jnp.float32)
    normed_moe = (attended * scale_two * moe_gain).astype(jnp.bfloat16)
    logits = jnp.dot(normed_moe, router_full, preferred_element_type=jnp.float32)
    matches = routes[:, :, None] == jnp.arange(experts, dtype=jnp.int32)[None, None, :]
    chosen = jnp.sum(jnp.where(matches, logits[:, None, :], 0.0), axis=2)
    gate_share = jax.nn.softmax(chosen, axis=1)
    pair_count = tok_rows * top_count
    capacity = 3 * tok_rows * top_count // devices
    half_cap = capacity // 2
    flat_route = routes.reshape(pair_count)
    one_hot = (flat_route[:, None] == jnp.arange(experts, dtype=jnp.int32)[None, :]).astype(
        jnp.int32
    )
    slot_rank = jnp.sum(jnp.cumsum(one_hot, axis=0) * one_hot, axis=1) - 1
    target_device = 2 * flat_route + slot_rank // half_cap
    target_slot = slot_rank % half_cap
    flat_slot = target_device * half_cap + target_slot
    slot_total = devices * half_cap
    outgoing = (
        jnp.zeros((slot_total, model_width), jnp.bfloat16)
        .at[flat_slot]
        .set(jnp.repeat(normed_moe, top_count, axis=0))
    )
    live_out = jnp.zeros((slot_total,), jnp.int32).at[flat_slot].set(1)
    incoming, live_in = (
        lax.all_to_all(outgoing, "fsdp", split_axis=0, concat_axis=0, tiled=True),
        lax.all_to_all(live_out, "fsdp", split_axis=0, concat_axis=0, tiled=True),
    )
    packed_order = jnp.cumsum(live_in) - 1
    packed_index = jnp.where(live_in > 0, packed_order, slot_total)
    back_index = jnp.clip(packed_order, 0, slot_total - 1)
    live_count = jnp.sum(live_in)
    tile_rows = 128
    tile_count = (live_count + tile_rows - 1) // tile_rows
    packed_rows = (
        jnp.zeros((slot_total + 1, model_width), jnp.bfloat16)
        .at[packed_index]
        .set(incoming)[:slot_total]
    )
    partner_half = swapped((w_gate, w_up, w_down), "fsdp", 0)
    lower = device % 2 == 0

    def joined(own_half, other_half):
        return jnp.where(
            lower, jnp.concatenate((own_half, other_half)), jnp.concatenate((other_half, own_half))
        )

    gate_full = joined(w_gate, partner_half[0])
    up_full = joined(w_up, partner_half[1])
    down_full = joined(w_down, partner_half[2])
    hidden_units = gate_full.shape[0]

    def forward_tile(tile_step, loop_state):
        out_rows, gate_keep, up_keep = loop_state
        tile_start = tile_step * tile_rows
        tile_input = lax.dynamic_slice_in_dim(packed_rows, tile_start, tile_rows, 0)
        gate_pre = contract(tile_input, gate_full, 1, 1)
        up_pre = contract(tile_input, up_full, 1, 1)
        hidden = (jax.nn.silu(gate_pre) * up_pre).astype(jnp.bfloat16)
        result = jnp.dot(hidden, down_full, preferred_element_type=jnp.float32).astype(jnp.bfloat16)
        return (
            lax.dynamic_update_slice_in_dim(out_rows, result, tile_start, 0),
            lax.dynamic_update_slice_in_dim(gate_keep, gate_pre, tile_start, 0),
            lax.dynamic_update_slice_in_dim(up_keep, up_pre, tile_start, 0),
        )

    start_state = (
        jnp.zeros((slot_total, model_width), jnp.bfloat16),
        jnp.zeros((slot_total, hidden_units), jnp.float32),
        jnp.zeros((slot_total, hidden_units), jnp.float32),
    )
    expert_out, gate_keep, up_keep = lax.fori_loop(0, tile_count, forward_tile, start_state)
    returning = jnp.where(live_in[:, None] > 0, expert_out[back_index], jnp.zeros((), jnp.bfloat16))
    came_back = lax.all_to_all(returning, "fsdp", split_axis=0, concat_axis=0, tiled=True)
    pair_out = came_back[flat_slot].reshape(tok_rows, top_count, model_width)
    mixture = jnp.sum(gate_share[:, :, None] * pair_out, axis=1)
    mixed = (attended + mixture).astype(jnp.bfloat16)
    query_back, key_back, value_back, out_back = (
        lax.all_gather(w_query, "fsdp", axis=0, tiled=True),
        lax.all_gather(w_key, "fsdp", axis=0, tiled=True),
        lax.all_gather(w_value, "fsdp", axis=0, tiled=True),
        lax.all_gather(w_out, "fsdp", axis=0, tiled=True),
    )
    grad_mixed = cotangent.astype(jnp.float32)
    grad_share = jnp.sum(grad_mixed[:, None, :] * pair_out, axis=2)
    grad_pair = (
        (gate_share[:, :, None] * grad_mixed[:, None, :])
        .astype(jnp.bfloat16)
        .reshape(pair_count, model_width)
    )
    grad_outgoing = jnp.zeros((slot_total, model_width), jnp.bfloat16).at[flat_slot].set(grad_pair)
    grad_incoming = lax.all_to_all(grad_outgoing, "fsdp", split_axis=0, concat_axis=0, tiled=True)
    grad_packed = (
        jnp.zeros((slot_total + 1, model_width), jnp.bfloat16)
        .at[packed_index]
        .set(grad_incoming)[:slot_total]
    )

    def backward_tile(tile_step, loop_state):
        grad_rows, gate_sum, up_sum, down_sum = loop_state
        tile_start = tile_step * tile_rows
        tile_input = lax.dynamic_slice_in_dim(packed_rows, tile_start, tile_rows, 0)
        tile_grad = lax.dynamic_slice_in_dim(grad_packed, tile_start, tile_rows, 0)
        gate_pre = lax.dynamic_slice_in_dim(gate_keep, tile_start, tile_rows, 0)
        up_pre = lax.dynamic_slice_in_dim(up_keep, tile_start, tile_rows, 0)
        sigmoid_gate = jax.nn.sigmoid(gate_pre)
        silu_gate = gate_pre * sigmoid_gate
        hidden = (silu_gate * up_pre).astype(jnp.bfloat16)
        grad_hidden = contract(tile_grad, down_full, 1, 1)
        grad_gate_pre = (
            grad_hidden * up_pre * sigmoid_gate * (1.0 + gate_pre * (1.0 - sigmoid_gate))
        ).astype(jnp.bfloat16)
        grad_up_pre = (grad_hidden * silu_gate).astype(jnp.bfloat16)
        down_sum = down_sum + contract(hidden, tile_grad, 0, 0)
        gate_sum = gate_sum + contract(grad_gate_pre, tile_input, 0, 0)
        up_sum = up_sum + contract(grad_up_pre, tile_input, 0, 0)
        grad_input = (
            jnp.dot(grad_gate_pre, gate_full, preferred_element_type=jnp.float32)
            + jnp.dot(grad_up_pre, up_full, preferred_element_type=jnp.float32)
        ).astype(jnp.bfloat16)
        return (
            lax.dynamic_update_slice_in_dim(grad_rows, grad_input, tile_start, 0),
            gate_sum,
            up_sum,
            down_sum,
        )

    weight_zero = jnp.zeros((hidden_units, model_width), jnp.float32)
    back_state = (
        jnp.zeros((slot_total, model_width), jnp.bfloat16),
        weight_zero,
        weight_zero,
        weight_zero,
    )
    grad_rows, gate_sum, up_sum, down_sum = lax.fori_loop(0, tile_count, backward_tile, back_state)
    grad_returning = jnp.where(
        live_in[:, None] > 0, grad_rows[back_index], jnp.zeros((), jnp.bfloat16)
    )
    grad_came = lax.all_to_all(grad_returning, "fsdp", split_axis=0, concat_axis=0, tiled=True)
    grad_from_experts = jnp.sum(
        grad_came[flat_slot].reshape(tok_rows, top_count, model_width), axis=1, dtype=jnp.float32
    )
    half_units = w_gate.shape[0]

    def partner_part(grad_sum):
        return jnp.where(lower, grad_sum[half_units:], grad_sum[:half_units])

    def own_part(grad_sum):
        return jnp.where(lower, grad_sum[:half_units], grad_sum[half_units:])

    partner_terms = (
        swapped(partner_part(gate_sum).astype(jnp.bfloat16), "fsdp", 0).astype(jnp.float32),
        swapped(partner_part(up_sum).astype(jnp.bfloat16), "fsdp", 0).astype(jnp.float32),
        swapped(partner_part(down_sum).astype(jnp.bfloat16), "fsdp", 0).astype(jnp.float32),
    )
    grad_gate = own_part(gate_sum) + partner_terms[0]
    grad_up = own_part(up_sum) + partner_terms[1]
    grad_down = own_part(down_sum) + partner_terms[2]
    grad_chosen = gate_share * (
        grad_share - jnp.sum(gate_share * grad_share, axis=1, keepdims=True)
    )
    grad_logits = jnp.sum(jnp.where(matches, grad_chosen[:, :, None], 0.0), axis=1)
    grad_router_part = jnp.dot(normed_moe.astype(jnp.float32).T, grad_logits, precision=highest)
    grad_normed_moe = grad_from_experts + jnp.dot(
        grad_logits, router_full.astype(jnp.float32).T, precision=highest
    )
    grad_from_norm, grad_gain_two = norm_back(grad_normed_moe, attended, scale_two, moe_gain)
    grad_attended = grad_mixed + grad_from_norm
    grad_attended_low = grad_attended.astype(jnp.bfloat16)
    grad_out_part = contract(context, grad_attended_low, 0, 0)
    grad_context = (
        contract(grad_attended_low, out_back, 1, 1)
        .astype(jnp.bfloat16)
        .reshape(tok_rows, head_count, head_size)
    )
    probs = jnp.exp(scores_of() - log_total)
    probs_back = probs.astype(jnp.bfloat16)
    grad_values = jnp.einsum(
        "hqk,qhd->khd", probs_back, grad_context, preferred_element_type=jnp.float32
    )
    grad_probs = jnp.einsum(
        "qhd,khd->hqk", grad_context, value_heads, preferred_element_type=jnp.float32
    )
    grad_scores = (
        probs * (grad_probs - jnp.sum(probs * grad_probs, axis=2, keepdims=True))
    ).astype(jnp.bfloat16)
    grad_queries = (
        (
            jnp.einsum("hqk,khd->qhd", grad_scores, key_heads, preferred_element_type=jnp.float32)
            * score_scale
        )
        .reshape(tok_rows, model_width)
        .astype(jnp.bfloat16)
    )
    grad_keys = (
        jnp.einsum("hqk,qhd->khd", grad_scores, query_heads, preferred_element_type=jnp.float32)
        * score_scale
    )
    grad_kv = jnp.concatenate(
        (grad_keys.reshape(key_count, model_width), grad_values.reshape(key_count, model_width)),
        axis=1,
    )
    grad_blocks = [
        grad_kv[position * tok_rows : (position + 1) * tok_rows] for position in range(len(ordered))
    ]
    own_block = grad_blocks[reach_count]
    remote = grad_blocks[:reach_count] + grad_blocks[reach_count + 1 :]
    returned = [
        passed_along(grad_block.astype(jnp.bfloat16), "fsdp", -offset).astype(grad_block.dtype)
        for grad_block, offset in zip(remote, offsets)
    ]
    grad_kv_low = reduce(jnp.add, returned, own_block).astype(jnp.bfloat16)
    grad_query_part = contract(normed_attn, grad_queries, 0, 0)
    grad_kv_part = contract(normed_attn, grad_kv_low, 0, 0)
    grad_normed_attn = (
        contract(grad_queries, query_back, 1, 1)
        + contract(grad_kv_low[:, :model_width], key_back, 1, 1)
        + contract(grad_kv_low[:, model_width:], value_back, 1, 1)
    )
    grad_from_first, grad_gain_one = norm_back(grad_normed_attn, token_values, scale_one, attn_gain)
    grad_tokens = grad_attended + grad_from_first
    reduced = (
        lax.psum_scatter(grad_query_part, "fsdp", scatter_dimension=0, tiled=True),
        lax.psum_scatter(grad_kv_part[:, :model_width], "fsdp", scatter_dimension=0, tiled=True),
        lax.psum_scatter(grad_kv_part[:, model_width:], "fsdp", scatter_dimension=0, tiled=True),
        lax.psum_scatter(grad_out_part, "fsdp", scatter_dimension=0, tiled=True),
        lax.psum_scatter(grad_router_part, "fsdp", scatter_dimension=0, tiled=True),
        lax.psum_scatter(grad_gain_one, "fsdp", scatter_dimension=0, tiled=True),
        lax.psum_scatter(grad_gain_two, "fsdp", scatter_dimension=0, tiled=True),
    )
    return (
        mixed,
        grad_tokens,
        reduced[0],
        reduced[1],
        reduced[2],
        reduced[3],
        reduced[4],
        reduced[5],
        reduced[6],
        grad_gate,
        grad_up,
        grad_down,
        clipped_query,
        clipped_key,
    )


MESH = pl.DeviceIdType.MESH
f32 = jnp.float32
bf = jnp.bfloat16

def place():
    me = lax.axis_index("fsdp")
    core = lax.rem(me, 2)
    x = lax.rem(lax.div(me, 2), 2)
    y = lax.rem(lax.div(me, 4), 2)
    z = lax.div(me, 8)
    return z, y, x, core

def index_of(z, y, x, core):
    return ((z * 2 + y) * 2 + x) * 2 + core

def remote(src, dst, send, recv, device):
    return pltpu.make_async_remote_copy(
        src_ref=src, dst_ref=dst, send_sem=send, recv_sem=recv, device_id=(device,), device_id_type=MESH)

def greet(devices, conditions):
    barrier = pltpu.get_barrier_semaphore()
    for device, condition in zip(devices, conditions):
        if condition is None:
            pl.semaphore_signal(barrier, inc=1, device_id=(device,), device_id_type=MESH)
        else:
            @pl.when(condition)
            def _(device=device):
                pl.semaphore_signal(barrier, inc=1, device_id=(device,), device_id_type=MESH)
    count = 0
    for condition in conditions:
        count = count + (1 if condition is None else jnp.where(condition, 1, 0))
    pl.semaphore_wait(barrier, count)

def line_items(z):
    low = z < 2
    near = z + 1 - 2 * lax.rem(z, 2)
    return [z, near, jnp.where(low, 2, 1), jnp.where(low, 3, 0)]

def chain(z, y, x, core, per_seq):
    chip = (z * 2 + y) * 2 + x
    at = lax.rem(chip, per_seq)
    before, after = at > 0, at < per_seq - 1
    previous = (chip - jnp.where(before, 1, 0)) * 2 + core
    following = (chip + jnp.where(after, 1, 0)) * 2 + core
    return previous, following, before, after


class Near:
    def __init__(self, per_seq, ins, outs, blanks, holds, nsend, nrecv, lsem):
        z, y, x, core = place()
        self.core, self.ins, self.outs, self.blanks, self.holds = core, ins, outs, blanks, holds
        self.nsend, self.nrecv, self.lsem = nsend, nrecv, lsem
        self.c_dev = index_of(z, y, x, 1 - core)
        self.previous, self.following, self.before, self.after = chain(z, y, x, core, per_seq)
        self.passes = jnp.where(core == 0, self.after, self.before)
        self.gets = jnp.where(core == 0, self.before, self.after)

    def one(self, kind, a):
        src, slot, device = (
            (self.ins[a], 0, self.following),
            (self.ins[a], 4, self.previous),
            (self.ins[a], 1 + 2 * self.core, self.c_dev),
            (self.outs[a].at[4 * (1 - self.core)], 3 - 2 * self.core, self.c_dev),
        )[kind]
        return remote(src, self.outs[a].at[slot], self.nsend.at[kind, a], self.nrecv.at[kind, a], device)

    def own(self, a, store):
        if store:
            return pltpu.make_async_copy(self.holds[a], self.outs[a].at[2], self.lsem.at[0, a])
        return pltpu.make_async_copy(self.ins[a], self.holds[a], self.lsem.at[0, a])

    def fills(self, act):
        missing = (
            (jnp.logical_not(self.before), 0),
            (jnp.logical_not(self.before) & (self.core == 0), 1),
            (jnp.logical_not(self.after) & (self.core == 1), 3),
            (jnp.logical_not(self.after), 4),
        )
        for n, (condition, slot) in enumerate(missing):
            @pl.when(condition)
            def _(n=n, slot=slot):
                for a in range(len(self.ins)):
                    act(pltpu.make_async_copy(self.blanks[a], self.outs[a].at[slot], self.lsem.at[n + 1, a]))

    def start(self):
        for a in range(len(self.ins)):
            pl.when(self.after)(lambda a=a: self.one(0, a).start())
            pl.when(self.before)(lambda a=a: self.one(1, a).start())
            self.one(2, a).start()
            self.own(a, False).start()
            self.blanks[a][...] = jnp.zeros_like(self.blanks[a])
        self.fills(lambda copy: copy.start())
        for a in range(len(self.ins)):
            self.own(a, False).wait()
            self.own(a, True).start()

    def finish(self):
        for a in range(len(self.ins)):
            pl.when(self.before)(lambda a=a: self.one(0, a).wait_recv())
            pl.when(self.after)(lambda a=a: self.one(1, a).wait_recv())
            pl.when(self.passes)(lambda a=a: self.one(3, a).start())
        for a in range(len(self.ins)):
            self.one(2, a).wait_recv()
            pl.when(self.gets)(lambda a=a: self.one(3, a).wait_recv())
            pl.when(self.after)(lambda a=a: self.one(0, a).wait_send())
            pl.when(self.before)(lambda a=a: self.one(1, a).wait_send())
            self.one(2, a).wait_send()
            pl.when(self.passes)(lambda a=a: self.one(3, a).wait_send())
            self.own(a, True).wait()
        self.fills(lambda copy: copy.wait())


def near_scratch(arrays):
    sem = pltpu.SemaphoreType.DMA
    count = len(arrays)
    buffers = [pltpu.VMEM(a.shape, a.dtype) for a in arrays]
    return buffers + buffers + [sem((4, count)), sem((4, count)), sem((5, count))]


def near_shapes(arrays):
    return [jax.ShapeDtypeStruct((5,) + a.shape, a.dtype) for a in arrays]


def gather_all(near, ins, outs, ssem, rsem, lsem):
    count = len(ins)
    z, y, x, core = place()
    mid = (z == 1) | (z == 2)
    up, down = z < 3, z > 0
    x_dev = index_of(z, y, 1 - x, core)
    y_dev = index_of(z, 1 - y, x, core)
    c_dev = index_of(z, y, x, 1 - core)
    up_dev = index_of(jnp.minimum(z + 1, 3), y, x, core)
    down_dev = index_of(jnp.maximum(z - 1, 0), y, x, core)
    greet(
        [x_dev, y_dev, c_dev, up_dev, down_dev, near.previous, near.following],
        [None, None, None, up, down, near.before, near.after],
    )
    own = [pltpu.make_async_copy(ins[a], outs[a].at[index_of(z, y, x, core)], lsem.at[a]) for a in range(count)]
    for copy in own:
        copy.start()
    near.start()
    pending = []

    def go(kind, a, o, src, dst, device, condition=None):
        def make():
            return remote(src, dst, ssem.at[kind, o, a], rsem.at[kind, o, a], device)
        if condition is None:
            make().start()
        else:
            pl.when(condition)(lambda: make().start())
        pending.append((make, condition))

    def arrived(kind, a, o, land):
        remote(land, land, ssem.at[kind, o, a], rsem.at[kind, o, a], c_dev).wait_recv()

    items = line_items(z)

    def first(i):
        o = items[i]
        for a in range(count):
            slot = index_of(o, y, x, core)
            dst = outs[a].at[slot]
            src = ins[a] if i == 0 else dst
            if i == 0:
                go(0, a, o, src, dst, up_dev, up)
                go(1, a, o, src, dst, down_dev, down)
            else:
                from_below = o < z
                for kind, condition in ((0, from_below), (1, jnp.logical_not(from_below))):
                    pl.when(condition)(lambda kind=kind, a=a, o=o, dst=dst: arrived(kind, a, o, dst))
                go(0, a, o, src, dst, up_dev, mid & from_below)
                go(1, a, o, src, dst, down_dev, mid & jnp.logical_not(from_below))
            go(2, a, o, src, dst, x_dev)
            go(3, a, o, src, dst, y_dev)
            go(6, a, o, src, dst, c_dev)

    def second(i):
        o = items[i]
        for a in range(count):
            half = ins[a].shape[0] // 2
            from_x = outs[a].at[index_of(o, y, 1 - x, core)]
            arrived(2, a, o, from_x)
            go(5, a, o, from_x.at[pl.ds(0, half)], from_x.at[pl.ds(0, half)], y_dev)
            from_y = outs[a].at[index_of(o, 1 - y, x, core)]
            arrived(3, a, o, from_y)
            go(4, a, o, from_y.at[pl.ds(half, half)], from_y.at[pl.ds(half, half)], x_dev)
            go(7, a, o, from_x, from_x, c_dev)
            go(8, a, o, from_y, from_y, c_dev)

    def third(i):
        o = items[i]
        for a in range(count):
            half = ins[a].shape[0] // 2
            corner = outs[a].at[index_of(o, 1 - y, 1 - x, core)]
            arrived(5, a, o, corner.at[pl.ds(0, half)])
            arrived(4, a, o, corner.at[pl.ds(half, half)])
            go(9, a, o, corner, corner, c_dev)

    first(0); first(1); second(0); first(2); second(1); third(0); first(3); second(2); third(1); second(3); third(2); third(3)
    near.finish()
    for i in range(4):
        o = items[i]
        for a in range(count):
            for kind, (yy, xx) in ((6, (y, x)), (7, (y, 1 - x)), (8, (1 - y, x)), (9, (1 - y, 1 - x))):
                arrived(kind, a, o, outs[a].at[index_of(o, yy, xx, 1 - core)])
    for make, condition in pending:
        if condition is None:
            make().wait_send()
        else:
            pl.when(condition)(lambda make=make: make().wait_send())
    for copy in own:
        copy.wait()

def full_gather(arrays, near_rows, per_seq, cid):
    count = len(arrays)
    anys = pl.BlockSpec(memory_space=pl.ANY)
    def body(*refs):
        it = iter(refs)
        take = lambda n: [next(it) for _ in range(n)]
        ins, near_in, outs, near_out = take(count), take(1), take(count), take(1)
        ssem, rsem, lsem = take(3)
        near = Near(per_seq, near_in, near_out, take(1), take(1), *take(3))
        gather_all(near, ins, outs, ssem, rsem, lsem)
    sem = pltpu.SemaphoreType.DMA
    return pl.pallas_call(
        body, in_specs=[anys] * (count + 1), out_specs=[anys] * (count + 1),
        out_shape=[jax.ShapeDtypeStruct((32,) + a.shape, a.dtype) for a in arrays] + near_shapes([near_rows]),
        scratch_shapes=[sem((10, 4, count)), sem((10, 4, count)), sem((count,))] + near_scratch([near_rows]),
        compiler_params=pltpu.CompilerParams(collective_id=cid, has_side_effects=True),
        name="full_gather")(*arrays, near_rows)

def add_into(target, *terms, rows=16):
    total = target.shape[0]
    step = min(rows, total)
    def one(r, carry):
        part = pl.ds(pl.multiple_of(r * step, step), step)
        value = target[part, :].astype(f32)
        for term in terms:
            value = value + term[part, :].astype(f32)
        target[part, :] = value.astype(target.dtype)
        return carry
    lax.fori_loop(0, total // step, one, 0)

def reduce_all(ins, extra, outs, held, accs, dxs, dys, xrecvs, yrecvs, zrecvs, ssem, rsem, lsem, csend, crecv):
    left, wide, narrow = ins
    left_v, right_v, extra_land = held
    count = 2
    z, y, x, core = place()
    mid = (z == 1) | (z == 2)
    up, down = z < 3, z > 0
    x_dev = index_of(z, y, 1 - x, core)
    y_dev = index_of(z, 1 - y, x, core)
    c_dev = index_of(z, y, x, 1 - core)
    up_dev = index_of(jnp.minimum(z + 1, 3), y, x, core)
    down_dev = index_of(jnp.maximum(z - 1, 0), y, x, core)
    greet([x_dev, y_dev, c_dev, up_dev, down_dev], [None, None, None, up, down])
    items = line_items(z)[::-1]
    mine, xp, yp, dp = y * 2 + x, y * 2 + 1 - x, (1 - y) * 2 + x, (1 - y) * 2 + 1 - x
    pending = []
    rows = left_v.shape[0] // 2
    wide_width, narrow_width = wide.shape[1], narrow.shape[1]
    features = left_v.shape[1] // 2
    own_part, other_part = pl.ds(0, rows), pl.ds(rows, rows)

    def go(make, condition=None):
        if condition is None:
            make().start()
        else:
            pl.when(condition)(lambda: make().start())
        pending.append((make, condition))

    def arrived(kind, a, o, land):
        remote(land, land, ssem.at[kind, 0, a], rsem.at[kind, o, a], c_dev).wait_recv()

    crossing = (
        (left.at[1 - core], left_v.at[other_part]),
        (wide, right_v.at[other_part, pl.ds(0, wide_width)]),
        (narrow, right_v.at[other_part, pl.ds(wide_width, narrow_width)]),
        (extra.at[:, 1 - core], extra_land),
    )
    staying = (
        (left.at[core], left_v.at[own_part]),
        (wide, right_v.at[own_part, pl.ds(0, wide_width)]),
        (narrow, right_v.at[own_part, pl.ds(wide_width, narrow_width)]),
    )

    def cross(n):
        return remote(crossing[n][0], crossing[n][1], csend.at[n], crecv.at[n], c_dev)

    for n in range(4):
        cross(n).start()
    loads = [pltpu.make_async_copy(src, dst, lsem.at[n]) for n, (src, dst) in enumerate(staying)]
    loads += [
        pltpu.make_async_copy(extra.at[pl.ds(o * 4, 4), core], accs[1].at[o], lsem.at[3 + o]) for o in range(4)
    ]
    for copy in loads:
        copy.start()
    for copy in loads:
        copy.wait()
    for n in range(4):
        cross(n).wait_recv()

    chunk = 1024

    def first(i):
        o = items[i]
        for at, begin, total in ((0, 0, wide_width), (features, wide_width, narrow_width)):
            lines = pl.ds(pl.multiple_of(at + o * (features // 4), features // 4), features // 4)

            def some(n, carry):
                columns = pl.ds(pl.multiple_of(begin + n * chunk, chunk), chunk)
                product = lax.dot_general(
                    left_v[:, lines], right_v[:, columns], (((0,), (0,)), ((), ())), preferred_element_type=f32
                )
                accs[0][o, :, :, columns] = product.astype(bf).reshape(4, features // 16, chunk)
                return carry

            lax.fori_loop(0, total // chunk, some, 0)
        for p in range(4):
            accs[1][o, p] = accs[1][o, p] + extra_land[o * 4 + p]
        for a in range(count):
            half = accs[a].shape[2] // 2
            go(lambda a=a, half=half: remote(accs[a].at[o, dp, pl.ds(0, half)], dxs[a].at[o], ssem.at[1, o, a], rsem.at[1, o, a], x_dev))
            go(lambda a=a, half=half: remote(accs[a].at[o, dp, pl.ds(half, half)], dys[a].at[o], ssem.at[2, o, a], rsem.at[2, o, a], y_dev))

    def second(i):
        o = items[i]
        for a in range(count):
            half = accs[a].shape[2] // 2
            arrived(1, a, o, dxs[a].at[o])
            add_into(accs[a].at[o, yp, pl.ds(0, half)], dxs[a].at[o])
            go(lambda a=a: remote(accs[a].at[o, yp], yrecvs[a].at[o], ssem.at[4, o, a], rsem.at[4, o, a], y_dev))
            arrived(2, a, o, dys[a].at[o])
            add_into(accs[a].at[o, xp, pl.ds(half, half)], dys[a].at[o])
            go(lambda a=a: remote(accs[a].at[o, xp], xrecvs[a].at[o], ssem.at[3, o, a], rsem.at[3, o, a], x_dev))

    def third(i):
        o = items[i]
        for a in range(count):
            acc = accs[a].at[o, mine]
            arrived(3, a, o, xrecvs[a].at[o])
            arrived(4, a, o, yrecvs[a].at[o])
            if i < 3:
                @pl.when(mid)
                def _():
                    arrived(5, a, o, zrecvs[a].at[o])
                    add_into(acc, xrecvs[a].at[o], yrecvs[a].at[o], zrecvs[a].at[o])
                @pl.when(jnp.logical_not(mid))
                def _():
                    add_into(acc, xrecvs[a].at[o], yrecvs[a].at[o])
                rising = o > z
                go(lambda o=o, a=a, acc=acc: remote(acc, zrecvs[a].at[o], ssem.at[5, o, a], rsem.at[5, o, a], up_dev), rising)
                def lower(o=o, a=a, acc=acc):
                    slot = jnp.where(z - 1 == o, 4, o)
                    return remote(acc, zrecvs[a].at[slot], ssem.at[5, o, a], rsem.at[5, slot, a], down_dev)
                go(lower, jnp.logical_not(rising))
            else:
                for condition, slots in ((z == 0, (4,)), (z == 3, (3,)), (mid, (None, 4))):
                    @pl.when(condition)
                    def _(slots=slots):
                        terms = [xrecvs[a].at[o], yrecvs[a].at[o]]
                        for slot in slots:
                            slot = o if slot is None else slot
                            arrived(5, a, slot, zrecvs[a].at[slot])
                            terms.append(zrecvs[a].at[slot])
                        rows, step = outs[a].shape[0], 16
                        def one(r, carry):
                            part = pl.ds(pl.multiple_of(r * step, step), step)
                            value = acc[part, :].astype(f32)
                            for term in terms:
                                value = value + term[part, :].astype(f32)
                            outs[a][part, :] = value
                            return carry
                        lax.fori_loop(0, rows // step, one, 0)

    first(0); first(1); second(0); first(2); second(1); third(0); first(3); second(2); third(1); second(3); third(2); third(3)
    for n in range(4):
        cross(n).wait_send()
    for make, condition in pending:
        if condition is None:
            make().wait_send()
        else:
            pl.when(condition)(lambda make=make: make().wait_send())

def full_reduce(left, wide, narrow, extra, cid):
    rows = extra.shape[2]
    columns = wide.shape[1] + narrow.shape[1]
    widths = ((columns, bf), (128, f32))
    anys = pl.BlockSpec(memory_space=pl.ANY)

    def body(*refs):
        it = iter(refs)
        take = lambda n: [next(it) for _ in range(n)]
        ins, extra_in, outs, held = take(3), next(it), take(2), take(3)
        reduce_all(ins, extra_in, outs, held, *[take(2) for _ in range(6)], *it)

    sem = pltpu.SemaphoreType.DMA
    tokens = left.shape[1]
    scratch = [
        pltpu.VMEM((2 * tokens, left.shape[2]), bf),
        pltpu.VMEM((2 * tokens, columns), bf),
        pltpu.VMEM((16, rows, 128), f32),
    ]
    for lead, cut in (((4, 4), 1), ((4,), 2), ((4,), 2), ((4,), 1), ((4,), 1), ((5,), 1)):
        scratch += [pltpu.VMEM(lead + (rows // cut, width), dtype) for width, dtype in widths]
    return pl.pallas_call(
        body, in_specs=[anys] * 4, out_specs=[pl.BlockSpec(memory_space=pltpu.VMEM)] * 2,
        out_shape=[jax.ShapeDtypeStruct((rows, width), f32) for width, dtype in widths],
        scratch_shapes=scratch + [sem((6, 5, 2)), sem((6, 5, 2)), sem((7,)), sem((4,)), sem((4,))],
        compiler_params=pltpu.CompilerParams(collective_id=cid, has_side_effects=True, vmem_limit_bytes=60 * 2**20),
        name="full_reduce")(left, wide, narrow, extra)
def nt(left, right):
    return lax.dot_general(left, right, (((1,), (1,)), ((), ())), preferred_element_type=f32)


def tn(left, right):
    return lax.dot_general(left, right, (((0,), (0,)), ((), ())), preferred_element_type=f32)


def nn(left, right):
    return lax.dot_general(left, right, (((1,), (0,)), ((), ())), preferred_element_type=f32)


def expert_body(shard, width, half, block, cut, *refs):
    it = iter(refs)
    take = lambda n: [next(it) for _ in range(n)]
    own, side, near, beyond = [take(1) for _ in range(4)]
    c_all = next(it)
    x_weights, corner_weights, own_weights = take(3), take(3), take(3)
    x_all, mix, gx, gx_sum, gs_sum, y_land, z_land = take(7)
    core_land = take(2)
    grad_sum = take(2)
    x_land = next(it)
    core_weights = take(3)
    xv, cv, sv, wv, acc, hid_s, gate_s, up_s, gst, gs_y, gs_z, ostage, prev = take(13)
    gsend, grecv, lsem, rsend, rrecv, csend, crecv, xsend, xrecv = take(9)
    wsem, insem, osem, psem, dsem, hsem, tsem, wsend, wrecv = take(9)
    hidden = 2 * half
    tile = 2 * shard
    cuts = width // cut
    tiles = 4
    z, y, x, core = place()
    mid = (z == 1) | (z == 2)
    up, down = z < 3, z > 0
    x_dev = index_of(z, y, 1 - x, core)
    y_dev = index_of(z, 1 - y, x, core)
    c_dev = index_of(z, y, x, 1 - core)
    up_dev = index_of(jnp.minimum(z + 1, 3), y, x, core)
    down_dev = index_of(jnp.maximum(z - 1, 0), y, x, core)
    chip = (z * 2 + y) * 2 + x
    experts = ((z * 2 + y) * 2 + 1 - x, chip)
    lane = lax.broadcasted_iota(jnp.int32, (1, 128), 1)
    items = line_items(z)

    def nearest(k):
        return jnp.where(k == 0, items[0], jnp.where(k == 1, items[1], jnp.where(k == 2, items[2], items[3])))

    def farthest(k):
        return nearest(3 - k)

    landings = (x_all,)
    marks = pl.ds(width, 128)
    ends = jnp.logical_not(mid)

    def part_of(r):
        return pl.ds(pl.multiple_of(r * shard, shard), shard)

    def hop(kind, a, o, src, device):
        return remote(src, landings[a].at[o * 2 + y], gsend.at[kind, o, a], grecv.at[kind, o, a], device)

    def column(k, a):
        return (own[a], near[a])[k] if k < 2 else landings[a].at[items[k] * 2 + y]

    def outwards(k, act):
        for a in range(1):
            src = beyond[a] if k == 2 else column(k, a)
            pl.when(z == 1)(lambda a=a, src=src: act(hop(1, a, items[k], src, down_dev)))
            pl.when(z == 2)(lambda a=a, src=src: act(hop(0, a, items[k], src, up_dev)))

    def over(act):
        for a in range(1):
            pl.when(z == 1)(lambda a=a: act(hop(0, a, items[1], near[a], up_dev)))
            pl.when(z == 2)(lambda a=a: act(hop(1, a, items[1], near[a], down_dev)))

    def sideways(k, act):
        for a in range(1):
            if k == 2:
                pl.when(mid)(lambda a=a: act(hop(2, a, items[k], beyond[a], y_dev)))
                pl.when(ends)(lambda a=a: act(hop(2, a, items[k], column(k, a), y_dev)))
            else:
                act(hop(2, a, items[k], column(k, a), y_dev))

    def column_landed(k, condition):
        o = items[k]
        for a in range(1):
            land = landings[a].at[o * 2 + y]
            pl.when(condition & (o < z))(lambda a=a, land=land: hop(0, a, o, land, y_dev).wait_recv())
            pl.when(condition & (o > z))(lambda a=a, land=land: hop(1, a, o, land, y_dev).wait_recv())

    shares_over = [
        (
            pltpu.make_async_copy(
                block[0].at[pl.ds(0, 16), marks], x_all.at[slot, pl.ds(0, 16), marks], lsem.at[n]
            ),
            condition,
        )
        for n, (block, slot, condition) in enumerate(
            (
                (own, z * 2 + y, None),
                (side, z * 2 + 1 - y, None),
                (near, items[1] * 2 + y, None),
                (beyond, items[2] * 2 + y, mid),
            )
        )
    ]

    def shares(act):
        for copy, condition in shares_over:
            if condition is None:
                act(copy)
            else:
                pl.when(condition)(lambda copy=copy: act(copy))

    def gather_landed(o):
        for a in range(1):
            land = landings[a].at[o * 2 + 1 - y]
            remote(land, land, gsend.at[2, o, a], grecv.at[2, o, a], y_dev).wait_recv()

    def gather_sent():
        over(lambda copy: copy.wait_send())
        for k in (2, 3):
            outwards(k, lambda copy: copy.wait_send())
        for k in (1, 2, 3):
            sideways(k, lambda copy: copy.wait_send())

    def lines(block_index):
        return pl.ds(pl.multiple_of(block_index * shard, shard), shard)

    def y_copies(o):
        other = o * 2 + 1 - y
        return [
            remote(gx.at[lines(other)], y_land.at[o], rsend.at[0, o, 0], rrecv.at[0, o, 0], y_dev),
            remote(gst.at[other], gs_y.at[o], rsend.at[0, o, 1], rrecv.at[0, o, 1], y_dev),
        ]

    def z_copies(o, slot, device):
        own = o * 2 + y
        return [
            remote(gx.at[lines(own)], z_land.at[slot], rsend.at[1, o, 0], rrecv.at[1, slot, 0], device),
            remote(gst.at[own], gs_z.at[slot], rsend.at[1, o, 1], rrecv.at[1, slot, 1], device),
        ]

    def z_go(o, act):
        rising = o > z
        slot = jnp.where(z - 1 == o, 4, o)

        @pl.when(rising)
        def _():
            for copy in z_copies(o, o, up_dev):
                act(copy)

        @pl.when(jnp.logical_not(rising))
        def _():
            for copy in z_copies(o, slot, down_dev):
                act(copy)

    wide = width // 2

    def halves(hbm, vmem, slot, out=False):
        copies = []
        for h in range(2):
            far, near = hbm.at[:, pl.ds(h * wide, wide)], vmem.at[pl.ds(h * shard, shard)]
            if out:
                copies.append(pltpu.make_async_copy(near, far, tsem.at[slot, h]))
            else:
                copies.append(pltpu.make_async_copy(far, near, tsem.at[slot, h]))
        return copies

    def z_wait(slot):
        for copy in z_copies(z, slot, y_dev):
            copy.wait_recv()

    def add_up(terms):
        def some(r, carry):
            part = pl.ds(pl.multiple_of(r * 32, 32), 32)
            value = hid_s[part, :].astype(f32)
            for term in terms:
                value = value + term[part, :].astype(f32)
            hid_s[part, :] = value.astype(bf)
            return carry

        lax.fori_loop(0, tile // 32, some, 0)

    def pump(o, final):
        own = o * 2 + y
        load = halves(gx.at[lines(own)], hid_s, 0)
        for copy in load:
            copy.start()
        for copy in y_copies(o):
            copy.wait_recv()
        load_y = halves(y_land.at[o], gate_s, 1)
        for copy in load_y:
            copy.start()
        slot = jnp.where(z == 0, 4, o) if final else o

        def with_z():
            z_wait(slot)
            load_z = halves(z_land.at[slot], up_s, 2)
            for copy in load_z:
                copy.start()
            for copy in load + load_y + load_z:
                copy.wait()
            add_up([gate_s, up_s])
            gst[own] = gst[own] + gs_y[o] + gs_z[slot]

        if final:
            with_z()

            @pl.when(mid)
            def _():
                z_wait(4)
                load_z = halves(z_land.at[4], up_s, 2)
                for copy in load_z:
                    copy.start()
                for copy in load_z:
                    copy.wait()
                add_up([up_s])
                gst[own] = gst[own] + gs_z[4]

            store = halves(gx_sum, hid_s, 0, True)
            store.append(pltpu.make_async_copy(gst.at[own], gs_sum, tsem.at[1, 0]))
            for copy in store:
                copy.start()
            for copy in store:
                copy.wait()
        else:
            pl.when(mid)(with_z)

            @pl.when(jnp.logical_not(mid))
            def _():
                for copy in load + load_y:
                    copy.wait()
                add_up([gate_s])
                gst[own] = gst[own] + gs_y[o]

            store = halves(gx.at[lines(own)], hid_s, 0, True)
            for copy in store:
                copy.start()
            for copy in store:
                copy.wait()
            z_go(o, lambda copy: copy.start())

    tall = shard
    per_half = (half // tall) * (width // cut)
    pieces = 3 * per_half

    def piece(q):
        i, rest = lax.div(q, per_half), lax.rem(q, per_half)
        r, c = lax.div(rest, width // cut), lax.rem(rest, width // cut)
        return i, pl.multiple_of(r * tall, tall), pl.ds(pl.multiple_of(c * cut, cut), cut)

    slots = 8

    def eighth(ref, slot):
        low = pl.multiple_of(lax.rem(slot, 2) * tall, tall)
        return ref.at[lax.div(slot, 4), lax.rem(lax.div(slot, 2), 2), pl.ds(low, tall)]

    def stage(slot):
        return eighth(ostage, slot)

    def held(slot):
        return eighth(prev, slot)

    def flush(number):
        def across(q, slot):
            i, r, c = piece(q)
            land = core_land[number].at[i, pl.ds(r, tall), c]
            return remote(stage(slot), land, csend.at[number, slot], crecv.at[number], c_dev)

        def give(q, carry):
            slot = lax.rem(q, slots)
            pl.when(q >= slots)(lambda: across(q - slots, slot).wait_send())
            i, r, c = piece(q)
            stage(slot)[...] = acc[i, pl.ds(pl.multiple_of(half + r, tall), tall), c].astype(bf)
            across(q, slot).start()
            return carry

        lax.fori_loop(0, pieces, give, 0)

        def given(q, carry):
            across(q, lax.rem(q, slots)).wait_send()
            return carry

        lax.fori_loop(pieces - slots, pieces, given, 0)
        remote(core_land[number], core_land[number], csend.at[number, 0], crecv.at[number], c_dev).wait_recv()

        def bring(q, slot):
            i, r, c = piece(q)
            return pltpu.make_async_copy(core_land[number].at[i, pl.ds(r, tall), c], held(slot), hsem.at[slot])

        def store(q, slot):
            i, r, c = piece(q)
            return pltpu.make_async_copy(stage(slot), grad_sum[number].at[i, pl.ds(r, tall), c], dsem.at[slot])

        for q in range(slots - 1):
            bring(q, q).start()

        def keep(q, carry):
            slot = lax.rem(q, slots)
            coming = q + slots - 1
            pl.when(coming < pieces)(lambda: bring(coming, lax.rem(coming, slots)).start())
            pl.when(q >= slots)(lambda: store(q - slots, slot).wait())
            bring(q, slot).wait()
            i, r, c = piece(q)
            stage(slot)[...] = (acc[i, pl.ds(r, tall), c] + held(slot)[...].astype(f32)).astype(bf)
            store(q, slot).start()
            return carry

        lax.fori_loop(0, pieces, keep, 0)

        def kept(q, carry):
            store(q, lax.rem(q, slots)).wait()
            return carry

        lax.fori_loop(pieces - slots, pieces, kept, 0)

    def x_copy():
        return remote(grad_sum[0], x_land, xsend, xrecv, x_dev)

    def c_loads(o, slot):
        return [
            pltpu.make_async_copy(c_all.at[o * 2 + r], cv.at[slot, pl.ds(r * shard, shard)], insem.at[1, r, slot])
            for r in range(2)
        ]

    def x_load(k, slot, act):
        for n in range(4):
            o = items[n]

            def bring(column, other):
                for r, src in ((y, column[0]), (1 - y, other[0])):
                    for which, target, part in ((0, xv, pl.ds(0, width)), (2, sv, marks)):
                        act(
                            pltpu.make_async_copy(
                                src.at[:, part], target.at[slot, part_of(r)], insem.at[which, r, slot]
                            )
                        )

            landed = [ref.at[o * 2 + y] for ref in landings]
            other = side if n == 0 else [ref.at[o * 2 + 1 - y] for ref in landings]
            if n < 2:
                pl.when(k == n)(lambda n=n, other=other: bring((own, near)[n], other))
            elif n == 2:
                pl.when((k == n) & mid)(lambda other=other: bring(beyond, other))
                pl.when((k == n) & ends)(lambda landed=landed, other=other: bring(landed, other))
            else:
                pl.when(k == n)(lambda landed=landed, other=other: bring(landed, other))

    def start(copy):
        copy.start()

    def wait(copy):
        copy.wait()

    def spot(o, n):
        return pl.ds(pl.multiple_of(o * tile, tile), tile), pl.ds(pl.multiple_of(n * cut, cut), cut)

    def outgoing(o, n, slot):
        r, c = spot(o, n)
        return [
            pltpu.make_async_copy(ostage.at[slot, i], ref.at[r, c], osem.at[i, slot])
            for i, ref in enumerate((mix, gx))
        ]

    def earlier(o, n, slot):
        r, c = spot(o, n)
        return [
            pltpu.make_async_copy(ref.at[r, c], prev.at[slot, i], psem.at[i, slot])
            for i, ref in enumerate((mix, gx))
        ]

    def weight_loads(number):
        sources = list(zip(*((x_weights, corner_weights), (own_weights, core_weights))[number]))
        return [
            pltpu.make_async_copy(src, wv.at[i, pl.ds(h * half, half)], wsem.at[i, h])
            for i, pair in enumerate(sources)
            for h, src in enumerate(pair)
        ]

    def weights_across():
        return [remote(own_weights[i], core_weights[i], wsend.at[i], wrecv.at[i], c_dev) for i in range(3)]

    def run_tile(number, o, slot):
        if number:
            for copy in earlier(o, 0, 0):
                copy.start()
        pick = (lane == experts[number]).astype(f32)
        halves_of = pick + (lane == experts[number] + gst.shape[1]).astype(f32)
        share = jnp.sum(sv[slot].astype(f32) * halves_of, axis=1, keepdims=True)

        def hidden_block(j, dots):
            part = pl.ds(pl.multiple_of(j * block, block), block)
            rows_in, cots = xv[slot], cv[slot]
            gate_pre = nt(rows_in, wv[0, part, :])
            up_pre = nt(rows_in, wv[1, part, :])
            grad_raw = nt(cots, wv[2, part, :])
            sig = jax.nn.sigmoid(gate_pre)
            silu = gate_pre * sig
            low = (silu * up_pre).astype(bf).astype(f32)
            dots = dots + jnp.sum(low * grad_raw, axis=1, keepdims=True)
            grad_hid = grad_raw * share
            grad_gate = (grad_hid * up_pre * sig * (1.0 + gate_pre * (1.0 - sig))).astype(bf)
            grad_up = (grad_hid * silu).astype(bf)
            shared = (low * share).astype(bf)
            hid_s[:, part] = shared
            gate_s[:, part] = grad_gate
            up_s[:, part] = grad_up
            acc[0, part, :] += tn(grad_gate, rows_in)
            acc[1, part, :] += tn(grad_up, rows_in)
            acc[2, part, :] += tn(shared, cots)
            return dots

        dots = lax.fori_loop(0, hidden // block, hidden_block, jnp.zeros((tile, 1), f32))
        both = dots * pick
        for r in range(2):
            turned = jnp.transpose(both[r * shard : (r + 1) * shard, :])[: gst.shape[1], :]
            gst[o * 2 + r] = gst[o * 2 + r] + turned if number else turned

        def column_block(n, inner):
            now = lax.rem(n, 2)
            columns = pl.ds(pl.multiple_of(n * cut, cut), cut)

            @pl.when(n >= 2)
            def _():
                for copy in outgoing(o, n - 2, now):
                    copy.wait()

            out = nn(hid_s[...], wv[2, :, columns])
            back = nn(gate_s[...], wv[0, :, columns]) + nn(up_s[...], wv[1, :, columns])
            if number:
                @pl.when(n + 1 < cuts)
                def _():
                    for copy in earlier(o, n + 1, 1 - now):
                        copy.start()

                for copy in earlier(o, n, now):
                    copy.wait()
                out = out + prev[now, 0].astype(f32)
                back = back + prev[now, 1].astype(f32)
            ostage[now, 0] = out.astype(bf)
            ostage[now, 1] = back.astype(bf)
            for copy in outgoing(o, n, now):
                copy.start()
            return inner

        lax.fori_loop(0, cuts, column_block, 0)
        for n in (cuts - 2, cuts - 1):
            for copy in outgoing(o, n, n % 2):
                copy.wait()

    greet([x_dev, y_dev, c_dev, up_dev, down_dev], [None, None, None, up, down])
    across = weights_across()
    outwards(2, start)
    over(start)
    sideways(1, start)
    loads = weight_loads(0) + c_loads(items[0], 0)
    for copy in loads:
        copy.start()
    x_load(0, 0, start)
    shares(start)
    acc[...] = jnp.zeros_like(acc)
    for copy in loads[:6]:
        copy.wait()
    for copy in across:
        copy.start()

    def first_pass(t, carry):
        slot = lax.rem(t, 2)
        o = nearest(t)

        @pl.when(t == 1)
        def _():
            column_landed(3, mid)
            outwards(3, start)
            column_landed(2, ends)
            sideways(2, start)

        @pl.when(t == 2)
        def _():
            column_landed(3, ends)
            sideways(3, start)

        @pl.when(t + 1 < tiles)
        def _():
            for copy in c_loads(nearest(t + 1), 1 - slot):
                copy.start()

        @pl.when(t > 0)
        def _():
            gather_landed(o)
            x_load(t, slot, start)

        x_load(t, slot, wait)
        for copy in c_loads(o, slot):
            copy.wait()
        run_tile(0, o, slot)
        return carry

    lax.fori_loop(0, tiles, first_pass, 0)
    for copy in across:
        copy.wait()
    loads = weight_loads(1)
    for copy in loads + c_loads(items[3], 0):
        copy.start()
    x_load(3, 0, start)
    shares(wait)
    flush(0)
    x_copy().start()
    acc[...] = jnp.zeros_like(acc)
    for copy in loads:
        copy.wait()

    def second_pass(t, carry):
        slot = lax.rem(t, 2)
        o = farthest(t)

        @pl.when(t + 1 < tiles)
        def _():
            for copy in c_loads(farthest(t + 1), 1 - slot):
                copy.start()
            x_load(2 - t, 1 - slot, start)

        for copy in c_loads(o, slot):
            copy.wait()
        x_load(3 - t, slot, wait)
        run_tile(1, o, slot)
        for copy in y_copies(o):
            copy.start()
        k = jnp.where(mid, t - 2, t - 1)
        pl.when(k >= 0)(lambda: pump(farthest(k), False))
        return carry

    lax.fori_loop(0, tiles, second_pass, 0)
    pl.when(mid)(lambda: pump(items[1], False))
    flush(1)
    pump(z, True)
    for k in range(4):
        for copy in y_copies(items[k]):
            copy.wait_send()
        if k:
            z_go(items[k], lambda copy: copy.wait_send())
    gather_sent()
    x_copy().wait()


def expert_pass(rows_in, c_all, x_weights, corner_weights, own_weights, gs_rows, cid):
    blocks, shard, width = c_all.shape
    rows = blocks * shard
    half = own_weights[0].shape[0]
    hidden = 2 * half
    tile, block, cut = 2 * shard, half, 512
    anys = pl.BlockSpec(memory_space=pl.ANY)
    sem = pltpu.SemaphoreType.DMA
    flat = list(x_weights) + list(corner_weights) + list(own_weights)
    shaped = jax.ShapeDtypeStruct
    half_grads = shaped((3, half, width), bf)
    shapes = [
        shaped((blocks, shard, width + 128), bf),
        shaped((rows, width), bf),
        shaped((rows, width), bf),
        shaped((shard, width), bf),
        shaped((gs_rows, shard), f32),
        shaped((4, shard, width), bf),
        shaped((5, shard, width), bf),
    ] + [half_grads] * 5 + [shaped((half, width), bf)] * 3
    return pl.pallas_call(
        functools.partial(expert_body, shard, width, half, block, cut),
        in_specs=[anys] * (5 + len(flat)),
        out_specs=[anys] * len(shapes),
        out_shape=shapes,
        scratch_shapes=[
            pltpu.VMEM((2, tile, width), bf),
            pltpu.VMEM((2, tile, width), bf),
            pltpu.VMEM((2, tile, 128), bf),
            pltpu.VMEM((3, hidden, width), bf),
            pltpu.VMEM((3, hidden, width), f32),
            pltpu.VMEM((tile, hidden), bf),
            pltpu.VMEM((tile, hidden), bf),
            pltpu.VMEM((tile, hidden), bf),
            pltpu.VMEM((blocks, gs_rows, shard), f32),
            pltpu.VMEM((4, gs_rows, shard), f32),
            pltpu.VMEM((5, gs_rows, shard), f32),
            pltpu.VMEM((2, 2, tile, cut), bf),
            pltpu.VMEM((2, 2, tile, cut), bf),
            sem((3, 4, 2)),
            sem((3, 4, 2)),
            sem((8,)),
            sem((2, 5, 2)),
            sem((2, 5, 2)),
            sem((2, 8)),
            sem((2,)),
            sem,
            sem,
            sem((3, 2)),
            sem((3, 2, 2)),
            sem((2, 2)),
            sem((2, 2)),
            sem((8,)),
            sem((8,)),
            sem((3, 2)),
            sem((3,)),
            sem((3,)),
        ],
        compiler_params=pltpu.CompilerParams(
            vmem_limit_bytes=63 * 2**20, collective_id=cid, has_side_effects=True
        ),
        name="expert_pass",
    )(*rows_in, c_all, *flat)
def attend_body(scale, q_ref, k_ref, v_ref, bias_ref, out_ref, lse_ref, top_ref):
    head = pl.program_id(0)
    scores = nt(q_ref[...], k_ref[...]) * scale + bias_ref[...]
    top = jnp.max(scores, axis=1, keepdims=True)
    parts = jnp.exp(scores - top)
    total = jnp.sum(parts, axis=1, keepdims=True)
    probs = (parts * (1.0 / total)).astype(bf)
    out_ref[...] = nn(probs, v_ref[...]).astype(bf)
    lane = lax.broadcasted_iota(jnp.int32, lse_ref.shape, 1)

    @pl.when(head == 0)
    def _():
        lse_ref[...] = jnp.zeros_like(lse_ref)
        top_ref[...] = jnp.zeros_like(top_ref)

    lse_ref[...] = jnp.where(lane == head, top + jnp.log(total), lse_ref[...])
    row = lax.broadcasted_iota(jnp.int32, top_ref.shape, 1)
    top_ref[...] = jnp.where(row == head, jnp.max(top), top_ref[...])


def attend(near_qkv, bias, heads, width, scale):
    rows, keys = bias.shape
    size = width // heads
    middle = keys // rows // 2
    return pl.pallas_call(
        functools.partial(attend_body, scale),
        grid=(heads,),
        in_specs=[
            pl.BlockSpec((rows, size), lambda h: (middle, h)),
            pl.BlockSpec((keys, size), lambda h: (0, heads + h)),
            pl.BlockSpec((keys, size), lambda h: (0, 2 * heads + h)),
            pl.BlockSpec((rows, keys), lambda h: (0, 0)),
        ],
        out_specs=[
            pl.BlockSpec((rows, size), lambda h: (0, h)),
            pl.BlockSpec((rows, 128), lambda h: (0, 0)),
            pl.BlockSpec((8, 128), lambda h: (0, 0)),
        ],
        out_shape=[
            jax.ShapeDtypeStruct((rows, width), bf),
            jax.ShapeDtypeStruct((rows, 128), f32),
            jax.ShapeDtypeStruct((8, 128), f32),
        ],
        compiler_params=pltpu.CompilerParams(vmem_limit_bytes=48 * 2**20),
        name="attend",
    )(near_qkv, near_qkv, near_qkv, bias)


def attend_queries_body(scale, per_seq, heads, *refs):
    it = iter(refs)
    take = lambda n: [next(it) for _ in range(n)]
    q_ref, k_ref, v_ref, g_ref, bias_ref, lse_ref = take(6)
    sent, dq_ref, landed = take(2), next(it), take(2)
    near = Near(per_seq, sent, landed, take(2), take(2), *take(3))
    head = pl.program_id(0)

    @pl.when(head == 0)
    def _():
        greet([near.c_dev, near.previous, near.following], [None, near.before, near.after])
        near.start()

    lane = lax.broadcasted_iota(jnp.int32, lse_ref.shape, 1)
    lse = jnp.sum(jnp.where(lane == head, lse_ref[...], 0.0), axis=1, keepdims=True)
    keys = k_ref[...]
    probs = jnp.exp(nt(q_ref[...], keys) * scale + bias_ref[...] - lse)
    grad_probs = nt(g_ref[...], v_ref[...])
    shift = jnp.sum(probs * grad_probs, axis=1, keepdims=True)
    grad_scores = (probs * (grad_probs - shift)).astype(bf)
    dq_ref[...] = (nn(grad_scores, keys) * scale).astype(bf)
    pl.when(head == heads - 1)(near.finish)


def attend_queries(near_qkv, grads, bias, lse, stats, heads, scale, per_seq, cid):
    rows, keys = bias.shape
    width = grads.shape[1]
    size = width // heads
    middle = keys // rows // 2
    own = pl.BlockSpec((rows, size), lambda h: (0, h))
    anys = pl.BlockSpec(memory_space=pl.ANY)
    return pl.pallas_call(
        functools.partial(attend_queries_body, scale, per_seq, heads),
        grid=(heads,),
        in_specs=[
            pl.BlockSpec((rows, size), lambda h: (middle, h)),
            pl.BlockSpec((keys, size), lambda h: (0, heads + h)),
            pl.BlockSpec((keys, size), lambda h: (0, 2 * heads + h)),
            own,
            pl.BlockSpec((rows, keys), lambda h: (0, 0)),
            pl.BlockSpec((rows, 128), lambda h: (0, 0)),
            anys,
            anys,
        ],
        out_specs=[own, anys, anys],
        out_shape=[jax.ShapeDtypeStruct((rows, width), bf)] + near_shapes([grads, stats]),
        scratch_shapes=near_scratch([grads, stats]),
        compiler_params=pltpu.CompilerParams(
            vmem_limit_bytes=48 * 2**20, collective_id=cid, has_side_effects=True
        ),
        name="attend_queries",
    )(near_qkv, near_qkv, near_qkv, grads, bias, lse, grads, stats)


def attend_keys_body(scale, q_ref, k_ref, v_ref, g_ref, bias_ref, stats_ref, dk_ref, dv_ref):
    head = pl.program_id(0)
    heads = stats_ref.shape[1] // 2
    row = lax.broadcasted_iota(jnp.int32, stats_ref.shape[1:], 0)

    def line(at):
        parts = [
            jnp.sum(jnp.where(row == at, stats_ref[j], 0.0), axis=0, keepdims=True)
            for j in range(stats_ref.shape[0])
        ]
        return jnp.concatenate(parts, axis=1)

    queries, grads = q_ref[...], g_ref[...]
    probs = jnp.exp(nt(k_ref[...], queries) * scale + bias_ref[...] - line(head))
    dv_ref[...] = nn(probs.astype(bf), grads).astype(bf)
    grad_probs = nt(v_ref[...], grads)
    grad_scores = (probs * (grad_probs - line(heads + head))).astype(bf)
    dk_ref[...] = (nn(grad_scores, queries) * scale).astype(bf)


def attend_keys(near_qkv, near_grads, bias, near_stats, heads, scale):
    rows, keys = bias.shape
    width = near_grads.shape[1]
    size = width // heads
    middle = keys // rows // 2
    own = pl.BlockSpec((rows, size), lambda h: (0, h))
    return pl.pallas_call(
        functools.partial(attend_keys_body, scale),
        grid=(heads,),
        in_specs=[
            pl.BlockSpec((keys, size), lambda h: (0, h)),
            pl.BlockSpec((rows, size), lambda h: (middle, heads + h)),
            pl.BlockSpec((rows, size), lambda h: (middle, 2 * heads + h)),
            pl.BlockSpec((keys, size), lambda h: (0, h)),
            pl.BlockSpec((rows, keys), lambda h: (0, 0)),
            pl.BlockSpec(near_stats.shape, lambda h: (0, 0, 0)),
        ],
        out_specs=[own, own],
        out_shape=[jax.ShapeDtypeStruct((rows, width), bf)] * 2,
        compiler_params=pltpu.CompilerParams(vmem_limit_bytes=48 * 2**20),
        name="attend_keys",
    )(near_qkv, near_qkv, near_qkv, near_grads, bias, near_stats)


def rows_body(own, side, near, beyond, ssem, rsem):
    z, y, x, core = place()
    mid = (z == 1) | (z == 2)
    y_dev = index_of(z, 1 - y, x, core)
    near_dev = index_of(z + 1 - 2 * lax.rem(z, 2), y, x, core)
    beyond_dev = index_of(jnp.where(mid, 3 - z, z), y, x, core)
    greet([y_dev, near_dev, beyond_dev], [None, None, mid])
    copies = [
        (remote(own, target, ssem.at[n], rsem.at[n], device), condition)
        for n, (target, device, condition) in enumerate(
            ((beyond, beyond_dev, mid), (side, y_dev, None), (near, near_dev, None))
        )
    ]
    for act in (lambda copy: copy.start(), lambda copy: copy.wait()):
        for copy, condition in copies:
            if condition is None:
                act(copy)
            else:
                pl.when(condition)(lambda copy=copy, act=act: act(copy))


def rows_around(own, cid):
    anys = pl.BlockSpec(memory_space=pl.ANY)
    sem = pltpu.SemaphoreType.DMA((3,))
    return pl.pallas_call(
        rows_body,
        in_specs=[anys],
        out_specs=[anys] * 3,
        out_shape=[jax.ShapeDtypeStruct(own.shape, own.dtype)] * 3,
        scratch_shapes=[sem, sem],
        compiler_params=pltpu.CompilerParams(collective_id=cid, has_side_effects=True),
        name="rows_around",
    )(own)


def dense_layer(
    tokens,
    w_query,
    w_key,
    w_value,
    w_out,
    w_router,
    gain_attn,
    gain_moe,
    w_gate,
    w_up,
    w_down,
    routes,
    doc_lengths,
    clip_limit,
    cotangent,
):
    devices = lax.axis_size("fsdp")
    device = lax.axis_index("fsdp")
    tok_rows = tokens.shape[0]
    model_width = tokens.shape[1]
    weight_rows = w_query.shape[0]
    head_count = clip_limit.shape[0]
    head_size = model_width // head_count
    experts = w_router.shape[1]
    seq_len = devices * tok_rows // doc_lengths.shape[0]
    score_scale = head_size ** (-0.5)
    wide_width = 3 * model_width
    extra = jnp.pad(
        jnp.concatenate((w_router, gain_attn[:, None], gain_moe[:, None]), axis=1),
        ((0, 0), (0, 128 - experts - 2)),
    )
    wide_own = jnp.concatenate((w_query, w_key, w_value, extra), axis=1)
    per_seq = devices // (2 * doc_lengths.shape[0])
    wide_full, out_full, near_tokens = full_gather([wide_own, w_out], tokens, per_seq, 2)
    wide_full = wide_full.reshape(model_width, wide_width + 128)
    out_full = out_full.reshape(model_width, model_width)
    later = lax.optimization_barrier((out_full, cotangent, w_gate, w_up, w_down))
    out_full, cot_own, gate_own, up_own, down_own = later
    planes = [
        [index_of(z, y, x, core) for z in range(4) for y in range(2)] for x in range(2) for core in range(2)
    ]
    c_all = lax.all_gather(cot_own, "fsdp", axis_index_groups=planes)
    x_weights = [swapped(w, "fsdp", 1) for w in (gate_own, up_own, down_own)]
    router_full = wide_full[:, wide_width : wide_width + experts]
    gain_one = wide_full[:, wide_width + experts]
    gain_two = wide_full[:, wide_width + experts + 1]
    token_values = tokens.astype(f32)
    scale_one = rms_scale(token_values)
    attn_gain = gain_one.astype(f32)
    reach_count = (HALF - 2) // tok_rows + 1
    slots = 2 * reach_count + 1
    key_count = slots * tok_rows
    row_index = jnp.arange(tok_rows, dtype=jnp.int32)
    query_places = device * tok_rows + row_index
    key_places = (device - reach_count) * tok_rows + jnp.arange(key_count, dtype=jnp.int32)
    query_docs = document_of(query_places, doc_lengths, seq_len)
    key_docs = document_of(key_places, doc_lengths, seq_len)
    near_by = (key_docs >= 0) & (key_places // seq_len == query_places[0] // seq_len)
    visible = (
        (query_docs[:, None] == key_docs[None, :])
        & near_by[None, :]
        & (jnp.abs(query_places[:, None] - key_places[None, :]) < HALF)
    )
    bias = jnp.where(visible, 0.0, masked)
    near_values = near_tokens.reshape(key_count, model_width).astype(f32)
    near_normed = (near_values * rms_scale(near_values) * attn_gain).astype(bf)
    normed_attn = (token_values * scale_one * attn_gain).astype(bf)
    near_qkv = jnp.dot(near_normed, wide_full, preferred_element_type=f32).astype(bf)
    context, log_total, own_top = attend(near_qkv, bias, head_count, model_width, score_scale)
    both_left = jnp.stack((normed_attn, context)).reshape(2, tok_rows, devices // 2, 2, weight_rows)
    by_core = jnp.transpose(both_left, (3, 1, 0, 2, 4)).reshape(2, tok_rows, 2 * model_width // 2)
    attended = token_values + jnp.dot(context, out_full, preferred_element_type=f32)
    scale_two = rms_scale(attended)
    moe_gain = gain_two.astype(f32)
    normed_moe = (attended * scale_two * moe_gain).astype(bf)
    logits = jnp.dot(normed_moe, router_full, preferred_element_type=f32)
    named = jnp.any(routes[:, :, None] == jnp.arange(experts, dtype=jnp.int32)[None, None, :], axis=1)
    chosen = jnp.where(named, logits, masked)
    lifted = jnp.where(named, jnp.exp(logits - jnp.max(chosen, axis=1, keepdims=True)), 0.0)
    gate_share = lifted / jnp.sum(lifted, axis=1, keepdims=True)
    lanes = []
    for values in (gate_share, jnp.broadcast_to(own_top[:1, :head_count], (tok_rows, head_count))):
        most = lax.reduce_precision(values, 8, 7)
        lanes += [most.astype(bf), (values - most).astype(bf)]
    lanes = jnp.concatenate(lanes, axis=1)
    lane_count = lanes.shape[1]
    own_rows = jnp.concatenate((normed_moe, jnp.pad(lanes, ((0, 0), (0, 128 - lane_count)))), axis=1)
    rows_in = [own_rows, *rows_around(own_rows, 4)]
    x_weights = [lax.optimization_barrier((w, rows_in[1]))[0] for w in x_weights]
    corner_weights = [swapped(w, "fsdp", 0) for w in x_weights]
    expert_results = expert_pass(
        rows_in, c_all, x_weights, corner_weights, (gate_own, up_own, down_own), experts, 0
    )
    x_all, mix_part, grad_from_experts, grad_share = [expert_results[i] for i in (0, 1, 3, 4)]
    x_terms, own_sum = expert_results[11], expert_results[10]
    first_lane = model_width + 2 * experts
    tops = x_all[:, 0, first_lane : first_lane + 2 * head_count].astype(f32)
    head_max = jnp.max(tops[:, :head_count] + tops[:, head_count:], axis=0)
    head_max = jnp.maximum(head_max, swapped(head_max, "fsdp", 0))
    head_max = jnp.maximum(head_max, swapped(head_max, "fsdp", 1))
    factor = clip_limit / jnp.maximum(head_max, clip_limit)
    columns = jnp.repeat(jnp.sqrt(factor), head_size)
    clipped_query = (w_query.astype(f32) * columns[None, :]).astype(bf)
    clipped_key = (w_key.astype(f32) * columns[None, :]).astype(bf)
    mixture = lax.psum_scatter(mix_part, "fsdp", axis_index_groups=planes, tiled=True)
    grad_share = jnp.transpose(grad_share)
    grad_mixed = cotangent.astype(f32)
    grad_logits = gate_share * (grad_share - jnp.sum(gate_share * grad_share, axis=1, keepdims=True))
    grad_router_part = jnp.dot(normed_moe.astype(f32).T, grad_logits, precision=highest)
    grad_normed_moe = grad_from_experts.astype(f32) + jnp.dot(
        grad_logits, router_full.astype(f32).T, precision=highest
    )
    grad_from_norm, grad_gain_two = norm_back(grad_normed_moe, attended, scale_two, moe_gain)
    grad_attended = grad_mixed + grad_from_norm
    grad_attended_low = grad_attended.astype(bf)
    grad_context = contract(grad_attended_low, out_full, 1, 1).astype(bf)
    by_head = grad_context.astype(f32) * context.astype(f32)
    shifts = jnp.sum(by_head.reshape(tok_rows, head_count, head_size), axis=2)
    stats = jnp.transpose(jnp.concatenate((log_total[:, :head_count], shifts), axis=1))
    grad_queries, near_grads, near_stats = attend_queries(
        near_qkv, grad_context, bias, log_total, stats, head_count, score_scale, per_seq, 1
    )
    grad_keys, grad_values = attend_keys(
        near_qkv, near_grads.reshape(key_count, model_width), bias, near_stats, head_count, score_scale
    )
    grad_qkv = jnp.concatenate((grad_queries, grad_keys, grad_values), axis=1)
    grad_normed_attn = contract(jnp.pad(grad_qkv, ((0, 0), (0, 128))), wide_full, 1, 1)
    grad_from_first, grad_gain_one = norm_back(grad_normed_attn, token_values, scale_one, attn_gain)
    grad_tokens = grad_attended + grad_from_first
    extra_part = jnp.pad(
        jnp.concatenate((grad_router_part, grad_gain_one[:, None], grad_gain_two[:, None]), axis=1),
        ((0, 0), (0, 128 - experts - 2)),
    )
    owners = (devices // 2, 2, weight_rows)
    grads_sum, extra_sum = full_reduce(
        by_core, grad_qkv, grad_attended_low, extra_part.reshape(owners + (128,)), 3
    )
    mixture, own_sum, x_terms, grads_sum = lax.optimization_barrier(
        (mixture, own_sum, x_terms, grads_sum)
    )
    grad_gate, grad_up, grad_down = [own_sum[i].astype(f32) + x_terms[i].astype(f32) for i in range(3)]
    mixed = (attended + mixture.astype(f32)).astype(bf)
    return (
        mixed,
        grad_tokens,
        grads_sum[:, :model_width],
        grads_sum[:, model_width : 2 * model_width],
        grads_sum[:, 2 * model_width : wide_width],
        grads_sum[:, wide_width:],
        extra_sum[:, :experts],
        extra_sum[:, experts],
        extra_sum[:, experts + 1],
        grad_gate,
        grad_up,
        grad_down,
        clipped_query,
        clipped_key,
    )


def chosen_layer(mesh):
    def layer(*arrays):
        experts, top_count = arrays[5].shape[1], arrays[11].shape[1]
        if mesh.shape["fsdp"] == 32 and 2 * top_count >= experts:
            return dense_layer(*arrays)
        return routed_layer(*arrays)

    return layer


def solution(mesh):
    placed = (
        P("fsdp", None),
        P("fsdp", None),
        P("fsdp", None),
        P("fsdp", None),
        P("fsdp", None),
        P("fsdp", None),
        P("fsdp"),
        P("fsdp"),
        P("fsdp", None),
        P("fsdp", None),
        P("fsdp", None),
        P("fsdp", None),
        P(),
        P(),
        P("fsdp", None),
    )
    return jax.shard_map(
        chosen_layer(mesh),
        mesh=mesh,
        in_specs=placed,
        out_specs=(
            P("fsdp", None),
            P("fsdp", None),
            P("fsdp", None),
            P("fsdp", None),
            P("fsdp", None),
            P("fsdp", None),
            P("fsdp", None),
            P("fsdp"),
            P("fsdp"),
            P("fsdp", None),
            P("fsdp", None),
            P("fsdp", None),
            P("fsdp", None),
            P("fsdp", None),
        ),
        check_vma=False,
    )
```

```python
import functools
from functools import reduce

import jax
import jax.numpy as jnp
from jax import lax
from jax.experimental import pallas as pl
from jax.experimental.pallas import tpu as pltpu
from jax.sharding import PartitionSpec as P

HALF = 512


epsilon = 1e-05
masked = -1e30
highest = lax.Precision.HIGHEST


def passed_along(x, axis, by):
    length = lax.axis_size(axis)
    pairs = [(i, i + by) for i in range(length) if 0 <= i + by < length]
    return lax.ppermute(x, axis, pairs)


def swapped(block, axis, apart):
    count = lax.axis_size(axis)
    route = []
    for low in range(count):
        high = low | 1 << apart
        if high != low and high < count:
            route += [(low, high), (high, low)]
    return lax.ppermute(block, axis, route)


def rms_scale(source):
    return lax.rsqrt(jnp.mean(source * source, axis=-1, keepdims=True) + epsilon)


def norm_back(grad_normed, source, scale_rows, gain):
    unit_rows = source * scale_rows
    grad_unit = grad_normed * gain
    grad_gain = jnp.sum(grad_normed * unit_rows, axis=0)
    grad_source = scale_rows * (
        grad_unit - unit_rows * jnp.mean(grad_unit * unit_rows, axis=-1, keepdims=True)
    )
    return (grad_source, grad_gain)


def document_of(places, doc_lengths, seq_len):
    doc_ends = jnp.cumsum(doc_lengths, axis=1)
    seq_count = doc_lengths.shape[0]
    doc_count = doc_lengths.shape[1]
    sequence = places // seq_len
    within = places % seq_len
    picked = (sequence[:, None] == jnp.arange(seq_count, dtype=jnp.int32)[None, :]).astype(
        jnp.int32
    )
    ends_of = jnp.dot(picked, doc_ends)
    local_doc = jnp.sum((within[:, None] >= ends_of).astype(jnp.int32), axis=1)
    inside = (places >= 0) & (places < seq_count * seq_len)
    return jnp.where(inside, sequence * doc_count + local_doc, -1)


def contract(left, right, left_dim, right_dim):
    return lax.dot_general(
        left, right, (((left_dim,), (right_dim,)), ((), ())), preferred_element_type=jnp.float32
    )


def routed_layer(
    tokens,
    w_query,
    w_key,
    w_value,
    w_out,
    w_router,
    gain_attn,
    gain_moe,
    w_gate,
    w_up,
    w_down,
    routes,
    doc_lengths,
    clip_limit,
    cotangent,
):
    devices = lax.axis_size("fsdp")
    device = lax.axis_index("fsdp")
    tok_rows = tokens.shape[0]
    model_width = tokens.shape[1]
    head_count = clip_limit.shape[0]
    head_size = model_width // head_count
    experts = w_router.shape[1]
    top_count = routes.shape[1]
    seq_len = devices * tok_rows // doc_lengths.shape[0]
    score_scale = head_size ** (-0.5)
    gathered = (
        lax.all_gather(w_query, "fsdp", axis=0, tiled=True),
        lax.all_gather(w_key, "fsdp", axis=0, tiled=True),
        lax.all_gather(w_value, "fsdp", axis=0, tiled=True),
        lax.all_gather(w_out, "fsdp", axis=0, tiled=True),
        lax.all_gather(w_router, "fsdp", axis=0, tiled=True),
        lax.all_gather(gain_attn, "fsdp", axis=0, tiled=True),
        lax.all_gather(gain_moe, "fsdp", axis=0, tiled=True),
    )
    query_full, key_full, value_full, out_full, router_full, gain_one, gain_two = gathered
    token_values = tokens.astype(jnp.float32)
    scale_one = rms_scale(token_values)
    attn_gain = gain_one.astype(jnp.float32)
    normed_attn = (token_values * scale_one * attn_gain).astype(jnp.bfloat16)
    queries = jnp.dot(normed_attn, query_full, preferred_element_type=jnp.float32).astype(
        jnp.bfloat16
    )
    kv_own = jnp.concatenate(
        (
            jnp.dot(normed_attn, key_full, preferred_element_type=jnp.float32),
            jnp.dot(normed_attn, value_full, preferred_element_type=jnp.float32),
        ),
        axis=1,
    ).astype(jnp.bfloat16)
    reach_count = (HALF - 2) // tok_rows + 1
    offsets = list(range(reach_count, 0, -1)) + list(range(-1, -reach_count - 1, -1))
    arrived = [passed_along(kv_own, "fsdp", offset) for offset in offsets]
    kv_rows = jnp.concatenate(arrived[:reach_count] + [kv_own] + arrived[reach_count:], axis=0)
    ordered = offsets[:reach_count] + [0] + offsets[reach_count:]
    row_index = jnp.arange(tok_rows, dtype=jnp.int32)
    query_places = device * tok_rows + row_index
    key_places = jnp.concatenate([(device - offset) * tok_rows + row_index for offset in ordered])
    query_docs = document_of(query_places, doc_lengths, seq_len)
    key_docs = document_of(key_places, doc_lengths, seq_len)
    visible = (
        (query_docs[:, None] == key_docs[None, :])
        & (key_docs[None, :] >= 0)
        & (jnp.abs(query_places[:, None] - key_places[None, :]) < HALF)
    )
    key_count = kv_rows.shape[0]
    query_heads = queries.reshape(tok_rows, head_count, head_size)
    key_heads = kv_rows[:, :model_width].reshape(key_count, head_count, head_size)
    value_heads = kv_rows[:, model_width:].reshape(key_count, head_count, head_size)

    def scores_of():
        raw_scores = (
            jnp.einsum("qhd,khd->hqk", query_heads, key_heads, preferred_element_type=jnp.float32)
            * score_scale
        )
        return jnp.where(visible[None], raw_scores, masked)

    scores = scores_of()
    head_top = jnp.max(scores, axis=2, keepdims=True)
    exponents = jnp.exp(scores - head_top)
    totals = jnp.sum(exponents, axis=2, keepdims=True)
    log_total = head_top + jnp.log(totals)
    probs_low = (exponents / totals).astype(jnp.bfloat16)
    head_max = lax.pmax(jnp.max(head_top, axis=(1, 2)), "fsdp")
    context = (
        jnp.einsum("hqk,khd->qhd", probs_low, value_heads, preferred_element_type=jnp.float32)
        .reshape(tok_rows, model_width)
        .astype(jnp.bfloat16)
    )
    attended = token_values + jnp.dot(context, out_full, preferred_element_type=jnp.float32)
    factor = clip_limit / jnp.maximum(head_max, clip_limit)
    columns = jnp.repeat(jnp.sqrt(factor), head_size)
    clipped_query = (w_query.astype(jnp.float32) * columns[None, :]).astype(jnp.bfloat16)
    clipped_key = (w_key.astype(jnp.float32) * columns[None, :]).astype(jnp.bfloat16)
    scale_two = rms_scale(attended)
    moe_gain = gain_two.astype(jnp.float32)
    normed_moe = (attended * scale_two * moe_gain).astype(jnp.bfloat16)
    logits = jnp.dot(normed_moe, router_full, preferred_element_type=jnp.float32)
    matches = routes[:, :, None] == jnp.arange(experts, dtype=jnp.int32)[None, None, :]
    chosen = jnp.sum(jnp.where(matches, logits[:, None, :], 0.0), axis=2)
    gate_share = jax.nn.softmax(chosen, axis=1)
    pair_count = tok_rows * top_count
    capacity = 3 * tok_rows * top_count // devices
    half_cap = capacity // 2
    flat_route = routes.reshape(pair_count)
    one_hot = (flat_route[:, None] == jnp.arange(experts, dtype=jnp.int32)[None, :]).astype(
        jnp.int32
    )
    slot_rank = jnp.sum(jnp.cumsum(one_hot, axis=0) * one_hot, axis=1) - 1
    target_device = 2 * flat_route + slot_rank // half_cap
    target_slot = slot_rank % half_cap
    flat_slot = target_device * half_cap + target_slot
    slot_total = devices * half_cap
    outgoing = (
        jnp.zeros((slot_total, model_width), jnp.bfloat16)
        .at[flat_slot]
        .set(jnp.repeat(normed_moe, top_count, axis=0))
    )
    live_out = jnp.zeros((slot_total,), jnp.int32).at[flat_slot].set(1)
    incoming, live_in = (
        lax.all_to_all(outgoing, "fsdp", split_axis=0, concat_axis=0, tiled=True),
        lax.all_to_all(live_out, "fsdp", split_axis=0, concat_axis=0, tiled=True),
    )
    packed_order = jnp.cumsum(live_in) - 1
    packed_index = jnp.where(live_in > 0, packed_order, slot_total)
    back_index = jnp.clip(packed_order, 0, slot_total - 1)
    live_count = jnp.sum(live_in)
    tile_rows = 128
    tile_count = (live_count + tile_rows - 1) // tile_rows
    packed_rows = (
        jnp.zeros((slot_total + 1, model_width), jnp.bfloat16)
        .at[packed_index]
        .set(incoming)[:slot_total]
    )
    partner_half = swapped((w_gate, w_up, w_down), "fsdp", 0)
    lower = device % 2 == 0

    def joined(own_half, other_half):
        return jnp.where(
            lower, jnp.concatenate((own_half, other_half)), jnp.concatenate((other_half, own_half))
        )

    gate_full = joined(w_gate, partner_half[0])
    up_full = joined(w_up, partner_half[1])
    down_full = joined(w_down, partner_half[2])
    hidden_units = gate_full.shape[0]

    def forward_tile(tile_step, loop_state):
        out_rows, gate_keep, up_keep = loop_state
        tile_start = tile_step * tile_rows
        tile_input = lax.dynamic_slice_in_dim(packed_rows, tile_start, tile_rows, 0)
        gate_pre = contract(tile_input, gate_full, 1, 1)
        up_pre = contract(tile_input, up_full, 1, 1)
        hidden = (jax.nn.silu(gate_pre) * up_pre).astype(jnp.bfloat16)
        result = jnp.dot(hidden, down_full, preferred_element_type=jnp.float32).astype(jnp.bfloat16)
        return (
            lax.dynamic_update_slice_in_dim(out_rows, result, tile_start, 0),
            lax.dynamic_update_slice_in_dim(gate_keep, gate_pre, tile_start, 0),
            lax.dynamic_update_slice_in_dim(up_keep, up_pre, tile_start, 0),
        )

    start_state = (
        jnp.zeros((slot_total, model_width), jnp.bfloat16),
        jnp.zeros((slot_total, hidden_units), jnp.float32),
        jnp.zeros((slot_total, hidden_units), jnp.float32),
    )
    expert_out, gate_keep, up_keep = lax.fori_loop(0, tile_count, forward_tile, start_state)
    returning = jnp.where(live_in[:, None] > 0, expert_out[back_index], jnp.zeros((), jnp.bfloat16))
    came_back = lax.all_to_all(returning, "fsdp", split_axis=0, concat_axis=0, tiled=True)
    pair_out = came_back[flat_slot].reshape(tok_rows, top_count, model_width)
    mixture = jnp.sum(gate_share[:, :, None] * pair_out, axis=1)
    mixed = (attended + mixture).astype(jnp.bfloat16)
    query_back, key_back, value_back, out_back = (
        lax.all_gather(w_query, "fsdp", axis=0, tiled=True),
        lax.all_gather(w_key, "fsdp", axis=0, tiled=True),
        lax.all_gather(w_value, "fsdp", axis=0, tiled=True),
        lax.all_gather(w_out, "fsdp", axis=0, tiled=True),
    )
    grad_mixed = cotangent.astype(jnp.float32)
    grad_share = jnp.sum(grad_mixed[:, None, :] * pair_out, axis=2)
    grad_pair = (
        (gate_share[:, :, None] * grad_mixed[:, None, :])
        .astype(jnp.bfloat16)
        .reshape(pair_count, model_width)
    )
    grad_outgoing = jnp.zeros((slot_total, model_width), jnp.bfloat16).at[flat_slot].set(grad_pair)
    grad_incoming = lax.all_to_all(grad_outgoing, "fsdp", split_axis=0, concat_axis=0, tiled=True)
    grad_packed = (
        jnp.zeros((slot_total + 1, model_width), jnp.bfloat16)
        .at[packed_index]
        .set(grad_incoming)[:slot_total]
    )

    def backward_tile(tile_step, loop_state):
        grad_rows, gate_sum, up_sum, down_sum = loop_state
        tile_start = tile_step * tile_rows
        tile_input = lax.dynamic_slice_in_dim(packed_rows, tile_start, tile_rows, 0)
        tile_grad = lax.dynamic_slice_in_dim(grad_packed, tile_start, tile_rows, 0)
        gate_pre = lax.dynamic_slice_in_dim(gate_keep, tile_start, tile_rows, 0)
        up_pre = lax.dynamic_slice_in_dim(up_keep, tile_start, tile_rows, 0)
        sigmoid_gate = jax.nn.sigmoid(gate_pre)
        silu_gate = gate_pre * sigmoid_gate
        hidden = (silu_gate * up_pre).astype(jnp.bfloat16)
        grad_hidden = contract(tile_grad, down_full, 1, 1)
        grad_gate_pre = (
            grad_hidden * up_pre * sigmoid_gate * (1.0 + gate_pre * (1.0 - sigmoid_gate))
        ).astype(jnp.bfloat16)
        grad_up_pre = (grad_hidden * silu_gate).astype(jnp.bfloat16)
        down_sum = down_sum + contract(hidden, tile_grad, 0, 0)
        gate_sum = gate_sum + contract(grad_gate_pre, tile_input, 0, 0)
        up_sum = up_sum + contract(grad_up_pre, tile_input, 0, 0)
        grad_input = (
            jnp.dot(grad_gate_pre, gate_full, preferred_element_type=jnp.float32)
            + jnp.dot(grad_up_pre, up_full, preferred_element_type=jnp.float32)
        ).astype(jnp.bfloat16)
        return (
            lax.dynamic_update_slice_in_dim(grad_rows, grad_input, tile_start, 0),
            gate_sum,
            up_sum,
            down_sum,
        )

    weight_zero = jnp.zeros((hidden_units, model_width), jnp.float32)
    back_state = (
        jnp.zeros((slot_total, model_width), jnp.bfloat16),
        weight_zero,
        weight_zero,
        weight_zero,
    )
    grad_rows, gate_sum, up_sum, down_sum = lax.fori_loop(0, tile_count, backward_tile, back_state)
    grad_returning = jnp.where(
        live_in[:, None] > 0, grad_rows[back_index], jnp.zeros((), jnp.bfloat16)
    )
    grad_came = lax.all_to_all(grad_returning, "fsdp", split_axis=0, concat_axis=0, tiled=True)
    grad_from_experts = jnp.sum(
        grad_came[flat_slot].reshape(tok_rows, top_count, model_width), axis=1, dtype=jnp.float32
    )
    half_units = w_gate.shape[0]

    def partner_part(grad_sum):
        return jnp.where(lower, grad_sum[half_units:], grad_sum[:half_units])

    def own_part(grad_sum):
        return jnp.where(lower, grad_sum[:half_units], grad_sum[half_units:])

    partner_terms = (
        swapped(partner_part(gate_sum).astype(jnp.bfloat16), "fsdp", 0).astype(jnp.float32),
        swapped(partner_part(up_sum).astype(jnp.bfloat16), "fsdp", 0).astype(jnp.float32),
        swapped(partner_part(down_sum).astype(jnp.bfloat16), "fsdp", 0).astype(jnp.float32),
    )
    grad_gate = own_part(gate_sum) + partner_terms[0]
    grad_up = own_part(up_sum) + partner_terms[1]
    grad_down = own_part(down_sum) + partner_terms[2]
    grad_chosen = gate_share * (
        grad_share - jnp.sum(gate_share * grad_share, axis=1, keepdims=True)
    )
    grad_logits = jnp.sum(jnp.where(matches, grad_chosen[:, :, None], 0.0), axis=1)
    grad_router_part = jnp.dot(normed_moe.astype(jnp.float32).T, grad_logits, precision=highest)
    grad_normed_moe = grad_from_experts + jnp.dot(
        grad_logits, router_full.astype(jnp.float32).T, precision=highest
    )
    grad_from_norm, grad_gain_two = norm_back(grad_normed_moe, attended, scale_two, moe_gain)
    grad_attended = grad_mixed + grad_from_norm
    grad_attended_low = grad_attended.astype(jnp.bfloat16)
    grad_out_part = contract(context, grad_attended_low, 0, 0)
    grad_context = (
        contract(grad_attended_low, out_back, 1, 1)
        .astype(jnp.bfloat16)
        .reshape(tok_rows, head_count, head_size)
    )
    probs = jnp.exp(scores_of() - log_total)
    probs_back = probs.astype(jnp.bfloat16)
    grad_values = jnp.einsum(
        "hqk,qhd->khd", probs_back, grad_context, preferred_element_type=jnp.float32
    )
    grad_probs = jnp.einsum(
        "qhd,khd->hqk", grad_context, value_heads, preferred_element_type=jnp.float32
    )
    grad_scores = (
        probs * (grad_probs - jnp.sum(probs * grad_probs, axis=2, keepdims=True))
    ).astype(jnp.bfloat16)
    grad_queries = (
        (
            jnp.einsum("hqk,khd->qhd", grad_scores, key_heads, preferred_element_type=jnp.float32)
            * score_scale
        )
        .reshape(tok_rows, model_width)
        .astype(jnp.bfloat16)
    )
    grad_keys = (
        jnp.einsum("hqk,qhd->khd", grad_scores, query_heads, preferred_element_type=jnp.float32)
        * score_scale
    )
    grad_kv = jnp.concatenate(
        (grad_keys.reshape(key_count, model_width), grad_values.reshape(key_count, model_width)),
        axis=1,
    )
    grad_blocks = [
        grad_kv[position * tok_rows : (position + 1) * tok_rows] for position in range(len(ordered))
    ]
    own_block = grad_blocks[reach_count]
    remote = grad_blocks[:reach_count] + grad_blocks[reach_count + 1 :]
    returned = [
        passed_along(grad_block.astype(jnp.bfloat16), "fsdp", -offset).astype(grad_block.dtype)
        for grad_block, offset in zip(remote, offsets)
    ]
    grad_kv_low = reduce(jnp.add, returned, own_block).astype(jnp.bfloat16)
    grad_query_part = contract(normed_attn, grad_queries, 0, 0)
    grad_kv_part = contract(normed_attn, grad_kv_low, 0, 0)
    grad_normed_attn = (
        contract(grad_queries, query_back, 1, 1)
        + contract(grad_kv_low[:, :model_width], key_back, 1, 1)
        + contract(grad_kv_low[:, model_width:], value_back, 1, 1)
    )
    grad_from_first, grad_gain_one = norm_back(grad_normed_attn, token_values, scale_one, attn_gain)
    grad_tokens = grad_attended + grad_from_first
    reduced = (
        lax.psum_scatter(grad_query_part, "fsdp", scatter_dimension=0, tiled=True),
        lax.psum_scatter(grad_kv_part[:, :model_width], "fsdp", scatter_dimension=0, tiled=True),
        lax.psum_scatter(grad_kv_part[:, model_width:], "fsdp", scatter_dimension=0, tiled=True),
        lax.psum_scatter(grad_out_part, "fsdp", scatter_dimension=0, tiled=True),
        lax.psum_scatter(grad_router_part, "fsdp", scatter_dimension=0, tiled=True),
        lax.psum_scatter(grad_gain_one, "fsdp", scatter_dimension=0, tiled=True),
        lax.psum_scatter(grad_gain_two, "fsdp", scatter_dimension=0, tiled=True),
    )
    return (
        mixed,
        grad_tokens,
        reduced[0],
        reduced[1],
        reduced[2],
        reduced[3],
        reduced[4],
        reduced[5],
        reduced[6],
        grad_gate,
        grad_up,
        grad_down,
        clipped_query,
        clipped_key,
    )


MESH = pl.DeviceIdType.MESH
f32 = jnp.float32
bf = jnp.bfloat16

def place():
    me = lax.axis_index("fsdp")
    core = lax.rem(me, 2)
    x = lax.rem(lax.div(me, 2), 2)
    y = lax.rem(lax.div(me, 4), 2)
    z = lax.div(me, 8)
    return z, y, x, core

def index_of(z, y, x, core):
    return ((z * 2 + y) * 2 + x) * 2 + core

def remote(src, dst, send, recv, device):
    return pltpu.make_async_remote_copy(
        src_ref=src, dst_ref=dst, send_sem=send, recv_sem=recv, device_id=(device,), device_id_type=MESH)

def greet(devices, conditions):
    barrier = pltpu.get_barrier_semaphore()
    for device, condition in zip(devices, conditions):
        if condition is None:
            pl.semaphore_signal(barrier, inc=1, device_id=(device,), device_id_type=MESH)
        else:
            @pl.when(condition)
            def _(device=device):
                pl.semaphore_signal(barrier, inc=1, device_id=(device,), device_id_type=MESH)
    count = 0
    for condition in conditions:
        count = count + (1 if condition is None else jnp.where(condition, 1, 0))
    pl.semaphore_wait(barrier, count)

def line_items(z):
    low = z < 2
    near = z + 1 - 2 * lax.rem(z, 2)
    return [z, near, jnp.where(low, 2, 1), jnp.where(low, 3, 0)]

def chain(z, y, x, core, per_seq):
    chip = (z * 2 + y) * 2 + x
    at = lax.rem(chip, per_seq)
    before, after = at > 0, at < per_seq - 1
    previous = (chip - jnp.where(before, 1, 0)) * 2 + core
    following = (chip + jnp.where(after, 1, 0)) * 2 + core
    return previous, following, before, after


class Near:
    def __init__(self, per_seq, ins, outs, blanks, holds, nsend, nrecv, lsem):
        z, y, x, core = place()
        self.core, self.ins, self.outs, self.blanks, self.holds = core, ins, outs, blanks, holds
        self.nsend, self.nrecv, self.lsem = nsend, nrecv, lsem
        self.c_dev = index_of(z, y, x, 1 - core)
        self.previous, self.following, self.before, self.after = chain(z, y, x, core, per_seq)
        self.passes = jnp.where(core == 0, self.after, self.before)
        self.gets = jnp.where(core == 0, self.before, self.after)

    def one(self, kind, a):
        src, slot, device = (
            (self.ins[a], 0, self.following),
            (self.ins[a], 4, self.previous),
            (self.ins[a], 1 + 2 * self.core, self.c_dev),
            (self.outs[a].at[4 * (1 - self.core)], 3 - 2 * self.core, self.c_dev),
        )[kind]
        return remote(src, self.outs[a].at[slot], self.nsend.at[kind, a], self.nrecv.at[kind, a], device)

    def own(self, a, store):
        if store:
            return pltpu.make_async_copy(self.holds[a], self.outs[a].at[2], self.lsem.at[0, a])
        return pltpu.make_async_copy(self.ins[a], self.holds[a], self.lsem.at[0, a])

    def fills(self, act):
        missing = (
            (jnp.logical_not(self.before), 0),
            (jnp.logical_not(self.before) & (self.core == 0), 1),
            (jnp.logical_not(self.after) & (self.core == 1), 3),
            (jnp.logical_not(self.after), 4),
        )
        for n, (condition, slot) in enumerate(missing):
            @pl.when(condition)
            def _(n=n, slot=slot):
                for a in range(len(self.ins)):
                    act(pltpu.make_async_copy(self.blanks[a], self.outs[a].at[slot], self.lsem.at[n + 1, a]))

    def start(self):
        for a in range(len(self.ins)):
            pl.when(self.after)(lambda a=a: self.one(0, a).start())
            pl.when(self.before)(lambda a=a: self.one(1, a).start())
            self.one(2, a).start()
            self.own(a, False).start()
            self.blanks[a][...] = jnp.zeros_like(self.blanks[a])
        self.fills(lambda copy: copy.start())
        for a in range(len(self.ins)):
            self.own(a, False).wait()
            self.own(a, True).start()

    def finish(self):
        for a in range(len(self.ins)):
            pl.when(self.before)(lambda a=a: self.one(0, a).wait_recv())
            pl.when(self.after)(lambda a=a: self.one(1, a).wait_recv())
            pl.when(self.passes)(lambda a=a: self.one(3, a).start())
        for a in range(len(self.ins)):
            self.one(2, a).wait_recv()
            pl.when(self.gets)(lambda a=a: self.one(3, a).wait_recv())
            pl.when(self.after)(lambda a=a: self.one(0, a).wait_send())
            pl.when(self.before)(lambda a=a: self.one(1, a).wait_send())
            self.one(2, a).wait_send()
            pl.when(self.passes)(lambda a=a: self.one(3, a).wait_send())
            self.own(a, True).wait()
        self.fills(lambda copy: copy.wait())


def near_scratch(arrays):
    sem = pltpu.SemaphoreType.DMA
    count = len(arrays)
    buffers = [pltpu.VMEM(a.shape, a.dtype) for a in arrays]
    return buffers + buffers + [sem((4, count)), sem((4, count)), sem((5, count))]


def near_shapes(arrays):
    return [jax.ShapeDtypeStruct((5,) + a.shape, a.dtype) for a in arrays]


def gather_all(near, ins, outs, ssem, rsem, lsem):
    count = len(ins)
    z, y, x, core = place()
    mid = (z == 1) | (z == 2)
    up, down = z < 3, z > 0
    x_dev = index_of(z, y, 1 - x, core)
    y_dev = index_of(z, 1 - y, x, core)
    c_dev = index_of(z, y, x, 1 - core)
    up_dev = index_of(jnp.minimum(z + 1, 3), y, x, core)
    down_dev = index_of(jnp.maximum(z - 1, 0), y, x, core)
    greet(
        [x_dev, y_dev, c_dev, up_dev, down_dev, near.previous, near.following],
        [None, None, None, up, down, near.before, near.after],
    )
    own = [pltpu.make_async_copy(ins[a], outs[a].at[index_of(z, y, x, core)], lsem.at[a]) for a in range(count)]
    for copy in own:
        copy.start()
    near.start()
    pending = []

    def go(kind, a, o, src, dst, device, condition=None):
        def make():
            return remote(src, dst, ssem.at[kind, o, a], rsem.at[kind, o, a], device)
        if condition is None:
            make().start()
        else:
            pl.when(condition)(lambda: make().start())
        pending.append((make, condition))

    def arrived(kind, a, o, land):
        remote(land, land, ssem.at[kind, o, a], rsem.at[kind, o, a], c_dev).wait_recv()

    items = line_items(z)

    def first(i):
        o = items[i]
        for a in range(count):
            slot = index_of(o, y, x, core)
            dst = outs[a].at[slot]
            src = ins[a] if i == 0 else dst
            if i == 0:
                go(0, a, o, src, dst, up_dev, up)
                go(1, a, o, src, dst, down_dev, down)
            else:
                from_below = o < z
                for kind, condition in ((0, from_below), (1, jnp.logical_not(from_below))):
                    pl.when(condition)(lambda kind=kind, a=a, o=o, dst=dst: arrived(kind, a, o, dst))
                go(0, a, o, src, dst, up_dev, mid & from_below)
                go(1, a, o, src, dst, down_dev, mid & jnp.logical_not(from_below))
            go(2, a, o, src, dst, x_dev)
            go(3, a, o, src, dst, y_dev)
            go(6, a, o, src, dst, c_dev)

    def second(i):
        o = items[i]
        for a in range(count):
            half = ins[a].shape[0] // 2
            from_x = outs[a].at[index_of(o, y, 1 - x, core)]
            arrived(2, a, o, from_x)
            go(5, a, o, from_x.at[pl.ds(0, half)], from_x.at[pl.ds(0, half)], y_dev)
            from_y = outs[a].at[index_of(o, 1 - y, x, core)]
            arrived(3, a, o, from_y)
            go(4, a, o, from_y.at[pl.ds(half, half)], from_y.at[pl.ds(half, half)], x_dev)
            go(7, a, o, from_x, from_x, c_dev)
            go(8, a, o, from_y, from_y, c_dev)

    def third(i):
        o = items[i]
        for a in range(count):
            half = ins[a].shape[0] // 2
            corner = outs[a].at[index_of(o, 1 - y, 1 - x, core)]
            arrived(5, a, o, corner.at[pl.ds(0, half)])
            arrived(4, a, o, corner.at[pl.ds(half, half)])
            go(9, a, o, corner, corner, c_dev)

    first(0); first(1); second(0); first(2); second(1); third(0); first(3); second(2); third(1); second(3); third(2); third(3)
    near.finish()
    for i in range(4):
        o = items[i]
        for a in range(count):
            for kind, (yy, xx) in ((6, (y, x)), (7, (y, 1 - x)), (8, (1 - y, x)), (9, (1 - y, 1 - x))):
                arrived(kind, a, o, outs[a].at[index_of(o, yy, xx, 1 - core)])
    for make, condition in pending:
        if condition is None:
            make().wait_send()
        else:
            pl.when(condition)(lambda make=make: make().wait_send())
    for copy in own:
        copy.wait()

def full_gather(arrays, near_rows, per_seq, cid):
    count = len(arrays)
    anys = pl.BlockSpec(memory_space=pl.ANY)
    def body(*refs):
        it = iter(refs)
        take = lambda n: [next(it) for _ in range(n)]
        ins, near_in, outs, near_out = take(count), take(1), take(count), take(1)
        ssem, rsem, lsem = take(3)
        near = Near(per_seq, near_in, near_out, take(1), take(1), *take(3))
        gather_all(near, ins, outs, ssem, rsem, lsem)
    sem = pltpu.SemaphoreType.DMA
    return pl.pallas_call(
        body, in_specs=[anys] * (count + 1), out_specs=[anys] * (count + 1),
        out_shape=[jax.ShapeDtypeStruct((32,) + a.shape, a.dtype) for a in arrays] + near_shapes([near_rows]),
        scratch_shapes=[sem((10, 4, count)), sem((10, 4, count)), sem((count,))] + near_scratch([near_rows]),
        compiler_params=pltpu.CompilerParams(collective_id=cid, has_side_effects=True),
        name="full_gather")(*arrays, near_rows)

def add_into(target, *terms, rows=16):
    total = target.shape[0]
    step = min(rows, total)
    def one(r, carry):
        part = pl.ds(pl.multiple_of(r * step, step), step)
        value = target[part, :].astype(f32)
        for term in terms:
            value = value + term[part, :].astype(f32)
        target[part, :] = value.astype(target.dtype)
        return carry
    lax.fori_loop(0, total // step, one, 0)

def reduce_all(ins, extra, outs, held, accs, dxs, dys, xrecvs, yrecvs, zrecvs, ssem, rsem, lsem, csend, crecv):
    left, wide, narrow = ins
    left_v, right_v, extra_land = held
    count = 2
    z, y, x, core = place()
    mid = (z == 1) | (z == 2)
    up, down = z < 3, z > 0
    x_dev = index_of(z, y, 1 - x, core)
    y_dev = index_of(z, 1 - y, x, core)
    c_dev = index_of(z, y, x, 1 - core)
    up_dev = index_of(jnp.minimum(z + 1, 3), y, x, core)
    down_dev = index_of(jnp.maximum(z - 1, 0), y, x, core)
    greet([x_dev, y_dev, c_dev, up_dev, down_dev], [None, None, None, up, down])
    items = line_items(z)[::-1]
    mine, xp, yp, dp = y * 2 + x, y * 2 + 1 - x, (1 - y) * 2 + x, (1 - y) * 2 + 1 - x
    pending = []
    rows = left_v.shape[0] // 2
    wide_width, narrow_width = wide.shape[1], narrow.shape[1]
    features = left_v.shape[1] // 2
    own_part, other_part = pl.ds(0, rows), pl.ds(rows, rows)

    def go(make, condition=None):
        if condition is None:
            make().start()
        else:
            pl.when(condition)(lambda: make().start())
        pending.append((make, condition))

    def arrived(kind, a, o, land):
        remote(land, land, ssem.at[kind, 0, a], rsem.at[kind, o, a], c_dev).wait_recv()

    crossing = (
        (left.at[1 - core], left_v.at[other_part]),
        (wide, right_v.at[other_part, pl.ds(0, wide_width)]),
        (narrow, right_v.at[other_part, pl.ds(wide_width, narrow_width)]),
        (extra.at[:, 1 - core], extra_land),
    )
    staying = (
        (left.at[core], left_v.at[own_part]),
        (wide, right_v.at[own_part, pl.ds(0, wide_width)]),
        (narrow, right_v.at[own_part, pl.ds(wide_width, narrow_width)]),
    )

    def cross(n):
        return remote(crossing[n][0], crossing[n][1], csend.at[n], crecv.at[n], c_dev)

    for n in range(4):
        cross(n).start()
    loads = [pltpu.make_async_copy(src, dst, lsem.at[n]) for n, (src, dst) in enumerate(staying)]
    loads += [
        pltpu.make_async_copy(extra.at[pl.ds(o * 4, 4), core], accs[1].at[o], lsem.at[3 + o]) for o in range(4)
    ]
    for copy in loads:
        copy.start()
    for copy in loads:
        copy.wait()
    for n in range(4):
        cross(n).wait_recv()

    chunk = 1024

    def first(i):
        o = items[i]
        for at, begin, total in ((0, 0, wide_width), (features, wide_width, narrow_width)):
            lines = pl.ds(pl.multiple_of(at + o * (features // 4), features // 4), features // 4)

            def some(n, carry):
                columns = pl.ds(pl.multiple_of(begin + n * chunk, chunk), chunk)
                product = lax.dot_general(
                    left_v[:, lines], right_v[:, columns], (((0,), (0,)), ((), ())), preferred_element_type=f32
                )
                accs[0][o, :, :, columns] = product.astype(bf).reshape(4, features // 16, chunk)
                return carry

            lax.fori_loop(0, total // chunk, some, 0)
        for p in range(4):
            accs[1][o, p] = accs[1][o, p] + extra_land[o * 4 + p]
        for a in range(count):
            half = accs[a].shape[2] // 2
            go(lambda a=a, half=half: remote(accs[a].at[o, dp, pl.ds(0, half)], dxs[a].at[o], ssem.at[1, o, a], rsem.at[1, o, a], x_dev))
            go(lambda a=a, half=half: remote(accs[a].at[o, dp, pl.ds(half, half)], dys[a].at[o], ssem.at[2, o, a], rsem.at[2, o, a], y_dev))

    def second(i):
        o = items[i]
        for a in range(count):
            half = accs[a].shape[2] // 2
            arrived(1, a, o, dxs[a].at[o])
            add_into(accs[a].at[o, yp, pl.ds(0, half)], dxs[a].at[o])
            go(lambda a=a: remote(accs[a].at[o, yp], yrecvs[a].at[o], ssem.at[4, o, a], rsem.at[4, o, a], y_dev))
            arrived(2, a, o, dys[a].at[o])
            add_into(accs[a].at[o, xp, pl.ds(half, half)], dys[a].at[o])
            go(lambda a=a: remote(accs[a].at[o, xp], xrecvs[a].at[o], ssem.at[3, o, a], rsem.at[3, o, a], x_dev))

    def third(i):
        o = items[i]
        for a in range(count):
            acc = accs[a].at[o, mine]
            arrived(3, a, o, xrecvs[a].at[o])
            arrived(4, a, o, yrecvs[a].at[o])
            if i < 3:
                @pl.when(mid)
                def _():
                    arrived(5, a, o, zrecvs[a].at[o])
                    add_into(acc, xrecvs[a].at[o], yrecvs[a].at[o], zrecvs[a].at[o])
                @pl.when(jnp.logical_not(mid))
                def _():
                    add_into(acc, xrecvs[a].at[o], yrecvs[a].at[o])
                rising = o > z
                go(lambda o=o, a=a, acc=acc: remote(acc, zrecvs[a].at[o], ssem.at[5, o, a], rsem.at[5, o, a], up_dev), rising)
                def lower(o=o, a=a, acc=acc):
                    slot = jnp.where(z - 1 == o, 4, o)
                    return remote(acc, zrecvs[a].at[slot], ssem.at[5, o, a], rsem.at[5, slot, a], down_dev)
                go(lower, jnp.logical_not(rising))
            else:
                for condition, slots in ((z == 0, (4,)), (z == 3, (3,)), (mid, (None, 4))):
                    @pl.when(condition)
                    def _(slots=slots):
                        terms = [xrecvs[a].at[o], yrecvs[a].at[o]]
                        for slot in slots:
                            slot = o if slot is None else slot
                            arrived(5, a, slot, zrecvs[a].at[slot])
                            terms.append(zrecvs[a].at[slot])
                        rows, step = outs[a].shape[0], 16
                        def one(r, carry):
                            part = pl.ds(pl.multiple_of(r * step, step), step)
                            value = acc[part, :].astype(f32)
                            for term in terms:
                                value = value + term[part, :].astype(f32)
                            outs[a][part, :] = value
                            return carry
                        lax.fori_loop(0, rows // step, one, 0)

    first(0); first(1); second(0); first(2); second(1); third(0); first(3); second(2); third(1); second(3); third(2); third(3)
    for n in range(4):
        cross(n).wait_send()
    for make, condition in pending:
        if condition is None:
            make().wait_send()
        else:
            pl.when(condition)(lambda make=make: make().wait_send())

def full_reduce(left, wide, narrow, extra, cid):
    rows = extra.shape[2]
    columns = wide.shape[1] + narrow.shape[1]
    widths = ((columns, bf), (128, f32))
    anys = pl.BlockSpec(memory_space=pl.ANY)

    def body(*refs):
        it = iter(refs)
        take = lambda n: [next(it) for _ in range(n)]
        ins, extra_in, outs, held = take(3), next(it), take(2), take(3)
        reduce_all(ins, extra_in, outs, held, *[take(2) for _ in range(6)], *it)

    sem = pltpu.SemaphoreType.DMA
    tokens = left.shape[1]
    scratch = [
        pltpu.VMEM((2 * tokens, left.shape[2]), bf),
        pltpu.VMEM((2 * tokens, columns), bf),
        pltpu.VMEM((16, rows, 128), f32),
    ]
    for lead, cut in (((4, 4), 1), ((4,), 2), ((4,), 2), ((4,), 1), ((4,), 1), ((5,), 1)):
        scratch += [pltpu.VMEM(lead + (rows // cut, width), dtype) for width, dtype in widths]
    return pl.pallas_call(
        body, in_specs=[anys] * 4, out_specs=[pl.BlockSpec(memory_space=pltpu.VMEM)] * 2,
        out_shape=[jax.ShapeDtypeStruct((rows, width), f32) for width, dtype in widths],
        scratch_shapes=scratch + [sem((6, 5, 2)), sem((6, 5, 2)), sem((7,)), sem((4,)), sem((4,))],
        compiler_params=pltpu.CompilerParams(collective_id=cid, has_side_effects=True, vmem_limit_bytes=60 * 2**20),
        name="full_reduce")(left, wide, narrow, extra)
def nt(left, right):
    return lax.dot_general(left, right, (((1,), (1,)), ((), ())), preferred_element_type=f32)


def tn(left, right):
    return lax.dot_general(left, right, (((0,), (0,)), ((), ())), preferred_element_type=f32)


def nn(left, right):
    return lax.dot_general(left, right, (((1,), (0,)), ((), ())), preferred_element_type=f32)


def expert_body(shard, width, half, block, cut, *refs):
    it = iter(refs)
    take = lambda n: [next(it) for _ in range(n)]
    own, side, near, beyond = [take(1) for _ in range(4)]
    c_all = next(it)
    x_weights, corner_weights, own_weights = take(3), take(3), take(3)
    x_all, mix, gx, gx_sum, gs_sum, y_land, z_land = take(7)
    core_land = take(2)
    grad_sum = take(2)
    x_land = next(it)
    core_weights = take(3)
    xv, cv, sv, wv, acc, hid_s, gate_s, up_s, gst, gs_y, gs_z, ostage, prev = take(13)
    gsend, grecv, lsem, rsend, rrecv, csend, crecv, xsend, xrecv = take(9)
    wsem, insem, osem, psem, dsem, hsem, tsem, wsend, wrecv = take(9)
    hidden = 2 * half
    tile = 2 * shard
    cuts = width // cut
    tiles = 4
    z, y, x, core = place()
    mid = (z == 1) | (z == 2)
    up, down = z < 3, z > 0
    x_dev = index_of(z, y, 1 - x, core)
    y_dev = index_of(z, 1 - y, x, core)
    c_dev = index_of(z, y, x, 1 - core)
    up_dev = index_of(jnp.minimum(z + 1, 3), y, x, core)
    down_dev = index_of(jnp.maximum(z - 1, 0), y, x, core)
    chip = (z * 2 + y) * 2 + x
    experts = ((z * 2 + y) * 2 + 1 - x, chip)
    lane = lax.broadcasted_iota(jnp.int32, (1, 128), 1)
    items = line_items(z)

    def nearest(k):
        return jnp.where(k == 0, items[0], jnp.where(k == 1, items[1], jnp.where(k == 2, items[2], items[3])))

    def farthest(k):
        return nearest(3 - k)

    landings = (x_all,)
    marks = pl.ds(width, 128)
    ends = jnp.logical_not(mid)

    def part_of(r):
        return pl.ds(pl.multiple_of(r * shard, shard), shard)

    def hop(kind, a, o, src, device):
        return remote(src, landings[a].at[o * 2 + y], gsend.at[kind, o, a], grecv.at[kind, o, a], device)

    def column(k, a):
        return (own[a], near[a])[k] if k < 2 else landings[a].at[items[k] * 2 + y]

    def outwards(k, act):
        for a in range(1):
            src = beyond[a] if k == 2 else column(k, a)
            pl.when(z == 1)(lambda a=a, src=src: act(hop(1, a, items[k], src, down_dev)))
            pl.when(z == 2)(lambda a=a, src=src: act(hop(0, a, items[k], src, up_dev)))

    def over(act):
        for a in range(1):
            pl.when(z == 1)(lambda a=a: act(hop(0, a, items[1], near[a], up_dev)))
            pl.when(z == 2)(lambda a=a: act(hop(1, a, items[1], near[a], down_dev)))

    def sideways(k, act):
        for a in range(1):
            if k == 2:
                pl.when(mid)(lambda a=a: act(hop(2, a, items[k], beyond[a], y_dev)))
                pl.when(ends)(lambda a=a: act(hop(2, a, items[k], column(k, a), y_dev)))
            else:
                act(hop(2, a, items[k], column(k, a), y_dev))

    def column_landed(k, condition):
        o = items[k]
        for a in range(1):
            land = landings[a].at[o * 2 + y]
            pl.when(condition & (o < z))(lambda a=a, land=land: hop(0, a, o, land, y_dev).wait_recv())
            pl.when(condition & (o > z))(lambda a=a, land=land: hop(1, a, o, land, y_dev).wait_recv())

    shares_over = [
        (
            pltpu.make_async_copy(
                block[0].at[pl.ds(0, 16), marks], x_all.at[slot, pl.ds(0, 16), marks], lsem.at[n]
            ),
            condition,
        )
        for n, (block, slot, condition) in enumerate(
            (
                (own, z * 2 + y, None),
                (side, z * 2 + 1 - y, None),
                (near, items[1] * 2 + y, None),
                (beyond, items[2] * 2 + y, mid),
            )
        )
    ]

    def shares(act):
        for copy, condition in shares_over:
            if condition is None:
                act(copy)
            else:
                pl.when(condition)(lambda copy=copy: act(copy))

    def gather_landed(o):
        for a in range(1):
            land = landings[a].at[o * 2 + 1 - y]
            remote(land, land, gsend.at[2, o, a], grecv.at[2, o, a], y_dev).wait_recv()

    def gather_sent():
        over(lambda copy: copy.wait_send())
        for k in (2, 3):
            outwards(k, lambda copy: copy.wait_send())
        for k in (1, 2, 3):
            sideways(k, lambda copy: copy.wait_send())

    def lines(block_index):
        return pl.ds(pl.multiple_of(block_index * shard, shard), shard)

    def y_copies(o):
        other = o * 2 + 1 - y
        return [
            remote(gx.at[lines(other)], y_land.at[o], rsend.at[0, o, 0], rrecv.at[0, o, 0], y_dev),
            remote(gst.at[other], gs_y.at[o], rsend.at[0, o, 1], rrecv.at[0, o, 1], y_dev),
        ]

    def z_copies(o, slot, device):
        own = o * 2 + y
        return [
            remote(gx.at[lines(own)], z_land.at[slot], rsend.at[1, o, 0], rrecv.at[1, slot, 0], device),
            remote(gst.at[own], gs_z.at[slot], rsend.at[1, o, 1], rrecv.at[1, slot, 1], device),
        ]

    def z_go(o, act):
        rising = o > z
        slot = jnp.where(z - 1 == o, 4, o)

        @pl.when(rising)
        def _():
            for copy in z_copies(o, o, up_dev):
                act(copy)

        @pl.when(jnp.logical_not(rising))
        def _():
            for copy in z_copies(o, slot, down_dev):
                act(copy)

    wide = width // 2

    def halves(hbm, vmem, slot, out=False):
        copies = []
        for h in range(2):
            far, near = hbm.at[:, pl.ds(h * wide, wide)], vmem.at[pl.ds(h * shard, shard)]
            if out:
                copies.append(pltpu.make_async_copy(near, far, tsem.at[slot, h]))
            else:
                copies.append(pltpu.make_async_copy(far, near, tsem.at[slot, h]))
        return copies

    def z_wait(slot):
        for copy in z_copies(z, slot, y_dev):
            copy.wait_recv()

    def add_up(terms):
        def some(r, carry):
            part = pl.ds(pl.multiple_of(r * 32, 32), 32)
            value = hid_s[part, :].astype(f32)
            for term in terms:
                value = value + term[part, :].astype(f32)
            hid_s[part, :] = value.astype(bf)
            return carry

        lax.fori_loop(0, tile // 32, some, 0)

    def pump(o, final):
        own = o * 2 + y
        load = halves(gx.at[lines(own)], hid_s, 0)
        for copy in load:
            copy.start()
        for copy in y_copies(o):
            copy.wait_recv()
        load_y = halves(y_land.at[o], gate_s, 1)
        for copy in load_y:
            copy.start()
        slot = jnp.where(z == 0, 4, o) if final else o

        def with_z():
            z_wait(slot)
            load_z = halves(z_land.at[slot], up_s, 2)
            for copy in load_z:
                copy.start()
            for copy in load + load_y + load_z:
                copy.wait()
            add_up([gate_s, up_s])
            gst[own] = gst[own] + gs_y[o] + gs_z[slot]

        if final:
            with_z()

            @pl.when(mid)
            def _():
                z_wait(4)
                load_z = halves(z_land.at[4], up_s, 2)
                for copy in load_z:
                    copy.start()
                for copy in load_z:
                    copy.wait()
                add_up([up_s])
                gst[own] = gst[own] + gs_z[4]

            store = halves(gx_sum, hid_s, 0, True)
            store.append(pltpu.make_async_copy(gst.at[own], gs_sum, tsem.at[1, 0]))
            for copy in store:
                copy.start()
            for copy in store:
                copy.wait()
        else:
            pl.when(mid)(with_z)

            @pl.when(jnp.logical_not(mid))
            def _():
                for copy in load + load_y:
                    copy.wait()
                add_up([gate_s])
                gst[own] = gst[own] + gs_y[o]

            store = halves(gx.at[lines(own)], hid_s, 0, True)
            for copy in store:
                copy.start()
            for copy in store:
                copy.wait()
            z_go(o, lambda copy: copy.start())

    tall = shard
    per_half = (half // tall) * (width // cut)
    pieces = 3 * per_half

    def piece(q):
        i, rest = lax.div(q, per_half), lax.rem(q, per_half)
        r, c = lax.div(rest, width // cut), lax.rem(rest, width // cut)
        return i, pl.multiple_of(r * tall, tall), pl.ds(pl.multiple_of(c * cut, cut), cut)

    slots = 8

    def eighth(ref, slot):
        low = pl.multiple_of(lax.rem(slot, 2) * tall, tall)
        return ref.at[lax.div(slot, 4), lax.rem(lax.div(slot, 2), 2), pl.ds(low, tall)]

    def stage(slot):
        return eighth(ostage, slot)

    def held(slot):
        return eighth(prev, slot)

    def flush(number):
        def across(q, slot):
            i, r, c = piece(q)
            land = core_land[number].at[i, pl.ds(r, tall), c]
            return remote(stage(slot), land, csend.at[number, slot], crecv.at[number], c_dev)

        def give(q, carry):
            slot = lax.rem(q, slots)
            pl.when(q >= slots)(lambda: across(q - slots, slot).wait_send())
            i, r, c = piece(q)
            stage(slot)[...] = acc[i, pl.ds(pl.multiple_of(half + r, tall), tall), c].astype(bf)
            across(q, slot).start()
            return carry

        lax.fori_loop(0, pieces, give, 0)

        def given(q, carry):
            across(q, lax.rem(q, slots)).wait_send()
            return carry

        lax.fori_loop(pieces - slots, pieces, given, 0)
        remote(core_land[number], core_land[number], csend.at[number, 0], crecv.at[number], c_dev).wait_recv()

        def bring(q, slot):
            i, r, c = piece(q)
            return pltpu.make_async_copy(core_land[number].at[i, pl.ds(r, tall), c], held(slot), hsem.at[slot])

        def store(q, slot):
            i, r, c = piece(q)
            return pltpu.make_async_copy(stage(slot), grad_sum[number].at[i, pl.ds(r, tall), c], dsem.at[slot])

        for q in range(slots - 1):
            bring(q, q).start()

        def keep(q, carry):
            slot = lax.rem(q, slots)
            coming = q + slots - 1
            pl.when(coming < pieces)(lambda: bring(coming, lax.rem(coming, slots)).start())
            pl.when(q >= slots)(lambda: store(q - slots, slot).wait())
            bring(q, slot).wait()
            i, r, c = piece(q)
            stage(slot)[...] = (acc[i, pl.ds(r, tall), c] + held(slot)[...].astype(f32)).astype(bf)
            store(q, slot).start()
            return carry

        lax.fori_loop(0, pieces, keep, 0)

        def kept(q, carry):
            store(q, lax.rem(q, slots)).wait()
            return carry

        lax.fori_loop(pieces - slots, pieces, kept, 0)

    def x_copy():
        return remote(grad_sum[0], x_land, xsend, xrecv, x_dev)

    def c_loads(o, slot):
        return [
            pltpu.make_async_copy(c_all.at[o * 2 + r], cv.at[slot, pl.ds(r * shard, shard)], insem.at[1, r, slot])
            for r in range(2)
        ]

    def x_load(k, slot, act):
        for n in range(4):
            o = items[n]

            def bring(column, other):
                for r, src in ((y, column[0]), (1 - y, other[0])):
                    for which, target, part in ((0, xv, pl.ds(0, width)), (2, sv, marks)):
                        act(
                            pltpu.make_async_copy(
                                src.at[:, part], target.at[slot, part_of(r)], insem.at[which, r, slot]
                            )
                        )

            landed = [ref.at[o * 2 + y] for ref in landings]
            other = side if n == 0 else [ref.at[o * 2 + 1 - y] for ref in landings]
            if n < 2:
                pl.when(k == n)(lambda n=n, other=other: bring((own, near)[n], other))
            elif n == 2:
                pl.when((k == n) & mid)(lambda other=other: bring(beyond, other))
                pl.when((k == n) & ends)(lambda landed=landed, other=other: bring(landed, other))
            else:
                pl.when(k == n)(lambda landed=landed, other=other: bring(landed, other))

    def start(copy):
        copy.start()

    def wait(copy):
        copy.wait()

    def spot(o, n):
        return pl.ds(pl.multiple_of(o * tile, tile), tile), pl.ds(pl.multiple_of(n * cut, cut), cut)

    def outgoing(o, n, slot):
        r, c = spot(o, n)
        return [
            pltpu.make_async_copy(ostage.at[slot, i], ref.at[r, c], osem.at[i, slot])
            for i, ref in enumerate((mix, gx))
        ]

    def earlier(o, n, slot):
        r, c = spot(o, n)
        return [
            pltpu.make_async_copy(ref.at[r, c], prev.at[slot, i], psem.at[i, slot])
            for i, ref in enumerate((mix, gx))
        ]

    def weight_loads(number):
        sources = list(zip(*((x_weights, corner_weights), (own_weights, core_weights))[number]))
        return [
            pltpu.make_async_copy(src, wv.at[i, pl.ds(h * half, half)], wsem.at[i, h])
            for i, pair in enumerate(sources)
            for h, src in enumerate(pair)
        ]

    def weights_across():
        return [remote(own_weights[i], core_weights[i], wsend.at[i], wrecv.at[i], c_dev) for i in range(3)]

    def run_tile(number, o, slot):
        if number:
            for copy in earlier(o, 0, 0):
                copy.start()
        pick = (lane == experts[number]).astype(f32)
        halves_of = pick + (lane == experts[number] + gst.shape[1]).astype(f32)
        share = jnp.sum(sv[slot].astype(f32) * halves_of, axis=1, keepdims=True)

        def hidden_block(j, dots):
            part = pl.ds(pl.multiple_of(j * block, block), block)
            rows_in, cots = xv[slot], cv[slot]
            gate_pre = nt(rows_in, wv[0, part, :])
            up_pre = nt(rows_in, wv[1, part, :])
            grad_raw = nt(cots, wv[2, part, :])
            sig = jax.nn.sigmoid(gate_pre)
            silu = gate_pre * sig
            low = (silu * up_pre).astype(bf).astype(f32)
            dots = dots + jnp.sum(low * grad_raw, axis=1, keepdims=True)
            grad_hid = grad_raw * share
            grad_gate = (grad_hid * up_pre * sig * (1.0 + gate_pre * (1.0 - sig))).astype(bf)
            grad_up = (grad_hid * silu).astype(bf)
            shared = (low * share).astype(bf)
            hid_s[:, part] = shared
            gate_s[:, part] = grad_gate
            up_s[:, part] = grad_up
            acc[0, part, :] += tn(grad_gate, rows_in)
            acc[1, part, :] += tn(grad_up, rows_in)
            acc[2, part, :] += tn(shared, cots)
            return dots

        dots = lax.fori_loop(0, hidden // block, hidden_block, jnp.zeros((tile, 1), f32))
        both = dots * pick
        for r in range(2):
            turned = jnp.transpose(both[r * shard : (r + 1) * shard, :])[: gst.shape[1], :]
            gst[o * 2 + r] = gst[o * 2 + r] + turned if number else turned

        def column_block(n, inner):
            now = lax.rem(n, 2)
            columns = pl.ds(pl.multiple_of(n * cut, cut), cut)

            @pl.when(n >= 2)
            def _():
                for copy in outgoing(o, n - 2, now):
                    copy.wait()

            out = nn(hid_s[...], wv[2, :, columns])
            back = nn(gate_s[...], wv[0, :, columns]) + nn(up_s[...], wv[1, :, columns])
            if number:
                @pl.when(n + 1 < cuts)
                def _():
                    for copy in earlier(o, n + 1, 1 - now):
                        copy.start()

                for copy in earlier(o, n, now):
                    copy.wait()
                out = out + prev[now, 0].astype(f32)
                back = back + prev[now, 1].astype(f32)
            ostage[now, 0] = out.astype(bf)
            ostage[now, 1] = back.astype(bf)
            for copy in outgoing(o, n, now):
                copy.start()
            return inner

        lax.fori_loop(0, cuts, column_block, 0)
        for n in (cuts - 2, cuts - 1):
            for copy in outgoing(o, n, n % 2):
                copy.wait()

    greet([x_dev, y_dev, c_dev, up_dev, down_dev], [None, None, None, up, down])
    across = weights_across()
    outwards(2, start)
    over(start)
    sideways(1, start)
    loads = weight_loads(0) + c_loads(items[0], 0)
    for copy in loads:
        copy.start()
    x_load(0, 0, start)
    shares(start)
    acc[...] = jnp.zeros_like(acc)
    for copy in loads[:6]:
        copy.wait()
    for copy in across:
        copy.start()

    def first_pass(t, carry):
        slot = lax.rem(t, 2)
        o = nearest(t)

        @pl.when(t == 1)
        def _():
            column_landed(3, mid)
            outwards(3, start)
            column_landed(2, ends)
            sideways(2, start)

        @pl.when(t == 2)
        def _():
            column_landed(3, ends)
            sideways(3, start)

        @pl.when(t + 1 < tiles)
        def _():
            for copy in c_loads(nearest(t + 1), 1 - slot):
                copy.start()

        @pl.when(t > 0)
        def _():
            gather_landed(o)
            x_load(t, slot, start)

        x_load(t, slot, wait)
        for copy in c_loads(o, slot):
            copy.wait()
        run_tile(0, o, slot)
        return carry

    lax.fori_loop(0, tiles, first_pass, 0)
    for copy in across:
        copy.wait()
    loads = weight_loads(1)
    for copy in loads + c_loads(items[3], 0):
        copy.start()
    x_load(3, 0, start)
    shares(wait)
    flush(0)
    x_copy().start()
    acc[...] = jnp.zeros_like(acc)
    for copy in loads:
        copy.wait()

    def second_pass(t, carry):
        slot = lax.rem(t, 2)
        o = farthest(t)

        @pl.when(t + 1 < tiles)
        def _():
            for copy in c_loads(farthest(t + 1), 1 - slot):
                copy.start()
            x_load(2 - t, 1 - slot, start)

        for copy in c_loads(o, slot):
            copy.wait()
        x_load(3 - t, slot, wait)
        run_tile(1, o, slot)
        for copy in y_copies(o):
            copy.start()
        k = jnp.where(mid, t - 2, t - 1)
        pl.when(k >= 0)(lambda: pump(farthest(k), False))
        return carry

    lax.fori_loop(0, tiles, second_pass, 0)
    pl.when(mid)(lambda: pump(items[1], False))
    flush(1)
    pump(z, True)
    for k in range(4):
        for copy in y_copies(items[k]):
            copy.wait_send()
        if k:
            z_go(items[k], lambda copy: copy.wait_send())
    gather_sent()
    x_copy().wait()


def expert_pass(rows_in, c_all, x_weights, corner_weights, own_weights, gs_rows, cid):
    blocks, shard, width = c_all.shape
    rows = blocks * shard
    half = own_weights[0].shape[0]
    hidden = 2 * half
    tile, block, cut = 2 * shard, half, 512
    anys = pl.BlockSpec(memory_space=pl.ANY)
    sem = pltpu.SemaphoreType.DMA
    flat = list(x_weights) + list(corner_weights) + list(own_weights)
    shaped = jax.ShapeDtypeStruct
    half_grads = shaped((3, half, width), bf)
    shapes = [
        shaped((blocks, shard, width + 128), bf),
        shaped((rows, width), bf),
        shaped((rows, width), bf),
        shaped((shard, width), bf),
        shaped((gs_rows, shard), f32),
        shaped((4, shard, width), bf),
        shaped((5, shard, width), bf),
    ] + [half_grads] * 5 + [shaped((half, width), bf)] * 3
    return pl.pallas_call(
        functools.partial(expert_body, shard, width, half, block, cut),
        in_specs=[anys] * (5 + len(flat)),
        out_specs=[anys] * len(shapes),
        out_shape=shapes,
        scratch_shapes=[
            pltpu.VMEM((2, tile, width), bf),
            pltpu.VMEM((2, tile, width), bf),
            pltpu.VMEM((2, tile, 128), bf),
            pltpu.VMEM((3, hidden, width), bf),
            pltpu.VMEM((3, hidden, width), f32),
            pltpu.VMEM((tile, hidden), bf),
            pltpu.VMEM((tile, hidden), bf),
            pltpu.VMEM((tile, hidden), bf),
            pltpu.VMEM((blocks, gs_rows, shard), f32),
            pltpu.VMEM((4, gs_rows, shard), f32),
            pltpu.VMEM((5, gs_rows, shard), f32),
            pltpu.VMEM((2, 2, tile, cut), bf),
            pltpu.VMEM((2, 2, tile, cut), bf),
            sem((3, 4, 2)),
            sem((3, 4, 2)),
            sem((8,)),
            sem((2, 5, 2)),
            sem((2, 5, 2)),
            sem((2, 8)),
            sem((2,)),
            sem,
            sem,
            sem((3, 2)),
            sem((3, 2, 2)),
            sem((2, 2)),
            sem((2, 2)),
            sem((8,)),
            sem((8,)),
            sem((3, 2)),
            sem((3,)),
            sem((3,)),
        ],
        compiler_params=pltpu.CompilerParams(
            vmem_limit_bytes=63 * 2**20, collective_id=cid, has_side_effects=True
        ),
        name="expert_pass",
    )(*rows_in, c_all, *flat)
def attend_body(scale, q_ref, k_ref, v_ref, bias_ref, out_ref, lse_ref, top_ref):
    head = pl.program_id(0)
    scores = nt(q_ref[...], k_ref[...]) * scale + bias_ref[...]
    top = jnp.max(scores, axis=1, keepdims=True)
    parts = jnp.exp(scores - top)
    total = jnp.sum(parts, axis=1, keepdims=True)
    probs = (parts * (1.0 / total)).astype(bf)
    out_ref[...] = nn(probs, v_ref[...]).astype(bf)
    lane = lax.broadcasted_iota(jnp.int32, lse_ref.shape, 1)

    @pl.when(head == 0)
    def _():
        lse_ref[...] = jnp.zeros_like(lse_ref)
        top_ref[...] = jnp.zeros_like(top_ref)

    lse_ref[...] = jnp.where(lane == head, top + jnp.log(total), lse_ref[...])
    row = lax.broadcasted_iota(jnp.int32, top_ref.shape, 1)
    top_ref[...] = jnp.where(row == head, jnp.max(top), top_ref[...])


def attend(near_qkv, bias, heads, width, scale):
    rows, keys = bias.shape
    size = width // heads
    middle = keys // rows // 2
    return pl.pallas_call(
        functools.partial(attend_body, scale),
        grid=(heads,),
        in_specs=[
            pl.BlockSpec((rows, size), lambda h: (middle, h)),
            pl.BlockSpec((keys, size), lambda h: (0, heads + h)),
            pl.BlockSpec((keys, size), lambda h: (0, 2 * heads + h)),
            pl.BlockSpec((rows, keys), lambda h: (0, 0)),
        ],
        out_specs=[
            pl.BlockSpec((rows, size), lambda h: (0, h)),
            pl.BlockSpec((rows, 128), lambda h: (0, 0)),
            pl.BlockSpec((8, 128), lambda h: (0, 0)),
        ],
        out_shape=[
            jax.ShapeDtypeStruct((rows, width), bf),
            jax.ShapeDtypeStruct((rows, 128), f32),
            jax.ShapeDtypeStruct((8, 128), f32),
        ],
        compiler_params=pltpu.CompilerParams(vmem_limit_bytes=48 * 2**20),
        name="attend",
    )(near_qkv, near_qkv, near_qkv, bias)


def attend_queries_body(scale, per_seq, heads, *refs):
    it = iter(refs)
    take = lambda n: [next(it) for _ in range(n)]
    q_ref, k_ref, v_ref, g_ref, bias_ref, lse_ref = take(6)
    sent, dq_ref, landed = take(2), next(it), take(2)
    near = Near(per_seq, sent, landed, take(2), take(2), *take(3))
    head = pl.program_id(0)

    @pl.when(head == 0)
    def _():
        greet([near.c_dev, near.previous, near.following], [None, near.before, near.after])
        near.start()

    lane = lax.broadcasted_iota(jnp.int32, lse_ref.shape, 1)
    lse = jnp.sum(jnp.where(lane == head, lse_ref[...], 0.0), axis=1, keepdims=True)
    keys = k_ref[...]
    probs = jnp.exp(nt(q_ref[...], keys) * scale + bias_ref[...] - lse)
    grad_probs = nt(g_ref[...], v_ref[...])
    shift = jnp.sum(probs * grad_probs, axis=1, keepdims=True)
    grad_scores = (probs * (grad_probs - shift)).astype(bf)
    dq_ref[...] = (nn(grad_scores, keys) * scale).astype(bf)
    pl.when(head == heads - 1)(near.finish)


def attend_queries(near_qkv, grads, bias, lse, stats, heads, scale, per_seq, cid):
    rows, keys = bias.shape
    width = grads.shape[1]
    size = width // heads
    middle = keys // rows // 2
    own = pl.BlockSpec((rows, size), lambda h: (0, h))
    anys = pl.BlockSpec(memory_space=pl.ANY)
    return pl.pallas_call(
        functools.partial(attend_queries_body, scale, per_seq, heads),
        grid=(heads,),
        in_specs=[
            pl.BlockSpec((rows, size), lambda h: (middle, h)),
            pl.BlockSpec((keys, size), lambda h: (0, heads + h)),
            pl.BlockSpec((keys, size), lambda h: (0, 2 * heads + h)),
            own,
            pl.BlockSpec((rows, keys), lambda h: (0, 0)),
            pl.BlockSpec((rows, 128), lambda h: (0, 0)),
            anys,
            anys,
        ],
        out_specs=[own, anys, anys],
        out_shape=[jax.ShapeDtypeStruct((rows, width), bf)] + near_shapes([grads, stats]),
        scratch_shapes=near_scratch([grads, stats]),
        compiler_params=pltpu.CompilerParams(
            vmem_limit_bytes=48 * 2**20, collective_id=cid, has_side_effects=True
        ),
        name="attend_queries",
    )(near_qkv, near_qkv, near_qkv, grads, bias, lse, grads, stats)


def attend_keys_body(
    scale, q_ref, k_ref, v_ref, g_ref, bias_ref, stats_ref, sums_ref, terms_ref, dk_ref, dv_ref, *total_refs
):
    for n, total_ref in enumerate(total_refs):
        total_ref[...] = sums_ref[n].astype(f32) + terms_ref[n].astype(f32)
    head = pl.program_id(0)
    heads = stats_ref.shape[1] // 2
    row = lax.broadcasted_iota(jnp.int32, stats_ref.shape[1:], 0)

    def line(at):
        parts = [
            jnp.sum(jnp.where(row == at, stats_ref[j], 0.0), axis=0, keepdims=True)
            for j in range(stats_ref.shape[0])
        ]
        return jnp.concatenate(parts, axis=1)

    queries, grads = q_ref[...], g_ref[...]
    probs = jnp.exp(nt(k_ref[...], queries) * scale + bias_ref[...] - line(head))
    dv_ref[...] = nn(probs.astype(bf), grads).astype(bf)
    grad_probs = nt(v_ref[...], grads)
    grad_scores = (probs * (grad_probs - line(heads + head))).astype(bf)
    dk_ref[...] = (nn(grad_scores, queries) * scale).astype(bf)


def attend_keys(near_qkv, near_grads, bias, near_stats, sums, terms, heads, scale):
    count, units = sums.shape[:2]
    slice_rows = units // heads
    part = pl.BlockSpec((count, slice_rows, sums.shape[2]), lambda h: (0, h, 0))
    total = pl.BlockSpec((slice_rows, sums.shape[2]), lambda h: (h, 0))
    rows, keys = bias.shape
    width = near_grads.shape[1]
    size = width // heads
    middle = keys // rows // 2
    own = pl.BlockSpec((rows, size), lambda h: (0, h))
    return pl.pallas_call(
        functools.partial(attend_keys_body, scale),
        grid=(heads,),
        in_specs=[
            pl.BlockSpec((keys, size), lambda h: (0, h)),
            pl.BlockSpec((rows, size), lambda h: (middle, heads + h)),
            pl.BlockSpec((rows, size), lambda h: (middle, 2 * heads + h)),
            pl.BlockSpec((keys, size), lambda h: (0, h)),
            pl.BlockSpec((rows, keys), lambda h: (0, 0)),
            pl.BlockSpec(near_stats.shape, lambda h: (0, 0, 0)),
            part,
            part,
        ],
        out_specs=[own, own] + [total] * count,
        out_shape=[jax.ShapeDtypeStruct((rows, width), bf)] * 2
        + [jax.ShapeDtypeStruct(sums.shape[1:], f32)] * count,
        compiler_params=pltpu.CompilerParams(vmem_limit_bytes=48 * 2**20),
        name="attend_keys",
    )(near_qkv, near_qkv, near_qkv, near_grads, bias, near_stats, sums, terms)


def rows_body(own, side, near, beyond, ssem, rsem):
    z, y, x, core = place()
    mid = (z == 1) | (z == 2)
    y_dev = index_of(z, 1 - y, x, core)
    near_dev = index_of(z + 1 - 2 * lax.rem(z, 2), y, x, core)
    beyond_dev = index_of(jnp.where(mid, 3 - z, z), y, x, core)
    greet([y_dev, near_dev, beyond_dev], [None, None, mid])
    copies = [
        (remote(own, target, ssem.at[n], rsem.at[n], device), condition)
        for n, (target, device, condition) in enumerate(
            ((beyond, beyond_dev, mid), (side, y_dev, None), (near, near_dev, None))
        )
    ]
    for act in (lambda copy: copy.start(), lambda copy: copy.wait()):
        for copy, condition in copies:
            if condition is None:
                act(copy)
            else:
                pl.when(condition)(lambda copy=copy, act=act: act(copy))


def rows_around(own, cid):
    anys = pl.BlockSpec(memory_space=pl.ANY)
    sem = pltpu.SemaphoreType.DMA((3,))
    return pl.pallas_call(
        rows_body,
        in_specs=[anys],
        out_specs=[anys] * 3,
        out_shape=[jax.ShapeDtypeStruct(own.shape, own.dtype)] * 3,
        scratch_shapes=[sem, sem],
        compiler_params=pltpu.CompilerParams(collective_id=cid, has_side_effects=True),
        name="rows_around",
    )(own)


def dense_layer(
    tokens,
    w_query,
    w_key,
    w_value,
    w_out,
    w_router,
    gain_attn,
    gain_moe,
    w_gate,
    w_up,
    w_down,
    routes,
    doc_lengths,
    clip_limit,
    cotangent,
):
    devices = lax.axis_size("fsdp")
    device = lax.axis_index("fsdp")
    tok_rows = tokens.shape[0]
    model_width = tokens.shape[1]
    weight_rows = w_query.shape[0]
    head_count = clip_limit.shape[0]
    head_size = model_width // head_count
    experts = w_router.shape[1]
    seq_len = devices * tok_rows // doc_lengths.shape[0]
    score_scale = head_size ** (-0.5)
    wide_width = 3 * model_width
    extra = jnp.pad(
        jnp.concatenate((w_router, gain_attn[:, None], gain_moe[:, None]), axis=1),
        ((0, 0), (0, 128 - experts - 2)),
    )
    wide_own = jnp.concatenate((w_query, w_key, w_value, extra), axis=1)
    per_seq = devices // (2 * doc_lengths.shape[0])
    wide_full, out_full, near_tokens = full_gather([wide_own, w_out], tokens, per_seq, 2)
    wide_full = wide_full.reshape(model_width, wide_width + 128)
    out_full = out_full.reshape(model_width, model_width)
    later = lax.optimization_barrier((out_full, cotangent, w_gate, w_up, w_down))
    out_full, cot_own, gate_own, up_own, down_own = later
    planes = [
        [index_of(z, y, x, core) for z in range(4) for y in range(2)] for x in range(2) for core in range(2)
    ]
    c_all = lax.all_gather(cot_own, "fsdp", axis_index_groups=planes)
    x_weights = [swapped(w, "fsdp", 1) for w in (gate_own, up_own, down_own)]
    router_full = wide_full[:, wide_width : wide_width + experts]
    gain_one = wide_full[:, wide_width + experts]
    gain_two = wide_full[:, wide_width + experts + 1]
    token_values = tokens.astype(f32)
    scale_one = rms_scale(token_values)
    attn_gain = gain_one.astype(f32)
    reach_count = (HALF - 2) // tok_rows + 1
    slots = 2 * reach_count + 1
    key_count = slots * tok_rows
    row_index = jnp.arange(tok_rows, dtype=jnp.int32)
    query_places = device * tok_rows + row_index
    key_places = (device - reach_count) * tok_rows + jnp.arange(key_count, dtype=jnp.int32)
    query_docs = document_of(query_places, doc_lengths, seq_len)
    key_docs = document_of(key_places, doc_lengths, seq_len)
    near_by = (key_docs >= 0) & (key_places // seq_len == query_places[0] // seq_len)
    visible = (
        (query_docs[:, None] == key_docs[None, :])
        & near_by[None, :]
        & (jnp.abs(query_places[:, None] - key_places[None, :]) < HALF)
    )
    bias = jnp.where(visible, 0.0, masked)
    near_values = near_tokens.reshape(key_count, model_width).astype(f32)
    near_normed = (near_values * rms_scale(near_values) * attn_gain).astype(bf)
    normed_attn = (token_values * scale_one * attn_gain).astype(bf)
    near_qkv = jnp.dot(near_normed, wide_full, preferred_element_type=f32).astype(bf)
    context, log_total, own_top = attend(near_qkv, bias, head_count, model_width, score_scale)
    both_left = jnp.stack((normed_attn, context)).reshape(2, tok_rows, devices // 2, 2, weight_rows)
    by_core = jnp.transpose(both_left, (3, 1, 0, 2, 4)).reshape(2, tok_rows, 2 * model_width // 2)
    attended = token_values + jnp.dot(context, out_full, preferred_element_type=f32)
    scale_two = rms_scale(attended)
    moe_gain = gain_two.astype(f32)
    normed_moe = (attended * scale_two * moe_gain).astype(bf)
    logits = jnp.dot(normed_moe, router_full, preferred_element_type=f32)
    named = jnp.any(routes[:, :, None] == jnp.arange(experts, dtype=jnp.int32)[None, None, :], axis=1)
    chosen = jnp.where(named, logits, masked)
    lifted = jnp.where(named, jnp.exp(logits - jnp.max(chosen, axis=1, keepdims=True)), 0.0)
    gate_share = lifted / jnp.sum(lifted, axis=1, keepdims=True)
    lanes = []
    for values in (gate_share, jnp.broadcast_to(own_top[:1, :head_count], (tok_rows, head_count))):
        most = lax.reduce_precision(values, 8, 7)
        lanes += [most.astype(bf), (values - most).astype(bf)]
    lanes = jnp.concatenate(lanes, axis=1)
    lane_count = lanes.shape[1]
    own_rows = jnp.concatenate((normed_moe, jnp.pad(lanes, ((0, 0), (0, 128 - lane_count)))), axis=1)
    rows_in = [own_rows, *rows_around(own_rows, 4)]
    x_weights = [lax.optimization_barrier((w, rows_in[1]))[0] for w in x_weights]
    corner_weights = [swapped(w, "fsdp", 0) for w in x_weights]
    expert_results = expert_pass(
        rows_in, c_all, x_weights, corner_weights, (gate_own, up_own, down_own), experts, 0
    )
    x_all, mix_part, grad_from_experts, grad_share = [expert_results[i] for i in (0, 1, 3, 4)]
    x_terms, own_sum = expert_results[11], expert_results[10]
    first_lane = model_width + 2 * experts
    tops = x_all[:, 0, first_lane : first_lane + 2 * head_count].astype(f32)
    head_max = jnp.max(tops[:, :head_count] + tops[:, head_count:], axis=0)
    head_max = jnp.maximum(head_max, swapped(head_max, "fsdp", 0))
    head_max = jnp.maximum(head_max, swapped(head_max, "fsdp", 1))
    factor = clip_limit / jnp.maximum(head_max, clip_limit)
    columns = jnp.repeat(jnp.sqrt(factor), head_size)
    clipped_query = (w_query.astype(f32) * columns[None, :]).astype(bf)
    clipped_key = (w_key.astype(f32) * columns[None, :]).astype(bf)
    mixture = lax.psum_scatter(mix_part, "fsdp", axis_index_groups=planes, tiled=True)
    grad_share = jnp.transpose(grad_share)
    grad_mixed = cotangent.astype(f32)
    grad_logits = gate_share * (grad_share - jnp.sum(gate_share * grad_share, axis=1, keepdims=True))
    grad_router_part = jnp.dot(normed_moe.astype(f32).T, grad_logits, precision=highest)
    grad_normed_moe = grad_from_experts.astype(f32) + jnp.dot(
        grad_logits, router_full.astype(f32).T, precision=highest
    )
    grad_from_norm, grad_gain_two = norm_back(grad_normed_moe, attended, scale_two, moe_gain)
    grad_attended = grad_mixed + grad_from_norm
    grad_attended_low = grad_attended.astype(bf)
    grad_context = contract(grad_attended_low, out_full, 1, 1).astype(bf)
    by_head = grad_context.astype(f32) * context.astype(f32)
    shifts = jnp.sum(by_head.reshape(tok_rows, head_count, head_size), axis=2)
    stats = jnp.transpose(jnp.concatenate((log_total[:, :head_count], shifts), axis=1))
    grad_queries, near_grads, near_stats = attend_queries(
        near_qkv, grad_context, bias, log_total, stats, head_count, score_scale, per_seq, 1
    )
    grad_keys, grad_values, grad_gate, grad_up, grad_down = attend_keys(
        near_qkv,
        near_grads.reshape(key_count, model_width),
        bias,
        near_stats,
        own_sum,
        x_terms,
        head_count,
        score_scale,
    )
    grad_qkv = jnp.concatenate((grad_queries, grad_keys, grad_values), axis=1)
    grad_normed_attn = contract(jnp.pad(grad_qkv, ((0, 0), (0, 128))), wide_full, 1, 1)
    grad_from_first, grad_gain_one = norm_back(grad_normed_attn, token_values, scale_one, attn_gain)
    grad_tokens = grad_attended + grad_from_first
    extra_part = jnp.pad(
        jnp.concatenate((grad_router_part, grad_gain_one[:, None], grad_gain_two[:, None]), axis=1),
        ((0, 0), (0, 128 - experts - 2)),
    )
    owners = (devices // 2, 2, weight_rows)
    grads_sum, extra_sum = full_reduce(
        by_core, grad_qkv, grad_attended_low, extra_part.reshape(owners + (128,)), 3
    )
    mixture, grads_sum = lax.optimization_barrier((mixture, grads_sum))
    mixed = (attended + mixture.astype(f32)).astype(bf)
    return (
        mixed,
        grad_tokens,
        grads_sum[:, :model_width],
        grads_sum[:, model_width : 2 * model_width],
        grads_sum[:, 2 * model_width : wide_width],
        grads_sum[:, wide_width:],
        extra_sum[:, :experts],
        extra_sum[:, experts],
        extra_sum[:, experts + 1],
        grad_gate,
        grad_up,
        grad_down,
        clipped_query,
        clipped_key,
    )


def chosen_layer(mesh):
    def layer(*arrays):
        experts, top_count = arrays[5].shape[1], arrays[11].shape[1]
        if mesh.shape["fsdp"] == 32 and 2 * top_count >= experts:
            return dense_layer(*arrays)
        return routed_layer(*arrays)

    return layer


def solution(mesh):
    placed = (
        P("fsdp", None),
        P("fsdp", None),
        P("fsdp", None),
        P("fsdp", None),
        P("fsdp", None),
        P("fsdp", None),
        P("fsdp"),
        P("fsdp"),
        P("fsdp", None),
        P("fsdp", None),
        P("fsdp", None),
        P("fsdp", None),
        P(),
        P(),
        P("fsdp", None),
    )
    return jax.shard_map(
        chosen_layer(mesh),
        mesh=mesh,
        in_specs=placed,
        out_specs=(
            P("fsdp", None),
            P("fsdp", None),
            P("fsdp", None),
            P("fsdp", None),
            P("fsdp", None),
            P("fsdp", None),
            P("fsdp", None),
            P("fsdp"),
            P("fsdp"),
            P("fsdp", None),
            P("fsdp", None),
            P("fsdp", None),
            P("fsdp", None),
            P("fsdp", None),
        ),
        check_vma=False,
    )
```
